32 devices in a mesh: tiles: 8 (over z, y), rep: 4 (over x, core).
Axes of the slice: x: 2, y: 2, z: 4, core: 2. Of those that a mesh axis runs over, the one named last changes fastest.
Arguments:
- tiles: bfloat16 [64, 64, 4096], P(('tiles', 'rep')), may hold values from -6 to 6
- block_one: int32 [64], P(('tiles', 'rep')), may hold values from 0 to 7
- block_two: int32 [64], P(('tiles', 'rep')), may hold values from 0 to 15
- block_three: int32 [64], P(('tiles', 'rep')), may hold values from 0 to 15
- owner_map: int32 [8], replicated, may hold values from 0 to 7, each once
- u_one: float32 [32, 512], P(None, 'tiles'), may hold values from -6 to 6
- u_two: bfloat16 [32, 1024], P(None, 'tiles'), may hold values from -6 to 6
- u_three: bfloat16 [32, 1024], replicated, may hold values from -6 to 6
Outputs:
- factor: float32 [32, 512], P(None, 'tiles')
- tile_factor: bfloat16 [64, 2048], P(('tiles', 'rep'))
The draws below stay inside these ranges and needn't reach their ends.
All inputs are finite; a program needn't handle non-finite values.
Results may differ from the reference program's by a relative error of at most 0.0081.
Values may be sent and summed in bfloat16 or wider, within the bound.
No kernel may reach another device: no remote copies, remote signals or barrier semaphores. Data moves between devices by JAX's collectives and lax.ppermute only.
A program may use at most 64 MiB of HBM per device.

```python
import math
import jax
import jax.numpy as jnp
import numpy as np
from jax import lax

B = 64
R = 32
TILE_DEV = 2
NB3 = 16
ITERS = 1
NS_STEPS = 2
NB1 = 8
NB2 = 16
NROWS = 512
NT = 64


def draw_u_one(key, part):
    noise = jax.random.normal(jax.random.fold_in(key, 11), (R, NROWS), jnp.float32)
    signs = (jax.random.randint(jax.random.fold_in(key, 12), (R, 1), 0, 2) * 2 - 1).astype(jnp.float32)
    common = jax.random.normal(jax.random.fold_in(key, 13), (1, NROWS), jnp.float32)
    return jnp.clip(noise + signs * common, -6.0, 6.0).astype(jnp.float32)


def plant(array, key, least, top_value):
    longest = array.shape.index(max(array.shape))
    spots = []
    for shift in (0, 1):
        where = [jax.random.randint(jax.random.fold_in(key, axis), (), 0, length) for axis, length in enumerate(array.shape)]
        where[longest] = (where[longest] + shift) % array.shape[longest]
        spots.append(tuple(where))
    return array.at[spots[0]].set(least).at[spots[1]].set(top_value)


def shard_levels(rng, shape, cuts, smallest, largest):
    factor_of = 1.0
    for position, shards_of in cuts:
        draws = jax.random.uniform(jax.random.fold_in(jax.random.fold_in(rng, 6), position), (shards_of,), jnp.float32, smallest / len(cuts), largest / len(cuts))
        factor_of = factor_of * jnp.repeat(jnp.exp(draws), shape[position] // shards_of).reshape((-1,) + (1,) * (len(shape) - 1 - position))
    return factor_of


def rank_bounds(count, lean):
    portions = [(1 << 20) // math.isqrt(rank ** lean) + 1 for rank in range(1, count + 1)]
    scale = 1 + sum(portions) // (1 << 30)
    return np.cumsum(np.array([max(1, weight // scale) for weight in portions]))


def skewed_ids(stream_key, shape, amount, lean):
    table = rank_bounds(amount, lean)
    ticket = jax.random.randint(jax.random.fold_in(stream_key, 1), shape, 0, int(table[amount - 1]))
    grade = jnp.searchsorted(jnp.asarray(table, jnp.int32), ticket, side="right")
    return jax.random.permutation(jax.random.fold_in(stream_key, 2), amount)[grade].astype(jnp.int32)


def bell_draw(key, dims, spread, reach, cuts=(), kind=jnp.bfloat16):
    gain = shard_levels(key, dims, cuts, -0.22, 0.18) if cuts else 1.0
    array = jax.random.normal(key, dims, jnp.float32) * spread * gain
    return jnp.minimum(jnp.maximum(array, -reach), reach).astype(kind)


def setup_inputs(seed: int = 0) -> dict:
    streams_of = jax.random.split(jax.random.key(seed), 9)
    return {
        "tiles": bell_draw(streams_of[0], (NT, B, B * B), 1.0, 6.0, ((0, 32),)),
        "block_one": plant(skewed_ids(streams_of[1], (NT,), NB1, 1), jax.random.fold_in(streams_of[1], 3), 0, NB1 - 1).astype(jnp.int32),
        "block_two": plant(jax.random.randint(streams_of[2], (NT,), 0, NB2), jax.random.fold_in(streams_of[2], 1), 0, NB2 - 1).astype(jnp.int32),
        "block_three": plant(jax.random.randint(streams_of[3], (NT,), 0, NB3), jax.random.fold_in(streams_of[3], 1), 0, NB3 - 1).astype(jnp.int32),
        "owner_map": jax.random.permutation(streams_of[4], NB1).astype(jnp.int32),
        "u_one": draw_u_one(jax.random.fold_in(streams_of[8], 71), 0),
        "u_two": bell_draw(streams_of[6], (R, NB2 * B), 1.0, 6.0, ((1, 8),)),
        "u_three": bell_draw(streams_of[7], (R, NB3 * B), 1.0, 6.0),
    }


def pick(table, index, width):
    grid = table.reshape(table.shape[0], -1, width)
    return jnp.transpose(jnp.take(grid, index, axis=1), (1, 0, 2))

def orthonormal(rows):
    hi = lax.Precision.HIGHEST
    g0 = jnp.dot(rows, rows.T, precision=hi, preferred_element_type=jnp.float32)
    msq = jnp.trace(g0) / NROWS
    inv = 1.0 / jnp.sqrt(msq + 1e-06)
    x = rows * inv
    g = g0 * (inv * inv) / NROWS
    eye = jnp.eye(R, dtype=jnp.float32)
    for step in range(NS_STEPS):
        if step > 0:
            g = jnp.dot(x, x.T, precision=hi, preferred_element_type=jnp.float32) / NROWS
        x = jnp.dot(1.5 * eye - 0.5 * g, x, precision=hi, preferred_element_type=jnp.float32)
    return x

def reference(tiles, block_one, block_two, block_three, owner_map, u_one, u_two, u_three):
    hi = lax.Precision.HIGHEST
    count = tiles.shape[0]
    groups = count // TILE_DEV
    positions = jnp.take(owner_map, block_one).astype(jnp.int32)
    two_pick = pick(u_two, block_two, B).reshape(groups, TILE_DEV, R, B)
    three_pick = pick(u_three, block_three, B).reshape(groups, TILE_DEV, R, B)

    def product_group(args):
        cube, two, three = args
        cube = cube.reshape(TILE_DEV, B, B, B).astype(jnp.float32)
        first = jnp.einsum('tijk,tsk->tijs', cube, three.astype(jnp.float32), precision=hi).astype(jnp.bfloat16)
        second = jnp.einsum('tijs,trj->tirs', first.astype(jnp.float32), two.astype(jnp.float32), precision=hi)
        return second.reshape(TILE_DEV, B, R * R).astype(jnp.bfloat16)
    prods = lax.map(product_group, (tiles.reshape(groups, TILE_DEV, B, B * B), two_pick, three_pick))
    pos_groups = positions.reshape(groups, TILE_DEV)
    current = u_one
    for it in range(ITERS):
        blocks = pick(current.astype(jnp.bfloat16), positions, B).reshape(groups, TILE_DEV, R, B)

        def add_w(total, args):
            prod, blk = args
            return (total + jnp.einsum('tic,tri->rc', prod.astype(jnp.float32), blk.astype(jnp.float32), precision=hi), None)
        project, _ = lax.scan(add_w, jnp.zeros((R, R * R), jnp.float32), (prods, blocks))
        project = project.astype(jnp.bfloat16).astype(jnp.float32)

        def add_z(total, args):
            prod, pos = args
            z_tile = jnp.einsum('rc,tic->tri', project, prod.astype(jnp.float32), precision=hi)
            return (total.at[:, pos, :].add(jnp.transpose(z_tile, (1, 0, 2))), None)
        rows, _ = lax.scan(add_z, jnp.zeros((R, NB1, B), jnp.float32), (prods, pos_groups))
        current = orthonormal(rows.reshape(R, NB1 * B))
    tile_factor = pick(current.astype(jnp.bfloat16), positions, B).reshape(count, R * B)
    return (current, tile_factor)
```

```python
import functools

import jax
import jax.numpy as jnp
from jax import lax
from jax.experimental import pallas as pl
from jax.experimental.pallas import tpu as pltpu
from jax.sharding import PartitionSpec as P

NS_STEPS = 2
HI = lax.Precision.HIGHEST
LANES = 128
META = 16
F32 = jnp.float32
BF16 = jnp.bfloat16


def pick(table, index, width):
    grid = table.reshape(table.shape[0], -1, width)
    return jnp.transpose(jnp.take(grid, index, axis=1), (1, 0, 2))


def orthonormal(rows, rows_total):
    rank = rows.shape[0]
    g0 = jnp.dot(rows, rows.T, precision=HI, preferred_element_type=F32)
    msq = jnp.trace(g0) / rows_total
    inv = 1.0 / jnp.sqrt(msq + 1e-06)
    x = rows * inv
    g = g0 * (inv * inv) / rows_total
    eye = jnp.eye(rank, dtype=F32)
    for step in range(NS_STEPS):
        if step > 0:
            g = jnp.dot(x, x.T, precision=HI, preferred_element_type=F32) / rows_total
        x = jnp.dot(1.5 * eye - 0.5 * g, x, precision=HI, preferred_element_type=F32)
    return x


def general(tiles, block_one, block_two, block_three, owner_map, u_one, u_two, u_three):
    count, width = tiles.shape[:2]
    rank = u_three.shape[0]
    blocks_total = owner_map.shape[0]
    rows_total = blocks_total * width
    two_full = lax.all_gather(u_two, "tiles", axis=1, tiled=True)
    two_pick = pick(two_full, block_two, width)
    three_pick = pick(u_three, block_three, width)
    cube = tiles.reshape(count, width, width, width)
    first = jnp.einsum("tijk,tsk->tijs", cube, three_pick, preferred_element_type=F32).astype(BF16)
    second = jnp.einsum("tijs,trj->tirs", first, two_pick, preferred_element_type=F32)
    products = second.reshape(count, width, rank * rank).astype(BF16)
    positions = jnp.take(owner_map, block_one)
    onehot = (positions[:, None] == jnp.arange(blocks_total, dtype=jnp.int32)[None, :]).astype(F32)
    current = lax.all_gather(u_one.astype(BF16), "tiles", axis=1, tiled=True)
    readers = pick(current, positions, width)
    partial_value = jnp.einsum("tic,tri->rc", products, readers, preferred_element_type=F32)
    project = lax.psum(partial_value, ("tiles", "rep")).astype(BF16)
    z_tile = jnp.einsum("rc,tic->tri", project, products, preferred_element_type=F32)
    term = jnp.einsum("tri,tn->rni", z_tile, onehot, precision=HI).reshape(rank, rows_total)
    rows = lax.psum(term, ("tiles", "rep"))
    current = orthonormal(rows, rows_total)
    tile_factor = pick(current.astype(BF16), positions, width).reshape(count, rank * width)
    own = u_one.shape[1]
    factor = lax.dynamic_slice_in_dim(current, lax.axis_index("tiles") * own, own, 1)
    return (factor, tile_factor)


def lane_iota(shape):
    return lax.broadcasted_iota(jnp.int32, shape, len(shape) - 1)


def row_iota(shape):
    return lax.broadcasted_iota(jnp.int32, shape, len(shape) - 2)


def nt(a, b, precision=None):
    return lax.dot_general(
        a, b, (((1,), (1,)), ((), ())), precision=precision, preferred_element_type=F32
    )


def first_kernel(one, two, three, owner, tiles, u_three, u_two, u_one, out, scratch, two_f32):
    count, width = tiles.shape[:2]
    rank = u_three.shape[0]
    half = LANES // 2
    group = LANES // rank
    span = group * width
    weights = []
    for t in range(count):
        block = three[t]
        start = pl.multiple_of((block // 2) * LANES, LANES)
        window = u_three[:, pl.ds(start, LANES)].astype(F32)
        same = (lane_iota(window.shape) // half) == (block % 2)
        both = jnp.where(same, window, pltpu.roll(window, half, 1))
        full = jnp.concatenate([jnp.concatenate([both] * (span // LANES), axis=1)] * group, axis=0)
        keep = (row_iota(full.shape) // rank) == (lane_iota(full.shape) // width)
        weights.append(jnp.where(keep, full, 0.0).astype(BF16))
    for g in range(tiles.shape[2] // span):
        parts = [nt(weights[t], tiles[t, :, g * span : (g + 1) * span]) for t in range(count)]
        scratch[g * LANES : (g + 1) * LANES, :] = jnp.concatenate(parts, axis=1)

    share = META // 2
    q = lax.axis_index("rep")
    two_f32[...] = u_two[...].astype(F32)
    top = two_f32[pl.ds(pl.multiple_of(q * share, share), share), :]
    low = u_one[pl.ds(pl.multiple_of(q * share, share), share), :]
    lane = lane_iota((share, half))
    ints = jnp.zeros((share, half), F32)
    for t in range(count):
        ints = jnp.where(lane == t, two[t].astype(F32), ints)
        ints = jnp.where(lane == count + t, owner[one[t]].astype(F32), ints)
    meta = jnp.concatenate([top, jnp.concatenate([low, ints], axis=1)], axis=0).astype(BF16)
    for s in range(rank):
        out[s, 0:width, :] = scratch[pl.ds(s, width, stride=rank), :].astype(BF16)
        out[s, width : width + META, :] = meta


def rows_kernel(reps, got, out, two, one, ints, ints_smem, total):
    sources, depth = got.shape[:2]
    width = depth - META
    half = LANES // 2
    share = META // 2
    rank = share * reps
    count = LANES // width
    owners = sources // reps
    for src in range(sources):
        t, q = divmod(src, reps)
        meta = got[src, width:depth, :].astype(F32)
        two[t, q * share : (q + 1) * share, :] = meta[:share]
        one[t, q * share : (q + 1) * share, :] = meta[share:]
        ints[src : src + 1, :] = meta[share : share + 1].astype(jnp.int32)
    pltpu.sync_copy(ints, ints_smem)
    total[...] = jnp.zeros_like(total)
    lane = lane_iota((rank, LANES))
    for src in range(sources):
        block = got[src, 0:width, :]
        moving = jnp.concatenate([block, block], axis=0)
        picks = []
        for t in range(count):
            b = ints_smem[src, half + t]
            picks.append(jnp.where((lane // half) == (b % 2), two[b // 2], 0.0))
        stacked = jnp.concatenate(picks, axis=0).astype(BF16)
        product = jnp.dot(stacked, moving, preferred_element_type=F32)
        for t in range(count):
            p = ints_smem[src, half + count + t]
            mine = product[t * rank : (t + 1) * rank].astype(BF16).astype(F32)
            total[p] += jnp.where((lane // width) == t, mine, 0.0)
    sums = []
    for p in range(owners):
        value = total[p]
        sums.append((value + pltpu.roll(value, half, 1))[:, :half])
    table = jnp.concatenate(sums, axis=1)
    readers = jnp.concatenate([one[p][:, :half] for p in range(owners)], axis=1)
    project = nt(readers, table, HI).astype(BF16).astype(F32)
    out[...] = jnp.dot(project, table, precision=HI, preferred_element_type=F32).astype(BF16)


def final_kernel(one, owner, a, b, c, d, factor, tile_factor, table):
    rank, rows_total = a.shape
    half = LANES // 2
    rows = (a[...].astype(F32) + b[...].astype(F32)) + (c[...].astype(F32) + d[...].astype(F32))
    g0 = nt(rows, rows, HI)
    eye = (row_iota(g0.shape) == lane_iota(g0.shape)).astype(F32)
    msq = jnp.sum(g0 * eye, keepdims=True) / rows_total
    inv = 1.0 / jnp.sqrt(msq + 1e-06)
    x = rows * inv
    g = g0 * (inv * inv) / rows_total
    for step in range(NS_STEPS):
        if step > 0:
            g = nt(x, x, HI) / rows_total
        x = jnp.dot(1.5 * eye - 0.5 * g, x, precision=HI, preferred_element_type=F32)
    table[...] = x

    def block(p):
        window = table[:, pl.ds(pl.multiple_of((p // 2) * LANES, LANES), LANES)]
        return jnp.where(p % 2 == 1, pltpu.roll(window, half, 1), window)[:, :half]

    factor[...] = block(lax.axis_index("tiles"))
    for t in range(tile_factor.shape[0]):
        value = block(owner[one[t]])
        for r in range(0, rank, 2):
            line = jnp.concatenate([value[r : r + 1], value[r + 1 : r + 2]], axis=1)
            tile_factor[t : t + 1, r * half : (r + 2) * half] = line.astype(BF16)


def swap(x, size, mask):
    return lax.ppermute(x, ("tiles", "rep"), [(i, i ^ mask) for i in range(size)])


def sliced(tiles, block_one, block_two, block_three, owner_map, u_one, u_two, u_three):
    count, width = tiles.shape[:2]
    rank = u_three.shape[0]
    owners = lax.axis_size("tiles")
    reps = lax.axis_size("rep")
    size = owners * reps
    rows_total = owner_map.shape[0] * width
    smem = pl.BlockSpec(memory_space=pltpu.SMEM)
    vmem = pl.BlockSpec(memory_space=pltpu.VMEM)
    params = pltpu.CompilerParams(vmem_limit_bytes=32 * 1024 * 1024)
    sends = pl.pallas_call(
        first_kernel,
        out_shape=jax.ShapeDtypeStruct((rank, width + META, LANES), BF16),
        in_specs=[smem] * 4 + [vmem] * 4,
        out_specs=vmem,
        scratch_shapes=[
            pltpu.VMEM((width * rank, LANES), F32),
            pltpu.VMEM(u_two.shape, F32),
        ],
        compiler_params=params,
        name="first",
    )(block_one, block_two, block_three, owner_map, tiles, u_three, u_two, u_one)
    got = lax.all_to_all(sends, ("tiles", "rep"), 0, 0, tiled=True)
    part = pl.pallas_call(
        functools.partial(rows_kernel, reps),
        out_shape=jax.ShapeDtypeStruct((rank, rows_total), BF16),
        in_specs=[vmem],
        out_specs=vmem,
        scratch_shapes=[
            pltpu.VMEM((owners, rank, LANES), F32),
            pltpu.VMEM((owners, rank, LANES), F32),
            pltpu.VMEM((size, LANES), jnp.int32),
            pltpu.SMEM((size, LANES), jnp.int32),
            pltpu.VMEM((owners, rank, LANES), F32),
        ],
        compiler_params=params,
        name="rows_part",
    )(got)
    part = (part.astype(F32) + swap(part, size, 1).astype(F32)).astype(BF16)
    m, n = 2, 4
    pair = part.astype(F32) + swap(part, size, m | 1).astype(F32)
    other = swap(part, size, n | 1).astype(F32) + swap(part, size, m ^ n).astype(F32)
    part = (pair + other).astype(BF16)
    m, n = 8, 16
    parts = [part, swap(part, size, m | 1), swap(part, size, n | 1), swap(part, size, m ^ n)]
    return pl.pallas_call(
        final_kernel,
        out_shape=(
            jax.ShapeDtypeStruct(u_one.shape, F32),
            jax.ShapeDtypeStruct((count, rank * width), BF16),
        ),
        in_specs=[smem] * 2 + [vmem] * 4,
        out_specs=(vmem, vmem),
        scratch_shapes=[pltpu.VMEM((rank, rows_total), F32)],
        compiler_params=params,
        name="final",
    )(block_one, owner_map, *parts)


def per_device(*args):
    tiles, _, _, _, owner_map, u_one, u_two, u_three = args
    count, width = tiles.shape[:2]
    rank = u_three.shape[0]
    owners = lax.axis_size("tiles")
    reps = lax.axis_size("rep")
    fits = (
        owners * reps == rank == 32
        and reps * META // 2 == rank
        and width * 2 == LANES
        and count == 2
        and owner_map.shape[0] == owners
        and u_one.shape[1] == width
        and u_two.shape[1] == LANES
    )
    return (sliced if fits else general)(*args)


def solution(mesh):
    in_specs = (
        P(("tiles", "rep"), None, None),
        P(("tiles", "rep")),
        P(("tiles", "rep")),
        P(("tiles", "rep")),
        P(),
        P(None, "tiles"),
        P(None, "tiles"),
        P(),
    )
    out_specs = (P(None, "tiles"), P(("tiles", "rep"), None))
    return jax.shard_map(
        per_device, mesh=mesh, in_specs=in_specs, out_specs=out_specs, check_vma=False
    )
```

```python
import functools

import jax
import jax.numpy as jnp
from jax import lax
from jax.experimental import pallas as pl
from jax.experimental.pallas import tpu as pltpu
from jax.sharding import PartitionSpec as P

NS_STEPS = 2
HI = lax.Precision.HIGHEST
LANES = 128
WIDE = 60 * 1024 * 1024
NARROW = 16 * 1024 * 1024
META = 16
F32 = jnp.float32
BF16 = jnp.bfloat16


def pick(table, index, width):
    grid = table.reshape(table.shape[0], -1, width)
    return jnp.transpose(jnp.take(grid, index, axis=1), (1, 0, 2))


def orthonormal(rows, rows_total):
    rank = rows.shape[0]
    g0 = jnp.dot(rows, rows.T, precision=HI, preferred_element_type=F32)
    msq = jnp.trace(g0) / rows_total
    inv = 1.0 / jnp.sqrt(msq + 1e-06)
    x = rows * inv
    g = g0 * (inv * inv) / rows_total
    eye = jnp.eye(rank, dtype=F32)
    for step in range(NS_STEPS):
        if step > 0:
            g = jnp.dot(x, x.T, precision=HI, preferred_element_type=F32) / rows_total
        x = jnp.dot(1.5 * eye - 0.5 * g, x, precision=HI, preferred_element_type=F32)
    return x


def general(tiles, block_one, block_two, block_three, owner_map, u_one, u_two, u_three):
    count, width = tiles.shape[:2]
    rank = u_three.shape[0]
    blocks_total = owner_map.shape[0]
    rows_total = blocks_total * width
    two_full = lax.all_gather(u_two, "tiles", axis=1, tiled=True)
    two_pick = pick(two_full, block_two, width)
    three_pick = pick(u_three, block_three, width)
    cube = tiles.reshape(count, width, width, width)
    first = jnp.einsum("tijk,tsk->tijs", cube, three_pick, preferred_element_type=F32).astype(BF16)
    second = jnp.einsum("tijs,trj->tirs", first, two_pick, preferred_element_type=F32)
    products = second.reshape(count, width, rank * rank).astype(BF16)
    positions = jnp.take(owner_map, block_one)
    onehot = (positions[:, None] == jnp.arange(blocks_total, dtype=jnp.int32)[None, :]).astype(F32)
    current = lax.all_gather(u_one.astype(BF16), "tiles", axis=1, tiled=True)
    readers = pick(current, positions, width)
    partial_value = jnp.einsum("tic,tri->rc", products, readers, preferred_element_type=F32)
    project = lax.psum(partial_value, ("tiles", "rep")).astype(BF16)
    z_tile = jnp.einsum("rc,tic->tri", project, products, preferred_element_type=F32)
    term = jnp.einsum("tri,tn->rni", z_tile, onehot, precision=HI).reshape(rank, rows_total)
    rows = lax.psum(term, ("tiles", "rep"))
    current = orthonormal(rows, rows_total)
    tile_factor = pick(current.astype(BF16), positions, width).reshape(count, rank * width)
    own = u_one.shape[1]
    factor = lax.dynamic_slice_in_dim(current, lax.axis_index("tiles") * own, own, 1)
    return (factor, tile_factor)


def lane_iota(shape):
    return lax.broadcasted_iota(jnp.int32, shape, len(shape) - 1)


def row_iota(shape):
    return lax.broadcasted_iota(jnp.int32, shape, len(shape) - 2)


def nt(a, b, precision=None):
    return lax.dot_general(
        a, b, (((1,), (1,)), ((), ())), precision=precision, preferred_element_type=F32
    )


def first_kernel(
    one_hbm, two_hbm, three_hbm, owner_hbm, tiles_hbm, u_three_hbm, u_two_hbm, u_one_hbm, out,
    one, two, three, owner, tiles, u_three, u_two, u_one, scratch, two_f32, sems,
):
    count, width = tiles.shape[:2]
    rank = u_three.shape[0]
    half = LANES // 2
    group = LANES // rank
    span = group * width
    moves = [(three_hbm, three), (u_three_hbm, u_three)]
    moves += [(tiles_hbm.at[t], tiles.at[t]) for t in range(count)]
    moves += [(u_two_hbm, u_two), (u_one_hbm, u_one)]
    moves += [(two_hbm, two), (one_hbm, one), (owner_hbm, owner)]
    copies = [pltpu.make_async_copy(a, b, sems.at[i]) for i, (a, b) in enumerate(moves)]
    for copy in copies:
        copy.start()
    copies[0].wait()
    copies[1].wait()
    weights = []
    for t in range(count):
        block = three[t]
        start = pl.multiple_of((block // 2) * LANES, LANES)
        window = u_three[:, pl.ds(start, LANES)].astype(F32)
        same = (lane_iota(window.shape) // half) == (block % 2)
        both = jnp.where(same, window, pltpu.roll(window, half, 1))
        full = jnp.concatenate([jnp.concatenate([both] * (span // LANES), axis=1)] * group, axis=0)
        keep = (row_iota(full.shape) // rank) == (lane_iota(full.shape) // width)
        weights.append(jnp.where(keep, full, 0.0).astype(BF16))
    for copy in copies[2:]:
        copy.wait()
    for g in range(tiles.shape[2] // span):
        parts = [nt(weights[t], tiles[t, :, g * span : (g + 1) * span]) for t in range(count)]
        scratch[g * LANES : (g + 1) * LANES, :] = jnp.concatenate(parts, axis=1)

    share = META // 2
    q = lax.axis_index("rep")
    two_f32[...] = u_two[...].astype(F32)
    top = two_f32[pl.ds(pl.multiple_of(q * share, share), share), :]
    low = u_one[pl.ds(pl.multiple_of(q * share, share), share), :]
    lane = lane_iota((share, half))
    ints = jnp.zeros((share, half), F32)
    for t in range(count):
        ints = jnp.where(lane == t, two[t].astype(F32), ints)
        ints = jnp.where(lane == count + t, owner[one[t]].astype(F32), ints)
    meta = jnp.concatenate([top, jnp.concatenate([low, ints], axis=1)], axis=0).astype(BF16)
    for s in range(rank):
        out[s, 0:width, :] = scratch[pl.ds(s, width, stride=rank), :].astype(BF16)
        out[s, width : width + META, :] = meta


def rows_kernel(reps, got, out, two, one, ints, ints_smem, total):
    sources, depth = got.shape[:2]
    width = depth - META
    half = LANES // 2
    share = META // 2
    rank = share * reps
    count = LANES // width
    owners = sources // reps
    for src in range(sources):
        t, q = divmod(src, reps)
        meta = got[src, width:depth, :].astype(F32)
        two[t, q * share : (q + 1) * share, :] = meta[:share]
        one[t, q * share : (q + 1) * share, :] = meta[share:]
        ints[src : src + 1, :] = meta[share : share + 1].astype(jnp.int32)
    pltpu.sync_copy(ints, ints_smem)
    total[...] = jnp.zeros_like(total)
    lane = lane_iota((rank, LANES))
    for src in range(sources):
        block = got[src, 0:width, :]
        moving = jnp.concatenate([block, block], axis=0)
        picks = []
        for t in range(count):
            b = ints_smem[src, half + t]
            picks.append(jnp.where((lane // half) == (b % 2), two[b // 2], 0.0))
        stacked = jnp.concatenate(picks, axis=0).astype(BF16)
        product = jnp.dot(stacked, moving, preferred_element_type=F32)
        for t in range(count):
            p = ints_smem[src, half + count + t]
            mine = product[t * rank : (t + 1) * rank].astype(BF16).astype(F32)
            total[p] += jnp.where((lane // width) == t, mine, 0.0)
    sums = []
    for p in range(owners):
        value = total[p]
        sums.append((value + pltpu.roll(value, half, 1))[:, :half])
    table = jnp.concatenate(sums, axis=1)
    readers = jnp.concatenate([one[p][:, :half] for p in range(owners)], axis=1)
    project = nt(readers, table, HI).astype(BF16).astype(F32)
    out[...] = jnp.dot(project, table, precision=HI, preferred_element_type=F32).astype(BF16)


def final_kernel(one, owner, a, b, c, d, factor, tile_factor, table):
    rank, rows_total = a.shape
    half = LANES // 2
    rows = (a[...].astype(F32) + b[...].astype(F32)) + (c[...].astype(F32) + d[...].astype(F32))
    g0 = nt(rows, rows, HI)
    eye = (row_iota(g0.shape) == lane_iota(g0.shape)).astype(F32)
    msq = jnp.sum(g0 * eye, keepdims=True) / rows_total
    inv = 1.0 / jnp.sqrt(msq + 1e-06)
    x = rows * inv
    g = g0 * (inv * inv) / rows_total
    for step in range(NS_STEPS):
        if step > 0:
            g = nt(x, x, HI) / rows_total
        x = jnp.dot(1.5 * eye - 0.5 * g, x, precision=HI, preferred_element_type=F32)
    table[...] = x

    def block(p):
        window = table[:, pl.ds(pl.multiple_of((p // 2) * LANES, LANES), LANES)]
        return jnp.where(p % 2 == 1, pltpu.roll(window, half, 1), window)[:, :half]

    factor[...] = block(lax.axis_index("tiles"))
    for t in range(tile_factor.shape[0]):
        value = block(owner[one[t]])
        for r in range(0, rank, 2):
            line = jnp.concatenate([value[r : r + 1], value[r + 1 : r + 2]], axis=1)
            tile_factor[t : t + 1, r * half : (r + 2) * half] = line.astype(BF16)


def swap(x, size, mask):
    return lax.ppermute(x, ("tiles", "rep"), [(i, i ^ mask) for i in range(size)])


def sliced(tiles, block_one, block_two, block_three, owner_map, u_one, u_two, u_three):
    count, width = tiles.shape[:2]
    rank = u_three.shape[0]
    owners = lax.axis_size("tiles")
    reps = lax.axis_size("rep")
    size = owners * reps
    rows_total = owner_map.shape[0] * width
    smem = pl.BlockSpec(memory_space=pltpu.SMEM)
    vmem = pl.BlockSpec(memory_space=pltpu.VMEM)
    wide = pltpu.CompilerParams(vmem_limit_bytes=WIDE)
    narrow = pltpu.CompilerParams(vmem_limit_bytes=NARROW)
    ints = (block_one, block_two, block_three, owner_map)
    arrays = (tiles, u_three, u_two, u_one)
    sends = pl.pallas_call(
        first_kernel,
        out_shape=jax.ShapeDtypeStruct((rank, width + META, LANES), BF16),
        in_specs=[pl.BlockSpec(memory_space=pltpu.HBM)] * 8,
        out_specs=vmem,
        scratch_shapes=[pltpu.SMEM(x.shape, x.dtype) for x in ints]
        + [pltpu.VMEM(x.shape, x.dtype) for x in arrays]
        + [
            pltpu.VMEM((width * rank, LANES), F32),
            pltpu.VMEM(u_two.shape, F32),
            pltpu.SemaphoreType.DMA((len(ints) + len(arrays) + count - 1,)),
        ],
        compiler_params=wide,
        name="first",
    )(*ints, *arrays)
    got = lax.all_to_all(sends, ("tiles", "rep"), 0, 0, tiled=True)
    part = pl.pallas_call(
        functools.partial(rows_kernel, reps),
        out_shape=jax.ShapeDtypeStruct((rank, rows_total), BF16),
        in_specs=[vmem],
        out_specs=vmem,
        scratch_shapes=[
            pltpu.VMEM((owners, rank, LANES), F32),
            pltpu.VMEM((owners, rank, LANES), F32),
            pltpu.VMEM((size, LANES), jnp.int32),
            pltpu.SMEM((size, LANES), jnp.int32),
            pltpu.VMEM((owners, rank, LANES), F32),
        ],
        compiler_params=narrow,
        name="rows_part",
    )(got)
    part = (part.astype(F32) + swap(part, size, 1).astype(F32)).astype(BF16)
    m, n = 2, 4
    pair = part.astype(F32) + swap(part, size, m | 1).astype(F32)
    other = swap(part, size, n | 1).astype(F32) + swap(part, size, m ^ n).astype(F32)
    part = (pair + other).astype(BF16)
    m, n = 8, 16
    parts = [part, swap(part, size, m | 1), swap(part, size, n | 1), swap(part, size, m ^ n)]
    return pl.pallas_call(
        final_kernel,
        out_shape=(
            jax.ShapeDtypeStruct(u_one.shape, F32),
            jax.ShapeDtypeStruct((count, rank * width), BF16),
        ),
        in_specs=[smem] * 2 + [vmem] * 4,
        out_specs=(vmem, vmem),
        scratch_shapes=[pltpu.VMEM((rank, rows_total), F32)],
        compiler_params=narrow,
        name="final",
    )(block_one, owner_map, *parts)


def per_device(*args):
    tiles, _, _, _, owner_map, u_one, u_two, u_three = args
    count, width = tiles.shape[:2]
    rank = u_three.shape[0]
    owners = lax.axis_size("tiles")
    reps = lax.axis_size("rep")
    fits = (
        owners * reps == rank == 32
        and reps * META // 2 == rank
        and width * 2 == LANES
        and count == 2
        and owner_map.shape[0] == owners
        and u_one.shape[1] == width
        and u_two.shape[1] == LANES
    )
    return (sliced if fits else general)(*args)


def solution(mesh):
    in_specs = (
        P(("tiles", "rep"), None, None),
        P(("tiles", "rep")),
        P(("tiles", "rep")),
        P(("tiles", "rep")),
        P(),
        P(None, "tiles"),
        P(None, "tiles"),
        P(),
    )
    out_specs = (P(None, "tiles"), P(("tiles", "rep"), None))
    return jax.shard_map(
        per_device, mesh=mesh, in_specs=in_specs, out_specs=out_specs, check_vma=False
    )
```

```python
import functools

import jax
import jax.numpy as jnp
from jax import lax
from jax.experimental import pallas as pl
from jax.experimental.pallas import tpu as pltpu
from jax.sharding import PartitionSpec as P

NS_STEPS = 2
HI = lax.Precision.HIGHEST
LANES = 128
NARROW = 16 * 1024 * 1024
META = 16
F32 = jnp.float32
BF16 = jnp.bfloat16


def pick(table, index, width):
    grid = table.reshape(table.shape[0], -1, width)
    return jnp.transpose(jnp.take(grid, index, axis=1), (1, 0, 2))


def orthonormal(rows, rows_total):
    rank = rows.shape[0]
    g0 = jnp.dot(rows, rows.T, precision=HI, preferred_element_type=F32)
    msq = jnp.trace(g0) / rows_total
    inv = 1.0 / jnp.sqrt(msq + 1e-06)
    x = rows * inv
    g = g0 * (inv * inv) / rows_total
    eye = jnp.eye(rank, dtype=F32)
    for step in range(NS_STEPS):
        if step > 0:
            g = jnp.dot(x, x.T, precision=HI, preferred_element_type=F32) / rows_total
        x = jnp.dot(1.5 * eye - 0.5 * g, x, precision=HI, preferred_element_type=F32)
    return x


def general(tiles, block_one, block_two, block_three, owner_map, u_one, u_two, u_three):
    count, width = tiles.shape[:2]
    rank = u_three.shape[0]
    blocks_total = owner_map.shape[0]
    rows_total = blocks_total * width
    two_full = lax.all_gather(u_two, "tiles", axis=1, tiled=True)
    two_pick = pick(two_full, block_two, width)
    three_pick = pick(u_three, block_three, width)
    cube = tiles.reshape(count, width, width, width)
    first = jnp.einsum("tijk,tsk->tijs", cube, three_pick, preferred_element_type=F32).astype(BF16)
    second = jnp.einsum("tijs,trj->tirs", first, two_pick, preferred_element_type=F32)
    products = second.reshape(count, width, rank * rank).astype(BF16)
    positions = jnp.take(owner_map, block_one)
    onehot = (positions[:, None] == jnp.arange(blocks_total, dtype=jnp.int32)[None, :]).astype(F32)
    current = lax.all_gather(u_one.astype(BF16), "tiles", axis=1, tiled=True)
    readers = pick(current, positions, width)
    partial_value = jnp.einsum("tic,tri->rc", products, readers, preferred_element_type=F32)
    project = lax.psum(partial_value, ("tiles", "rep")).astype(BF16)
    z_tile = jnp.einsum("rc,tic->tri", project, products, preferred_element_type=F32)
    term = jnp.einsum("tri,tn->rni", z_tile, onehot, precision=HI).reshape(rank, rows_total)
    rows = lax.psum(term, ("tiles", "rep"))
    current = orthonormal(rows, rows_total)
    tile_factor = pick(current.astype(BF16), positions, width).reshape(count, rank * width)
    own = u_one.shape[1]
    factor = lax.dynamic_slice_in_dim(current, lax.axis_index("tiles") * own, own, 1)
    return (factor, tile_factor)


def split(a):
    high = a.astype(BF16)
    return high, (a - high.astype(F32)).astype(BF16)


def dot3(a, b, axis=0):
    (ah, al), (bh, bl) = split(a), split(b)
    left = jnp.concatenate([ah, al, ah], axis=1)
    right = jnp.concatenate([bh, bh, bl], axis=axis)
    return lax.dot_general(left, right, (((1,), (axis,)), ((), ())), preferred_element_type=F32)


def lane_iota(shape):
    return lax.broadcasted_iota(jnp.int32, shape, len(shape) - 1)


def row_iota(shape):
    return lax.broadcasted_iota(jnp.int32, shape, len(shape) - 2)


def nt(a, b, precision=None):
    return lax.dot_general(
        a, b, (((1,), (1,)), ((), ())), precision=precision, preferred_element_type=F32
    )


def first_kernel(
    one_hbm, two_hbm, three_hbm, owner_hbm, tiles_hbm, u_three_hbm, u_two_hbm, u_one_hbm, out,
    one, two, three, owner, tiles, u_three, u_two, u_one, two_f32, in_sems, tile_sems,
):
    count, width = tiles.shape[:2]
    rank = u_three.shape[0]
    half = LANES // 2
    share = META // 2
    span = share * width
    pieces = tiles.shape[2] // (2 * span)
    moves = [(three_hbm, three), (u_three_hbm, u_three), (two_hbm, two), (one_hbm, one)]
    moves += [(owner_hbm, owner), (u_two_hbm, u_two), (u_one_hbm, u_one)]
    copies = [pltpu.make_async_copy(a, b, in_sems.at[i]) for i, (a, b) in enumerate(moves)]
    loads = [
        pltpu.make_async_copy(tiles_hbm.at[t], tiles.at[t], tile_sems.at[t]) for t in range(count)
    ]
    for copy in copies[:2] + loads + copies[2:]:
        copy.start()
    copies[0].wait()
    copies[1].wait()
    weights = []
    for t in range(count):
        block = three[t]
        start = pl.multiple_of((block // 2) * LANES, LANES)
        window = u_three[:, pl.ds(start, LANES)].astype(F32)
        same = (lane_iota(window.shape) // half) == (block % 2)
        both = jnp.where(same, window, pltpu.roll(window, half, 1))
        tall = jnp.broadcast_to(both[:, None, :], (rank, share, LANES)).reshape(rank * share, LANES)
        full = jnp.concatenate([tall] * (span // LANES), axis=1)
        keep = (row_iota(full.shape) % share) == (lane_iota(full.shape) // width)
        weights.append(jnp.where(keep, full, 0.0).astype(BF16))
    for copy in loads:
        copy.wait()
    for n in range(pieces):
        pair = []
        for g in (2 * n, 2 * n + 1):
            columns = slice(g * span, (g + 1) * span)
            pair.append([nt(weights[t], tiles[t, :, columns]) for t in range(count)])
        rows = slice(2 * n * share, 2 * (n + 1) * share)
        for s in range(rank):
            at = slice(s * share, (s + 1) * share)
            block = [jnp.concatenate([part[at] for part in parts], axis=1) for parts in pair]
            out[s, rows, :] = jnp.concatenate(block, axis=0).astype(BF16)

    for copy in copies[2:]:
        copy.wait()
    q = lax.axis_index("rep")
    two_f32[...] = u_two[...].astype(F32)
    top = two_f32[pl.ds(pl.multiple_of(q * share, share), share), :]
    low = u_one[pl.ds(pl.multiple_of(q * share, share), share), :]
    lane = lane_iota((share, half))
    ints = jnp.zeros((share, half), F32)
    for t in range(count):
        ints = jnp.where(lane == t, two[t].astype(F32), ints)
        ints = jnp.where(lane == count + t, owner[one[t]].astype(F32), ints)
    meta = jnp.concatenate([top, jnp.concatenate([low, ints], axis=1)], axis=0).astype(BF16)
    rows = slice(width, width + META)
    for s in range(rank):
        out[s, rows, :] = meta


def rows_kernel(reps, got, out, two, one, total):
    sources, depth = got.shape[:2]
    width = depth - META
    half = LANES // 2
    share = META // 2
    rank = share * reps
    count = LANES // width
    owners = sources // reps
    blocks = 2 * owners
    lines = []
    for src in range(sources):
        t, q = divmod(src, reps)
        meta = got[src, width:depth, :].astype(F32)
        two[t, q * share : (q + 1) * share, :] = meta[:share]
        one[t, q * share : (q + 1) * share, :] = meta[share:]
        lines.append(meta[share : share + 1])
    lines = jnp.concatenate(lines, axis=0)
    lane = lane_iota(lines.shape)
    scale = jnp.zeros(lines.shape, F32)
    for k in range(2 * count):
        scale = jnp.where(lane == half + k, float(blocks**k), scale)
    code = jnp.sum(lines * scale, axis=1, keepdims=True).astype(jnp.int32)
    total[...] = jnp.zeros_like(total)
    lane = lane_iota((rank, LANES))
    for src in range(sources):
        block = got[src, 0:width, :]
        moving = jnp.concatenate([block, block], axis=0)
        left = code[src, 0]
        digits = []
        for _ in range(2 * count):
            digits.append(left % blocks)
            left = left // blocks
        picks = []
        for b in digits[:count]:
            picks.append(jnp.where((lane // half) == (b % 2), two[b // 2], 0.0))
        stacked = jnp.concatenate(picks, axis=0).astype(BF16)
        product = jnp.dot(stacked, moving, preferred_element_type=F32).astype(BF16).astype(F32)
        for t, p in enumerate(digits[count:]):
            total[t, src % 2, p] += product[t * rank : (t + 1) * rank]
    sums = []
    for p in range(owners):
        low = (total[0, 0, p] + total[0, 1, p])[:, :half]
        high = pltpu.roll(total[1, 0, p] + total[1, 1, p], half, 1)[:, :half]
        sums.append(low + high)
    table = jnp.concatenate(sums, axis=1)
    high = table.astype(BF16)
    low = (table - high.astype(F32)).astype(BF16)
    readers = jnp.concatenate([one[p][:, :half] for p in range(owners)], axis=1).astype(BF16)
    project = (nt(readers, high) + nt(readers, low)).astype(BF16)
    part = jnp.dot(project, high, preferred_element_type=F32)
    part += jnp.dot(project, low, preferred_element_type=F32)
    out[...] = part.astype(BF16)


def final_kernel(one, owner, a, b, c, d, factor, tile_factor, table):
    rank, rows_total = a.shape
    half = LANES // 2
    rows = (a[...].astype(F32) + b[...].astype(F32)) + (c[...].astype(F32) + d[...].astype(F32))
    table[...] = rows
    g0 = dot3(rows, rows, 1)
    eye = (row_iota(g0.shape) == lane_iota(g0.shape)).astype(F32)
    msq = jnp.sum(g0 * eye, keepdims=True) / rows_total
    inv = 1.0 / jnp.sqrt(msq + 1e-06)
    g = g0 * (inv * inv) / rows_total
    square = dot3(g, g)
    outer = dot3(square, 0.0625 * square - 0.5625 * g)
    step = (outer + (1.6875 * square - 2.4375 * g + 2.25 * eye)) * inv

    def block(p):
        window = table[:, pl.ds(pl.multiple_of((p // 2) * LANES, LANES), LANES)]
        return jnp.where(p % 2 == 1, pltpu.roll(window, half, 1), window)[:, :half]

    places = [lax.axis_index("tiles")] + [owner[one[t]] for t in range(tile_factor.shape[0])]
    picked = jnp.concatenate([block(p) for p in places], axis=1)
    x = dot3(step, picked)
    factor[...] = x[:, :half]
    for t in range(tile_factor.shape[0]):
        value = x[:, (t + 1) * half : (t + 2) * half]
        for r in range(0, rank, 2):
            line = jnp.concatenate([value[r : r + 1], value[r + 1 : r + 2]], axis=1)
            tile_factor[t : t + 1, r * half : (r + 2) * half] = line.astype(BF16)


def swap(x, size, mask):
    return lax.ppermute(x, ("tiles", "rep"), [(i, i ^ mask) for i in range(size)])


def sliced(tiles, block_one, block_two, block_three, owner_map, u_one, u_two, u_three):
    count, width = tiles.shape[:2]
    rank = u_three.shape[0]
    owners = lax.axis_size("tiles")
    reps = lax.axis_size("rep")
    size = owners * reps
    rows_total = owner_map.shape[0] * width
    smem = pl.BlockSpec(memory_space=pltpu.SMEM)
    vmem = pl.BlockSpec(memory_space=pltpu.VMEM)
    narrow = pltpu.CompilerParams(vmem_limit_bytes=NARROW)
    ints = (block_one, block_two, block_three, owner_map)
    arrays = (tiles, u_three, u_two, u_one)
    sends = pl.pallas_call(
        first_kernel,
        out_shape=jax.ShapeDtypeStruct((rank, width + META, LANES), BF16),
        in_specs=[pl.BlockSpec(memory_space=pltpu.HBM)] * 8,
        out_specs=vmem,
        scratch_shapes=[pltpu.SMEM(x.shape, x.dtype) for x in ints]
        + [pltpu.VMEM(x.shape, x.dtype) for x in arrays]
        + [
            pltpu.VMEM(u_two.shape, F32),
            pltpu.SemaphoreType.DMA((7,)),
            pltpu.SemaphoreType.DMA((count,)),
        ],
        compiler_params=narrow,
        name="first",
    )(*[pltpu.with_memory_space_constraint(x, pltpu.HBM) for x in ints + arrays])
    got = lax.all_to_all(sends, ("tiles", "rep"), 0, 0, tiled=True)
    part = pl.pallas_call(
        functools.partial(rows_kernel, reps),
        out_shape=jax.ShapeDtypeStruct((rank, rows_total), BF16),
        in_specs=[vmem],
        out_specs=vmem,
        scratch_shapes=[
            pltpu.VMEM((owners, rank, LANES), F32),
            pltpu.VMEM((owners, rank, LANES), F32),
            pltpu.VMEM((count, 2, owners, rank, LANES), F32),
        ],
        compiler_params=narrow,
        name="rows_part",
    )(got)
    part = (part.astype(F32) + swap(part, size, 1).astype(F32)).astype(BF16)
    m, n = 2, 4
    pair = part.astype(F32) + swap(part, size, m | 1).astype(F32)
    other = swap(part, size, n | 1).astype(F32) + swap(part, size, m ^ n).astype(F32)
    part = (pair + other).astype(BF16)
    m, n = 16, 8
    parts = [part, swap(part, size, m | 1), swap(part, size, n | 1), swap(part, size, m ^ n)]
    return pl.pallas_call(
        final_kernel,
        out_shape=(
            jax.ShapeDtypeStruct(u_one.shape, F32),
            jax.ShapeDtypeStruct((count, rank * width), BF16),
        ),
        in_specs=[smem] * 2 + [vmem] * 4,
        out_specs=(vmem, vmem),
        scratch_shapes=[pltpu.VMEM((rank, rows_total), F32)],
        compiler_params=narrow,
        name="final",
    )(block_one, owner_map, *parts)


def per_device(*args):
    tiles, _, _, _, owner_map, u_one, u_two, u_three = args
    count, width = tiles.shape[:2]
    rank = u_three.shape[0]
    owners = lax.axis_size("tiles")
    reps = lax.axis_size("rep")
    fits = (
        owners * reps == rank == 32
        and reps * META // 2 == rank
        and width * 2 == LANES
        and count == 2
        and owner_map.shape[0] == owners
        and u_one.shape[1] == width
        and u_two.shape[1] == LANES
    )
    return (sliced if fits else general)(*args)


def solution(mesh):
    in_specs = (
        P(("tiles", "rep"), None, None),
        P(("tiles", "rep")),
        P(("tiles", "rep")),
        P(("tiles", "rep")),
        P(),
        P(None, "tiles"),
        P(None, "tiles"),
        P(),
    )
    out_specs = (P(None, "tiles"), P(("tiles", "rep"), None))
    return jax.shard_map(
        per_device, mesh=mesh, in_specs=in_specs, out_specs=out_specs, check_vma=False
    )
```

```python
import functools

import jax
import jax.numpy as jnp
from jax import lax
from jax.experimental import pallas as pl
from jax.experimental.pallas import tpu as pltpu
from jax.sharding import PartitionSpec as P

NS_STEPS = 2
HI = lax.Precision.HIGHEST
LANES = 128
NARROW = 16 * 1024 * 1024
META = 16
F32 = jnp.float32
BF16 = jnp.bfloat16


def pick(table, index, width):
    grid = table.reshape(table.shape[0], -1, width)
    return jnp.transpose(jnp.take(grid, index, axis=1), (1, 0, 2))


def orthonormal(rows, rows_total):
    rank = rows.shape[0]
    g0 = jnp.dot(rows, rows.T, precision=HI, preferred_element_type=F32)
    msq = jnp.trace(g0) / rows_total
    inv = 1.0 / jnp.sqrt(msq + 1e-06)
    x = rows * inv
    g = g0 * (inv * inv) / rows_total
    eye = jnp.eye(rank, dtype=F32)
    for step in range(NS_STEPS):
        if step > 0:
            g = jnp.dot(x, x.T, precision=HI, preferred_element_type=F32) / rows_total
        x = jnp.dot(1.5 * eye - 0.5 * g, x, precision=HI, preferred_element_type=F32)
    return x


def general(tiles, block_one, block_two, block_three, owner_map, u_one, u_two, u_three):
    count, width = tiles.shape[:2]
    rank = u_three.shape[0]
    blocks_total = owner_map.shape[0]
    rows_total = blocks_total * width
    two_full = lax.all_gather(u_two, "tiles", axis=1, tiled=True)
    two_pick = pick(two_full, block_two, width)
    three_pick = pick(u_three, block_three, width)
    cube = tiles.reshape(count, width, width, width)
    first = jnp.einsum("tijk,tsk->tijs", cube, three_pick, preferred_element_type=F32).astype(BF16)
    second = jnp.einsum("tijs,trj->tirs", first, two_pick, preferred_element_type=F32)
    products = second.reshape(count, width, rank * rank).astype(BF16)
    positions = jnp.take(owner_map, block_one)
    onehot = (positions[:, None] == jnp.arange(blocks_total, dtype=jnp.int32)[None, :]).astype(F32)
    current = lax.all_gather(u_one.astype(BF16), "tiles", axis=1, tiled=True)
    readers = pick(current, positions, width)
    partial_value = jnp.einsum("tic,tri->rc", products, readers, preferred_element_type=F32)
    project = lax.psum(partial_value, ("tiles", "rep")).astype(BF16)
    z_tile = jnp.einsum("rc,tic->tri", project, products, preferred_element_type=F32)
    term = jnp.einsum("tri,tn->rni", z_tile, onehot, precision=HI).reshape(rank, rows_total)
    rows = lax.psum(term, ("tiles", "rep"))
    current = orthonormal(rows, rows_total)
    tile_factor = pick(current.astype(BF16), positions, width).reshape(count, rank * width)
    own = u_one.shape[1]
    factor = lax.dynamic_slice_in_dim(current, lax.axis_index("tiles") * own, own, 1)
    return (factor, tile_factor)


def split(a):
    high = a.astype(BF16)
    return high, (a - high.astype(F32)).astype(BF16)


def dot3(a, b, axis=0):
    (ah, al), (bh, bl) = split(a), split(b)
    left = jnp.concatenate([ah, al, ah], axis=1)
    right = jnp.concatenate([bh, bh, bl], axis=axis)
    return lax.dot_general(left, right, (((1,), (axis,)), ((), ())), preferred_element_type=F32)


def lane_iota(shape):
    return lax.broadcasted_iota(jnp.int32, shape, len(shape) - 1)


def row_iota(shape):
    return lax.broadcasted_iota(jnp.int32, shape, len(shape) - 2)


def nt(a, b, precision=None):
    return lax.dot_general(
        a, b, (((1,), (1,)), ((), ())), precision=precision, preferred_element_type=F32
    )


def first_kernel(
    one_hbm, two_hbm, three_hbm, owner_hbm, tiles_hbm, u_three_hbm, u_two_hbm, u_one_hbm, out,
    one, two, three, owner, tiles, u_three, u_two, u_one, two_f32, in_sems, tile_sems,
):
    count, width = tiles.shape[:2]
    rank = u_three.shape[0]
    half = LANES // 2
    share = META // 2
    span = share * width
    pieces = tiles.shape[2] // (2 * span)
    moves = [(three_hbm, three), (u_three_hbm, u_three), (two_hbm, two), (one_hbm, one)]
    moves += [(owner_hbm, owner), (u_two_hbm, u_two), (u_one_hbm, u_one)]
    copies = [pltpu.make_async_copy(a, b, in_sems.at[i]) for i, (a, b) in enumerate(moves)]
    loads = [
        pltpu.make_async_copy(tiles_hbm.at[t], tiles.at[t], tile_sems.at[t]) for t in range(count)
    ]
    for copy in copies + loads:
        copy.start()
    copies[0].wait()
    copies[1].wait()
    weights = []
    for t in range(count):
        block = three[t]
        start = pl.multiple_of((block // 2) * LANES, LANES)
        window = u_three[:, pl.ds(start, LANES)].astype(F32)
        same = (lane_iota(window.shape) // half) == (block % 2)
        both = jnp.where(same, window, pltpu.roll(window, half, 1))
        tall = jnp.broadcast_to(both[:, None, :], (rank, share, LANES)).reshape(rank * share, LANES)
        full = jnp.concatenate([tall] * (span // LANES), axis=1)
        keep = (row_iota(full.shape) % share) == (lane_iota(full.shape) // width)
        weights.append(jnp.where(keep, full, 0.0).astype(BF16))
    for copy in copies[2:]:
        copy.wait()
    q = lax.axis_index("rep")
    two_f32[...] = u_two[...].astype(F32)
    top = two_f32[pl.ds(pl.multiple_of(q * share, share), share), :]
    low = u_one[pl.ds(pl.multiple_of(q * share, share), share), :]
    lane = lane_iota((share, half))
    ints = jnp.zeros((share, half), F32)
    for t in range(count):
        ints = jnp.where(lane == t, two[t].astype(F32), ints)
        ints = jnp.where(lane == count + t, owner[one[t]].astype(F32), ints)
    meta = jnp.concatenate([top, jnp.concatenate([low, ints], axis=1)], axis=0).astype(BF16)
    rows = slice(width, width + META)
    for s in range(rank):
        out[s, rows, :] = meta
    for copy in loads:
        copy.wait()
    for n in range(pieces // 2):
        wide = []
        for t in range(count):
            groups = [tiles[t, :, (4 * n + g) * span : (4 * n + g + 1) * span] for g in range(4)]
            wide.append(nt(weights[t], jnp.concatenate(groups, axis=0)))
        for s in range(rank):
            at = slice(s * share, (s + 1) * share)
            for h in range(2):
                block = []
                for g in (2 * h, 2 * h + 1):
                    lanes = slice(g * width, (g + 1) * width)
                    block.append(jnp.concatenate([part[at, lanes] for part in wide], axis=1))
                rows = slice((2 * n + h) * META, (2 * n + h + 1) * META)
                out[s, rows, :] = jnp.concatenate(block, axis=0).astype(BF16)


def rows_kernel(reps, got, out, two, one, total):
    sources, depth = got.shape[:2]
    width = depth - META
    half = LANES // 2
    share = META // 2
    rank = share * reps
    count = LANES // width
    owners = sources // reps
    blocks = 2 * owners
    lines = []
    for src in range(sources):
        t, q = divmod(src, reps)
        meta = got[src, width:depth, :].astype(F32)
        two[t, q * share : (q + 1) * share, :] = meta[:share]
        one[t, q * share : (q + 1) * share, :] = meta[share:]
        lines.append(meta[share : share + 1])
    lines = jnp.concatenate(lines, axis=0)
    lane = lane_iota(lines.shape)
    scale = jnp.zeros(lines.shape, F32)
    for k in range(2 * count):
        scale = jnp.where(lane == half + k, float(blocks**k), scale)
    code = jnp.sum(lines * scale, axis=1, keepdims=True).astype(jnp.int32)
    total[...] = jnp.zeros_like(total)
    lane = lane_iota((rank, LANES))
    for src in range(sources):
        block = got[src, 0:width, :]
        moving = jnp.concatenate([block, block], axis=0)
        left = code[src, 0]
        digits = []
        for _ in range(2 * count):
            digits.append(left % blocks)
            left = left // blocks
        picks = []
        for b in digits[:count]:
            picks.append(jnp.where((lane // half) == (b % 2), two[b // 2], 0.0))
        stacked = jnp.concatenate(picks, axis=0).astype(BF16)
        product = jnp.dot(stacked, moving, preferred_element_type=F32).astype(BF16).astype(F32)
        for t, p in enumerate(digits[count:]):
            total[t, src % 2, p] += product[t * rank : (t + 1) * rank]
    sums = []
    for p in range(owners):
        low = (total[0, 0, p] + total[0, 1, p])[:, :half]
        high = pltpu.roll(total[1, 0, p] + total[1, 1, p], half, 1)[:, :half]
        sums.append(low + high)
    table = jnp.concatenate(sums, axis=1)
    high = table.astype(BF16)
    low = (table - high.astype(F32)).astype(BF16)
    readers = jnp.concatenate([one[p][:, :half] for p in range(owners)], axis=1).astype(BF16)
    project = (nt(readers, high) + nt(readers, low)).astype(BF16)
    part = jnp.dot(project, high, preferred_element_type=F32)
    part += jnp.dot(project, low, preferred_element_type=F32)
    out[...] = part.astype(BF16)


def final_kernel(one, owner, a, b, c, d, factor, tile_factor, table):
    rank, rows_total = a.shape
    half = LANES // 2
    rows = (a[...].astype(F32) + b[...].astype(F32)) + (c[...].astype(F32) + d[...].astype(F32))
    table[...] = rows
    g0 = dot3(rows, rows, 1)
    eye = (row_iota(g0.shape) == lane_iota(g0.shape)).astype(F32)
    msq = jnp.sum(rows * rows, keepdims=True) / rows_total
    inv = 1.0 / jnp.sqrt(msq + 1e-06)
    g = g0 * (inv * inv) / rows_total
    square = dot3(g, g)
    outer = dot3(square, 0.0625 * square - 0.5625 * g)
    step = (outer + (1.6875 * square - 2.4375 * g + 2.25 * eye)) * inv

    def block(p):
        window = table[:, pl.ds(pl.multiple_of((p // 2) * LANES, LANES), LANES)]
        return jnp.where(p % 2 == 1, pltpu.roll(window, half, 1), window)[:, :half]

    places = [lax.axis_index("tiles")] + [owner[one[t]] for t in range(tile_factor.shape[0])]
    picked = jnp.concatenate([block(p) for p in places], axis=1)
    x = dot3(step, picked)
    factor[...] = x[:, :half]
    for t in range(tile_factor.shape[0]):
        value = x[:, (t + 1) * half : (t + 2) * half]
        for r in range(0, rank, 2):
            line = jnp.concatenate([value[r : r + 1], value[r + 1 : r + 2]], axis=1)
            tile_factor[t : t + 1, r * half : (r + 2) * half] = line.astype(BF16)


def swap(x, size, mask):
    return lax.ppermute(x, ("tiles", "rep"), [(i, i ^ mask) for i in range(size)])


def sliced(tiles, block_one, block_two, block_three, owner_map, u_one, u_two, u_three):
    count, width = tiles.shape[:2]
    rank = u_three.shape[0]
    owners = lax.axis_size("tiles")
    reps = lax.axis_size("rep")
    size = owners * reps
    rows_total = owner_map.shape[0] * width
    smem = pl.BlockSpec(memory_space=pltpu.SMEM)
    vmem = pl.BlockSpec(memory_space=pltpu.VMEM)
    narrow = pltpu.CompilerParams(vmem_limit_bytes=NARROW)
    ints = (block_one, block_two, block_three, owner_map)
    arrays = (tiles, u_three, u_two, u_one)
    sends = pl.pallas_call(
        first_kernel,
        out_shape=jax.ShapeDtypeStruct((rank, width + META, LANES), BF16),
        in_specs=[pl.BlockSpec(memory_space=pltpu.HBM)] * 8,
        out_specs=vmem,
        scratch_shapes=[pltpu.SMEM(x.shape, x.dtype) for x in ints]
        + [pltpu.VMEM(x.shape, x.dtype) for x in arrays]
        + [
            pltpu.VMEM(u_two.shape, F32),
            pltpu.SemaphoreType.DMA((7,)),
            pltpu.SemaphoreType.DMA((count,)),
        ],
        compiler_params=narrow,
        name="first",
    )(*[pltpu.with_memory_space_constraint(x, pltpu.HBM) for x in ints + arrays])
    got = lax.all_to_all(sends, ("tiles", "rep"), 0, 0, tiled=True)
    part = pl.pallas_call(
        functools.partial(rows_kernel, reps),
        out_shape=jax.ShapeDtypeStruct((rank, rows_total), BF16),
        in_specs=[vmem],
        out_specs=vmem,
        scratch_shapes=[
            pltpu.VMEM((owners, rank, LANES), F32),
            pltpu.VMEM((owners, rank, LANES), F32),
            pltpu.VMEM((count, 2, owners, rank, LANES), F32),
        ],
        compiler_params=narrow,
        name="rows_part",
    )(got)
    part = (part.astype(F32) + swap(part, size, 1).astype(F32)).astype(BF16)
    m, n = 2, 4
    pair = part.astype(F32) + swap(part, size, m | 1).astype(F32)
    other = swap(part, size, n | 1).astype(F32) + swap(part, size, m ^ n).astype(F32)
    part = (pair + other).astype(BF16)
    m, n = 16, 8
    parts = [part, swap(part, size, m | 1), swap(part, size, n | 1), swap(part, size, m ^ n)]
    return pl.pallas_call(
        final_kernel,
        out_shape=(
            jax.ShapeDtypeStruct(u_one.shape, F32),
            jax.ShapeDtypeStruct((count, rank * width), BF16),
        ),
        in_specs=[smem] * 2 + [vmem] * 4,
        out_specs=(vmem, vmem),
        scratch_shapes=[pltpu.VMEM((rank, rows_total), F32)],
        compiler_params=narrow,
        name="final",
    )(block_one, owner_map, *parts)


def per_device(*args):
    tiles, _, _, _, owner_map, u_one, u_two, u_three = args
    count, width = tiles.shape[:2]
    rank = u_three.shape[0]
    owners = lax.axis_size("tiles")
    reps = lax.axis_size("rep")
    fits = (
        owners * reps == rank == 32
        and reps * META // 2 == rank
        and width * 2 == LANES
        and count == 2
        and owner_map.shape[0] == owners
        and u_one.shape[1] == width
        and u_two.shape[1] == LANES
    )
    return (sliced if fits else general)(*args)


def solution(mesh):
    in_specs = (
        P(("tiles", "rep"), None, None),
        P(("tiles", "rep")),
        P(("tiles", "rep")),
        P(("tiles", "rep")),
        P(),
        P(None, "tiles"),
        P(None, "tiles"),
        P(),
    )
    out_specs = (P(None, "tiles"), P(("tiles", "rep"), None))
    return jax.shard_map(
        per_device, mesh=mesh, in_specs=in_specs, out_specs=out_specs, check_vma=False
    )
```

```python
import functools

import jax
import jax.numpy as jnp
from jax import lax
from jax.experimental import pallas as pl
from jax.experimental.pallas import tpu as pltpu
from jax.sharding import PartitionSpec as P

NS_STEPS = 2
HI = lax.Precision.HIGHEST
LANES = 128
NARROW = 16 * 1024 * 1024
META = 16
F32 = jnp.float32
BF16 = jnp.bfloat16


def pick(table, index, width):
    grid = table.reshape(table.shape[0], -1, width)
    return jnp.transpose(jnp.take(grid, index, axis=1), (1, 0, 2))


def orthonormal(rows, rows_total):
    rank = rows.shape[0]
    g0 = jnp.dot(rows, rows.T, precision=HI, preferred_element_type=F32)
    msq = jnp.trace(g0) / rows_total
    inv = 1.0 / jnp.sqrt(msq + 1e-06)
    x = rows * inv
    g = g0 * (inv * inv) / rows_total
    eye = jnp.eye(rank, dtype=F32)
    for step in range(NS_STEPS):
        if step > 0:
            g = jnp.dot(x, x.T, precision=HI, preferred_element_type=F32) / rows_total
        x = jnp.dot(1.5 * eye - 0.5 * g, x, precision=HI, preferred_element_type=F32)
    return x


def general(tiles, block_one, block_two, block_three, owner_map, u_one, u_two, u_three):
    count, width = tiles.shape[:2]
    rank = u_three.shape[0]
    blocks_total = owner_map.shape[0]
    rows_total = blocks_total * width
    two_full = lax.all_gather(u_two, "tiles", axis=1, tiled=True)
    two_pick = pick(two_full, block_two, width)
    three_pick = pick(u_three, block_three, width)
    cube = tiles.reshape(count, width, width, width)
    first = jnp.einsum("tijk,tsk->tijs", cube, three_pick, preferred_element_type=F32).astype(BF16)
    second = jnp.einsum("tijs,trj->tirs", first, two_pick, preferred_element_type=F32)
    products = second.reshape(count, width, rank * rank).astype(BF16)
    positions = jnp.take(owner_map, block_one)
    onehot = (positions[:, None] == jnp.arange(blocks_total, dtype=jnp.int32)[None, :]).astype(F32)
    current = lax.all_gather(u_one.astype(BF16), "tiles", axis=1, tiled=True)
    readers = pick(current, positions, width)
    partial_value = jnp.einsum("tic,tri->rc", products, readers, preferred_element_type=F32)
    project = lax.psum(partial_value, ("tiles", "rep")).astype(BF16)
    z_tile = jnp.einsum("rc,tic->tri", project, products, preferred_element_type=F32)
    term = jnp.einsum("tri,tn->rni", z_tile, onehot, precision=HI).reshape(rank, rows_total)
    rows = lax.psum(term, ("tiles", "rep"))
    current = orthonormal(rows, rows_total)
    tile_factor = pick(current.astype(BF16), positions, width).reshape(count, rank * width)
    own = u_one.shape[1]
    factor = lax.dynamic_slice_in_dim(current, lax.axis_index("tiles") * own, own, 1)
    return (factor, tile_factor)


def split(a):
    high = a.astype(BF16)
    return high, (a - high.astype(F32)).astype(BF16)


def dot3(a, b, axis=0):
    (ah, al), (bh, bl) = split(a), split(b)
    left = jnp.concatenate([ah, al, ah], axis=1)
    right = jnp.concatenate([bh, bh, bl], axis=axis)
    return lax.dot_general(left, right, (((1,), (axis,)), ((), ())), preferred_element_type=F32)


def lane_iota(shape):
    return lax.broadcasted_iota(jnp.int32, shape, len(shape) - 1)


def row_iota(shape):
    return lax.broadcasted_iota(jnp.int32, shape, len(shape) - 2)


def nt(a, b, precision=None):
    return lax.dot_general(
        a, b, (((1,), (1,)), ((), ())), precision=precision, preferred_element_type=F32
    )


def first_kernel(
    one_hbm, two_hbm, three_hbm, owner_hbm, tiles_hbm, u_three_hbm, u_two_hbm, u_one_hbm, out, places,
    one, two, three, owner, tiles, u_three, u_two, u_one, two_f32, in_sems, tile_sems,
):
    count, width = tiles.shape[:2]
    rank = u_three.shape[0]
    half = LANES // 2
    share = META // 2
    span = share * width
    pieces = tiles.shape[2] // (2 * span)
    moves = [(three_hbm, three), (u_three_hbm, u_three), (two_hbm, two), (one_hbm, one)]
    moves += [(owner_hbm, owner), (u_two_hbm, u_two), (u_one_hbm, u_one)]
    copies = [pltpu.make_async_copy(a, b, in_sems.at[i]) for i, (a, b) in enumerate(moves)]
    loads = [
        pltpu.make_async_copy(tiles_hbm.at[t], tiles.at[t], tile_sems.at[t]) for t in range(count)
    ]
    for copy in copies + loads:
        copy.start()
    copies[0].wait()
    copies[1].wait()
    weights = []
    for t in range(count):
        block = three[t]
        start = pl.multiple_of((block // 2) * LANES, LANES)
        window = u_three[:, pl.ds(start, LANES)].astype(F32)
        same = (lane_iota(window.shape) // half) == (block % 2)
        both = jnp.where(same, window, pltpu.roll(window, half, 1))
        tall = jnp.broadcast_to(both[:, None, :], (rank, share, LANES)).reshape(rank * share, LANES)
        full = jnp.concatenate([tall] * (span // LANES), axis=1)
        keep = (row_iota(full.shape) % share) == (lane_iota(full.shape) // width)
        weights.append(jnp.where(keep, full, 0.0).astype(BF16))
    for copy in copies[2:]:
        copy.wait()
    q = lax.axis_index("rep")
    two_f32[...] = u_two[...].astype(F32)
    top = two_f32[pl.ds(pl.multiple_of(q * share, share), share), :]
    low = u_one[pl.ds(pl.multiple_of(q * share, share), share), :]
    lane = lane_iota((share, half))
    ints = jnp.zeros((share, half), F32)
    spot = lane_iota(places.shape)
    place = jnp.zeros(places.shape, jnp.int32)
    for t in range(count):
        position = owner[one[t]]
        ints = jnp.where(lane == t, two[t].astype(F32), ints)
        ints = jnp.where(lane == count + t, position.astype(F32), ints)
        place = jnp.where(spot == t, position, place)
    places[...] = place
    meta = jnp.concatenate([top, jnp.concatenate([low, ints], axis=1)], axis=0).astype(BF16)
    rows = slice(width, width + META)
    for s in range(rank):
        out[s, rows, :] = meta
    for copy in loads:
        copy.wait()
    for n in range(pieces // 2):
        wide = []
        for t in range(count):
            groups = [tiles[t, :, (4 * n + g) * span : (4 * n + g + 1) * span] for g in range(4)]
            wide.append(nt(weights[t], jnp.concatenate(groups, axis=0)))
        for s in range(rank):
            at = slice(s * share, (s + 1) * share)
            for h in range(2):
                block = []
                for g in (2 * h, 2 * h + 1):
                    lanes = slice(g * width, (g + 1) * width)
                    block.append(jnp.concatenate([part[at, lanes] for part in wide], axis=1))
                rows = slice((2 * n + h) * META, (2 * n + h + 1) * META)
                out[s, rows, :] = jnp.concatenate(block, axis=0).astype(BF16)


def rows_kernel(reps, got, out, two, one, total):
    sources, depth = got.shape[:2]
    width = depth - META
    half = LANES // 2
    share = META // 2
    rank = share * reps
    count = LANES // width
    owners = sources // reps
    blocks = 2 * owners
    lines = []
    halves = lane_iota((META, LANES)) // half
    for src in range(0, sources, 2):
        t, q = divmod(src, reps)
        pair = [got[src + k, width:depth, :].astype(F32) for k in range(2)]
        rows = slice(q * share, (q + 2) * share)
        both = jnp.concatenate([meta[:share] for meta in pair], axis=0)
        for k in range(2):
            two[2 * t + k, rows, :] = jnp.where(halves == k, both, 0.0).astype(BF16)
        one[t, rows, :] = jnp.concatenate([meta[share:] for meta in pair], axis=0)
        lines += [meta[share : share + 1] for meta in pair]
    lines = jnp.concatenate(lines, axis=0)
    lane = lane_iota(lines.shape)
    scale = jnp.zeros(lines.shape, F32)
    for k in range(2 * count):
        scale = jnp.where(lane == half + k, float(blocks**k), scale)
    code = jnp.sum(lines * scale, axis=1, keepdims=True).astype(jnp.int32)
    total[...] = jnp.zeros_like(total)
    for src in range(sources):
        block = got[src, 0:width, :]
        moving = jnp.concatenate([block, block], axis=0)
        left = code[src, 0]
        digits = []
        for _ in range(2 * count):
            digits.append(left % blocks)
            left = left // blocks
        stacked = jnp.concatenate([two[b] for b in digits[:count]], axis=0)
        product = jnp.dot(stacked, moving, preferred_element_type=F32).astype(BF16).astype(F32)
        for t, p in enumerate(digits[count:]):
            total[t, src % 2, p] += product[t * rank : (t + 1) * rank]
    sums = []
    for p in range(owners):
        low = (total[0, 0, p] + total[0, 1, p])[:, :half]
        high = pltpu.roll(total[1, 0, p] + total[1, 1, p], half, 1)[:, :half]
        sums.append(low + high)
    table = jnp.concatenate(sums, axis=1)
    high = table.astype(BF16)
    low = (table - high.astype(F32)).astype(BF16)
    readers = jnp.concatenate([one[p][:, :half] for p in range(owners)], axis=1).astype(BF16)
    project = (nt(readers, high) + nt(readers, low)).astype(BF16)
    part = jnp.dot(project, high, preferred_element_type=F32)
    part += jnp.dot(project, low, preferred_element_type=F32)
    out[...] = part.astype(BF16)


def final_kernel(places, a, b, c, d, factor, tile_factor, table):
    rank, rows_total = a.shape
    half = LANES // 2
    rows = (a[...].astype(F32) + b[...].astype(F32)) + (c[...].astype(F32) + d[...].astype(F32))
    table[...] = rows
    g0 = dot3(rows, rows, 1)
    eye = (row_iota(g0.shape) == lane_iota(g0.shape)).astype(F32)
    msq = jnp.sum(rows * rows, keepdims=True) / rows_total
    inv = 1.0 / jnp.sqrt(msq + 1e-06)
    g = g0 * (inv * inv) / rows_total
    square = dot3(g, g)
    outer = dot3(square, 0.0625 * square - 0.5625 * g)
    step = (outer + (1.6875 * square - 2.4375 * g + 2.25 * eye)) * inv

    def block(p):
        window = table[:, pl.ds(pl.multiple_of((p // 2) * LANES, LANES), LANES)]
        return jnp.where(p % 2 == 1, pltpu.roll(window, half, 1), window)[:, :half]

    place = places[...]
    picks = [lax.axis_index("tiles")] + [place[0, t] for t in range(tile_factor.shape[0])]
    picked = jnp.concatenate([block(p) for p in picks], axis=1)
    x = dot3(step, picked)
    factor[...] = x[:, :half]
    for t in range(tile_factor.shape[0]):
        value = x[:, (t + 1) * half : (t + 2) * half]
        for r in range(0, rank, 2):
            line = jnp.concatenate([value[r : r + 1], value[r + 1 : r + 2]], axis=1)
            tile_factor[t : t + 1, r * half : (r + 2) * half] = line.astype(BF16)


def swap(x, size, mask):
    return lax.ppermute(x, ("tiles", "rep"), [(i, i ^ mask) for i in range(size)])


def sliced(tiles, block_one, block_two, block_three, owner_map, u_one, u_two, u_three):
    count, width = tiles.shape[:2]
    rank = u_three.shape[0]
    owners = lax.axis_size("tiles")
    reps = lax.axis_size("rep")
    size = owners * reps
    rows_total = owner_map.shape[0] * width
    vmem = pl.BlockSpec(memory_space=pltpu.VMEM)
    narrow = pltpu.CompilerParams(vmem_limit_bytes=NARROW)
    ints = (block_one, block_two, block_three, owner_map)
    arrays = (tiles, u_three, u_two, u_one)
    sends, places = pl.pallas_call(
        first_kernel,
        out_shape=(
            jax.ShapeDtypeStruct((rank, width + META, LANES), BF16),
            jax.ShapeDtypeStruct((META // 2, LANES), jnp.int32),
        ),
        in_specs=[pl.BlockSpec(memory_space=pltpu.HBM)] * 8,
        out_specs=(vmem, vmem),
        scratch_shapes=[pltpu.SMEM(x.shape, x.dtype) for x in ints]
        + [pltpu.VMEM(x.shape, x.dtype) for x in arrays]
        + [
            pltpu.VMEM(u_two.shape, F32),
            pltpu.SemaphoreType.DMA((7,)),
            pltpu.SemaphoreType.DMA((count,)),
        ],
        compiler_params=narrow,
        name="first",
    )(*[pltpu.with_memory_space_constraint(x, pltpu.HBM) for x in ints + arrays])
    got = lax.all_to_all(sends, ("tiles", "rep"), 0, 0, tiled=True)
    part = pl.pallas_call(
        functools.partial(rows_kernel, reps),
        out_shape=jax.ShapeDtypeStruct((rank, rows_total), BF16),
        in_specs=[vmem],
        out_specs=vmem,
        scratch_shapes=[
            pltpu.VMEM((2 * owners, rank, LANES), BF16),
            pltpu.VMEM((owners, rank, LANES), F32),
            pltpu.VMEM((count, 2, owners, rank, LANES), F32),
        ],
        compiler_params=narrow,
        name="rows_part",
    )(got)
    part = (part.astype(F32) + swap(part, size, 1).astype(F32)).astype(BF16)
    m, n = 2, 4
    pair = part.astype(F32) + swap(part, size, m | 1).astype(F32)
    other = swap(part, size, n | 1).astype(F32) + swap(part, size, m ^ n).astype(F32)
    part = (pair + other).astype(BF16)
    m, n = 16, 8
    parts = [part, swap(part, size, m | 1), swap(part, size, n | 1), swap(part, size, m ^ n)]
    return pl.pallas_call(
        final_kernel,
        out_shape=(
            jax.ShapeDtypeStruct(u_one.shape, F32),
            jax.ShapeDtypeStruct((count, rank * width), BF16),
        ),
        in_specs=[vmem] * 5,
        out_specs=(vmem, vmem),
        scratch_shapes=[pltpu.VMEM((rank, rows_total), F32)],
        compiler_params=narrow,
        name="final",
    )(places, *parts)


def per_device(*args):
    tiles, _, _, _, owner_map, u_one, u_two, u_three = args
    count, width = tiles.shape[:2]
    rank = u_three.shape[0]
    owners = lax.axis_size("tiles")
    reps = lax.axis_size("rep")
    fits = (
        owners * reps == rank == 32
        and reps * META // 2 == rank
        and reps % 2 == 0
        and width * 2 == LANES
        and count == 2
        and owner_map.shape[0] == owners
        and u_one.shape[1] == width
        and u_two.shape[1] == LANES
    )
    return (sliced if fits else general)(*args)


def solution(mesh):
    in_specs = (
        P(("tiles", "rep"), None, None),
        P(("tiles", "rep")),
        P(("tiles", "rep")),
        P(("tiles", "rep")),
        P(),
        P(None, "tiles"),
        P(None, "tiles"),
        P(),
    )
    out_specs = (P(None, "tiles"), P(("tiles", "rep"), None))
    return jax.shard_map(
        per_device, mesh=mesh, in_specs=in_specs, out_specs=out_specs, check_vma=False
    )
```

```python
import functools

import jax
import jax.numpy as jnp
from jax import lax
from jax.experimental import pallas as pl
from jax.experimental.pallas import tpu as pltpu
from jax.sharding import PartitionSpec as P

NS_STEPS = 2
HI = lax.Precision.HIGHEST
LANES = 128
NARROW = 16 * 1024 * 1024
META = 16
F32 = jnp.float32
BF16 = jnp.bfloat16


def pick(table, index, width):
    grid = table.reshape(table.shape[0], -1, width)
    return jnp.transpose(jnp.take(grid, index, axis=1), (1, 0, 2))


def orthonormal(rows, rows_total):
    rank = rows.shape[0]
    g0 = jnp.dot(rows, rows.T, precision=HI, preferred_element_type=F32)
    msq = jnp.trace(g0) / rows_total
    inv = 1.0 / jnp.sqrt(msq + 1e-06)
    x = rows * inv
    g = g0 * (inv * inv) / rows_total
    eye = jnp.eye(rank, dtype=F32)
    for step in range(NS_STEPS):
        if step > 0:
            g = jnp.dot(x, x.T, precision=HI, preferred_element_type=F32) / rows_total
        x = jnp.dot(1.5 * eye - 0.5 * g, x, precision=HI, preferred_element_type=F32)
    return x


def general(tiles, block_one, block_two, block_three, owner_map, u_one, u_two, u_three):
    count, width = tiles.shape[:2]
    rank = u_three.shape[0]
    blocks_total = owner_map.shape[0]
    rows_total = blocks_total * width
    two_full = lax.all_gather(u_two, "tiles", axis=1, tiled=True)
    two_pick = pick(two_full, block_two, width)
    three_pick = pick(u_three, block_three, width)
    cube = tiles.reshape(count, width, width, width)
    first = jnp.einsum("tijk,tsk->tijs", cube, three_pick, preferred_element_type=F32).astype(BF16)
    second = jnp.einsum("tijs,trj->tirs", first, two_pick, preferred_element_type=F32)
    products = second.reshape(count, width, rank * rank).astype(BF16)
    positions = jnp.take(owner_map, block_one)
    onehot = (positions[:, None] == jnp.arange(blocks_total, dtype=jnp.int32)[None, :]).astype(F32)
    current = lax.all_gather(u_one.astype(BF16), "tiles", axis=1, tiled=True)
    readers = pick(current, positions, width)
    partial_value = jnp.einsum("tic,tri->rc", products, readers, preferred_element_type=F32)
    project = lax.psum(partial_value, ("tiles", "rep")).astype(BF16)
    z_tile = jnp.einsum("rc,tic->tri", project, products, preferred_element_type=F32)
    term = jnp.einsum("tri,tn->rni", z_tile, onehot, precision=HI).reshape(rank, rows_total)
    rows = lax.psum(term, ("tiles", "rep"))
    current = orthonormal(rows, rows_total)
    tile_factor = pick(current.astype(BF16), positions, width).reshape(count, rank * width)
    own = u_one.shape[1]
    factor = lax.dynamic_slice_in_dim(current, lax.axis_index("tiles") * own, own, 1)
    return (factor, tile_factor)


def split(a):
    high = a.astype(BF16)
    return high, (a - high.astype(F32)).astype(BF16)


def dot3(a, b, axis=0):
    (ah, al), (bh, bl) = split(a), split(b)
    left = jnp.concatenate([ah, al, ah], axis=1)
    right = jnp.concatenate([bh, bh, bl], axis=axis)
    return lax.dot_general(left, right, (((1,), (axis,)), ((), ())), preferred_element_type=F32)


def lane_iota(shape):
    return lax.broadcasted_iota(jnp.int32, shape, len(shape) - 1)


def row_iota(shape):
    return lax.broadcasted_iota(jnp.int32, shape, len(shape) - 2)


def nt(a, b, precision=None):
    return lax.dot_general(
        a, b, (((1,), (1,)), ((), ())), precision=precision, preferred_element_type=F32
    )


def first_kernel(
    one_hbm, two_hbm, three_hbm, owner_hbm, tiles_hbm, u_three_hbm, u_two_hbm, u_one_hbm, out, places,
    one, two, three, owner, tiles, u_three, u_two, u_one, two_f32, in_sems, tile_sems,
):
    side = lax.axis_index("half")
    count, width = tiles.shape[:2]
    rank = u_three.shape[0]
    half = LANES // 2
    share = META // 2
    span = share * width
    pieces = tiles.shape[2] // (2 * span)
    moves = [(three_hbm, three), (u_three_hbm, u_three), (two_hbm, two), (one_hbm, one)]
    moves += [(owner_hbm, owner), (u_two_hbm, u_two), (u_one_hbm, u_one)]
    copies = [pltpu.make_async_copy(a, b, in_sems.at[i]) for i, (a, b) in enumerate(moves)]
    loads = [
        pltpu.make_async_copy(tiles_hbm.at[t], tiles.at[t], tile_sems.at[t]) for t in range(count)
    ]
    for copy in copies + loads:
        copy.start()
    copies[0].wait()
    copies[1].wait()
    weights = []
    for t in range(count):
        block = three[t]
        start = pl.multiple_of((block // 2) * LANES, LANES)
        window = u_three[:, pl.ds(start, LANES)].astype(F32)
        same = (lane_iota(window.shape) // half) == (block % 2)
        both = jnp.where(same, window, pltpu.roll(window, half, 1))
        tall = jnp.broadcast_to(both[:, None, :], (rank, share, LANES)).reshape(rank * share, LANES)
        full = jnp.concatenate([tall] * (span // LANES), axis=1)
        keep = (row_iota(full.shape) % share) == (lane_iota(full.shape) // width)
        weights.append(jnp.where(keep, full, 0.0).astype(BF16))
    for copy in copies[2:]:
        copy.wait()
    q = lax.axis_index("rep")
    two_f32[...] = u_two[...].astype(F32)
    top = two_f32[pl.ds(pl.multiple_of(q * share, share), share), :]
    low = u_one[pl.ds(pl.multiple_of(q * share, share), share), :]
    lane = lane_iota((share, half))
    ints = jnp.zeros((share, half), F32)
    spot = lane_iota(places.shape)
    place = jnp.zeros(places.shape, jnp.int32)
    for t in range(count):
        position = owner[one[t]]
        ints = jnp.where(lane == t, two[t].astype(F32), ints)
        ints = jnp.where(lane == count + t, position.astype(F32), ints)
        place = jnp.where(spot == t, position, place)
    places[...] = place
    meta = jnp.concatenate([top, jnp.concatenate([low, ints], axis=1)], axis=0).astype(BF16)
    rows = slice(2 * width, 2 * width + META)
    for k in range(out.shape[0]):
        out[k, rows, :] = meta
    for copy in loads:
        copy.wait()
    for n in range(pieces // 2):
        wide = []
        for t in range(count):
            groups = [tiles[t, :, (4 * n + g) * span : (4 * n + g + 1) * span] for g in range(4)]
            wide.append(nt(weights[t], jnp.concatenate(groups, axis=0)))
        for s in range(rank):
            at = slice(s * share, (s + 1) * share)
            for h in range(2):
                block = []
                for g in (2 * h, 2 * h + 1):
                    lanes = slice(g * width, (g + 1) * width)
                    block.append(jnp.concatenate([part[at, lanes] for part in wide], axis=1))
                start = (s % 2) * width + (2 * n + h) * META
                rows = slice(start, start + META)
                out[(s // 2) ^ side, rows, :] = jnp.concatenate(block, axis=0).astype(BF16)


def share_kernel(sends, u_two, out, two_f32):
    share = META // 2
    two_f32[...] = u_two[...].astype(F32)
    start = pl.multiple_of(lax.axis_index("rep") * share, share)
    line = two_f32[pl.ds(start, share), :].astype(BF16)
    depth = out.shape[1]
    for k in range(out.shape[0]):
        out[k, depth - share : depth, :] = line


def table_kernel(reps, got, out, two, one, total):
    sources, depth = got.shape[:2]
    half = LANES // 2
    share = META // 2
    width = (depth - META - share) // 2
    rank = share * reps
    count = LANES // width
    owners = 2 * sources // reps
    blocks = 2 * owners
    side = lax.axis_index("half")
    lines = []
    halves = lane_iota((META, LANES)) // half
    for src in range(0, sources, 2):
        t, q = divmod(src, reps)
        rows = slice(q * share, (q + 2) * share)
        pair = [got[src + k, 2 * width : 2 * width + META, :].astype(F32) for k in range(2)]
        last = [got[src + k, depth - share : depth, :].astype(F32) for k in range(2)]
        mine = jnp.concatenate([meta[:share] for meta in pair], axis=0)
        theirs = jnp.concatenate(last, axis=0)
        for at, both in ((side, mine), (1 - side, theirs)):
            shard = at * (owners // 2) + t
            for k in range(2):
                two[2 * shard + k, rows, :] = jnp.where(halves == k, both, 0.0).astype(BF16)
        one[t, rows, :] = jnp.concatenate([meta[share:] for meta in pair], axis=0)
        lines += [meta[share : share + 1] for meta in pair]
    lines = jnp.concatenate(lines, axis=0)
    lane = lane_iota(lines.shape)
    scale = jnp.zeros(lines.shape, F32)
    for k in range(2 * count):
        scale = jnp.where(lane == half + k, float(blocks**k), scale)
    code = jnp.sum(lines * scale, axis=1, keepdims=True).astype(jnp.int32)
    total[...] = jnp.zeros_like(total)
    for src in range(sources):
        moving = []
        for s in range(2):
            block = got[src, s * width : (s + 1) * width, :]
            moving.append(jnp.concatenate([block, block], axis=0))
        moving = jnp.concatenate(moving, axis=1)
        left = code[src, 0]
        digits = []
        for _ in range(2 * count):
            digits.append(left % blocks)
            left = left // blocks
        stacked = jnp.concatenate([two[b] for b in digits[:count]], axis=0)
        product = jnp.dot(stacked, moving, preferred_element_type=F32).astype(BF16).astype(F32)
        for t, p in enumerate(digits[count:]):
            total[t, src % 2, p] += product[t * rank : (t + 1) * rank]
    for s in range(2):
        sums = []
        lanes = slice(s * LANES, (s + 1) * LANES)
        for p in range(owners):
            low = (total[0, 0, p, :, lanes] + total[0, 1, p, :, lanes])[:, :half]
            high = total[1, 0, p, :, lanes] + total[1, 1, p, :, lanes]
            sums.append(low + pltpu.roll(high, half, 1)[:, :half])
        out[s * rank : (s + 1) * rank, :] = jnp.concatenate(sums, axis=1).astype(BF16)
    known = jnp.concatenate([one[p][:, :half] for p in range(owners // 2)], axis=1)
    known = jnp.concatenate([known[: rank // 2], known[rank // 2 :]], axis=1)
    out[2 * rank :, :] = known.astype(BF16)


def rows_kernel(mine, theirs, out):
    rank, rows_total = out.shape
    table = mine[: 2 * rank, :].astype(F32) + theirs[: 2 * rank, :].astype(F32)
    known = []
    for ref in (mine, theirs):
        lines = ref[2 * rank :, :].astype(F32)
        known.append(
            jnp.concatenate([lines[:, : rows_total // 2], lines[:, rows_total // 2 :]], axis=0)
        )
    first = lax.axis_index("half") == 0
    readers = jnp.concatenate(
        [jnp.where(first, known[0], known[1]), jnp.where(first, known[1], known[0])], axis=1
    ).astype(BF16)
    high, low = split(table)
    project = (nt(readers, high) + nt(readers, low)).astype(BF16)
    part = jnp.dot(project, high, preferred_element_type=F32)
    part += jnp.dot(project, low, preferred_element_type=F32)
    out[...] = part.astype(BF16)


def final_kernel(places, a, b, factor, tile_factor, table):
    rank, rows_total = a.shape
    half = LANES // 2
    rows = a[...].astype(F32) + b[...].astype(F32)
    table[...] = rows
    g0 = dot3(rows, rows, 1)
    eye = (row_iota(g0.shape) == lane_iota(g0.shape)).astype(F32)
    msq = jnp.sum(rows * rows, keepdims=True) / rows_total
    inv = 1.0 / jnp.sqrt(msq + 1e-06)
    g = g0 * (inv * inv) / rows_total
    square = dot3(g, g)
    outer = dot3(square, 0.0625 * square - 0.5625 * g)
    step = (outer + (1.6875 * square - 2.4375 * g + 2.25 * eye)) * inv

    def block(p):
        window = table[:, pl.ds(pl.multiple_of((p // 2) * LANES, LANES), LANES)]
        return jnp.where(p % 2 == 1, pltpu.roll(window, half, 1), window)[:, :half]

    place = places[...]
    picks = [lax.axis_index(("half", "rest"))] + [place[0, t] for t in range(tile_factor.shape[0])]
    picked = jnp.concatenate([block(p) for p in picks], axis=1)
    x = dot3(step, picked)
    factor[...] = x[:, :half]
    for t in range(tile_factor.shape[0]):
        value = x[:, (t + 1) * half : (t + 2) * half]
        for r in range(0, rank, 2):
            line = jnp.concatenate([value[r : r + 1], value[r + 1 : r + 2]], axis=1)
            tile_factor[t : t + 1, r * half : (r + 2) * half] = line.astype(BF16)


def swap(x, size, mask):
    return lax.ppermute(x, ("half", "rest", "rep"), [(i, i ^ mask) for i in range(size)])


def sliced(tiles, block_one, block_two, block_three, owner_map, u_one, u_two, u_three):
    count, width = tiles.shape[:2]
    rank = u_three.shape[0]
    owners = 2 * lax.axis_size("rest")
    reps = lax.axis_size("rep")
    size = owners * reps
    sources = size // 2
    rows_total = owner_map.shape[0] * width
    depth = 2 * width + META + META // 2
    vmem = pl.BlockSpec(memory_space=pltpu.VMEM)
    narrow = pltpu.CompilerParams(vmem_limit_bytes=NARROW)
    core, x, y, near, far = 1, 2, 4, 8, 16
    their_two = swap(u_two, size, far | core)
    ints = (block_one, block_two, block_three, owner_map)
    arrays = (tiles, u_three, u_two, u_one)
    sends, places = pl.pallas_call(
        first_kernel,
        out_shape=(
            jax.ShapeDtypeStruct((sources, depth, LANES), BF16),
            jax.ShapeDtypeStruct((META // 2, LANES), jnp.int32),
        ),
        in_specs=[pl.BlockSpec(memory_space=pltpu.HBM)] * 8,
        out_specs=(vmem, vmem),
        scratch_shapes=[pltpu.SMEM(a.shape, a.dtype) for a in ints]
        + [pltpu.VMEM(a.shape, a.dtype) for a in arrays]
        + [
            pltpu.VMEM(u_two.shape, F32),
            pltpu.SemaphoreType.DMA((7,)),
            pltpu.SemaphoreType.DMA((count,)),
        ],
        compiler_params=narrow,
        name="first",
    )(*[pltpu.with_memory_space_constraint(a, pltpu.HBM) for a in ints + arrays])
    sends = pl.pallas_call(
        share_kernel,
        out_shape=jax.ShapeDtypeStruct(sends.shape, sends.dtype),
        in_specs=[vmem] * 2,
        out_specs=vmem,
        scratch_shapes=[pltpu.VMEM(u_two.shape, F32)],
        input_output_aliases={0: 0},
        compiler_params=narrow,
        name="share",
    )(sends, their_two)
    got = lax.all_to_all(sends, ("rest", "rep"), 0, 0, tiled=True)
    table = pl.pallas_call(
        functools.partial(table_kernel, reps),
        out_shape=jax.ShapeDtypeStruct((2 * rank + rank // 2, rows_total), BF16),
        in_specs=[vmem],
        out_specs=vmem,
        scratch_shapes=[
            pltpu.VMEM((2 * owners, rank, LANES), BF16),
            pltpu.VMEM((owners // 2, rank, LANES), F32),
            pltpu.VMEM((count, 2, owners, rank, 2 * LANES), F32),
        ],
        compiler_params=narrow,
        name="table",
    )(got)
    part = pl.pallas_call(
        rows_kernel,
        out_shape=jax.ShapeDtypeStruct((rank, rows_total), BF16),
        in_specs=[vmem] * 2,
        out_specs=vmem,
        compiler_params=narrow,
        name="rows_part",
    )(table, swap(table, size, far | core))
    part = (part.astype(F32) + swap(part, size, core).astype(F32)).astype(BF16)
    pair = part.astype(F32) + swap(part, size, x | core).astype(F32)
    other = swap(part, size, y | core).astype(F32) + swap(part, size, x ^ y).astype(F32)
    part = (pair + other).astype(BF16)
    return pl.pallas_call(
        final_kernel,
        out_shape=(
            jax.ShapeDtypeStruct(u_one.shape, F32),
            jax.ShapeDtypeStruct((count, rank * width), BF16),
        ),
        in_specs=[vmem] * 3,
        out_specs=(vmem, vmem),
        scratch_shapes=[pltpu.VMEM((rank, rows_total), F32)],
        compiler_params=narrow,
        name="final",
    )(places, part, swap(part, size, near | core))


def fits(mesh, tiles, block_one, block_two, block_three, owner_map, u_one, u_two, u_three):
    owners, reps = mesh.shape["tiles"], mesh.shape["rep"]
    rank = u_three.shape[0]
    width = tiles.shape[1]
    return (
        owners == 8
        and reps == 4
        and rank == owners * reps == reps * META // 2
        and tiles.shape[0] == 2 * owners * reps
        and 2 * width == LANES
        and owner_map.shape[0] == owners
        and u_one.shape[1] == owners * width
        and u_two.shape[1] == owners * LANES
        and u_three.shape[1] % LANES == 0
    )


def specs(tiles, rep):
    both = tiles + rep
    ins = (P(both, None, None), P(both), P(both), P(both), P(), P(None, tiles), P(None, tiles), P())
    return ins, (P(None, tiles), P(both, None))


def solution(mesh):
    def run(*args):
        if fits(mesh, *args):
            axes = ("half", "rest", "rep")
            grid = mesh.devices.reshape(2, -1, mesh.shape["rep"])
            halves = jax.sharding.Mesh(grid, axes)
            ins, outs = specs(axes[:2], axes[2:])
            body, where = sliced, halves
        else:
            ins, outs = specs(("tiles",), ("rep",))
            body, where = general, mesh
        return jax.shard_map(body, mesh=where, in_specs=ins, out_specs=outs, check_vma=False)(*args)

    return run
```

```python
import functools

import jax
import jax.numpy as jnp
from jax import lax
from jax.experimental import pallas as pl
from jax.experimental.pallas import tpu as pltpu
from jax.sharding import PartitionSpec as P

NS_STEPS = 2
HI = lax.Precision.HIGHEST
LANES = 128
NARROW = 16 * 1024 * 1024
META = 16
F32 = jnp.float32
BF16 = jnp.bfloat16


def pick(table, index, width):
    grid = table.reshape(table.shape[0], -1, width)
    return jnp.transpose(jnp.take(grid, index, axis=1), (1, 0, 2))


def orthonormal(rows, rows_total):
    rank = rows.shape[0]
    g0 = jnp.dot(rows, rows.T, precision=HI, preferred_element_type=F32)
    msq = jnp.trace(g0) / rows_total
    inv = 1.0 / jnp.sqrt(msq + 1e-06)
    x = rows * inv
    g = g0 * (inv * inv) / rows_total
    eye = jnp.eye(rank, dtype=F32)
    for step in range(NS_STEPS):
        if step > 0:
            g = jnp.dot(x, x.T, precision=HI, preferred_element_type=F32) / rows_total
        x = jnp.dot(1.5 * eye - 0.5 * g, x, precision=HI, preferred_element_type=F32)
    return x


def general(tiles, block_one, block_two, block_three, owner_map, u_one, u_two, u_three):
    count, width = tiles.shape[:2]
    rank = u_three.shape[0]
    blocks_total = owner_map.shape[0]
    rows_total = blocks_total * width
    two_full = lax.all_gather(u_two, "tiles", axis=1, tiled=True)
    two_pick = pick(two_full, block_two, width)
    three_pick = pick(u_three, block_three, width)
    cube = tiles.reshape(count, width, width, width)
    first = jnp.einsum("tijk,tsk->tijs", cube, three_pick, preferred_element_type=F32).astype(BF16)
    second = jnp.einsum("tijs,trj->tirs", first, two_pick, preferred_element_type=F32)
    products = second.reshape(count, width, rank * rank).astype(BF16)
    positions = jnp.take(owner_map, block_one)
    onehot = (positions[:, None] == jnp.arange(blocks_total, dtype=jnp.int32)[None, :]).astype(F32)
    current = lax.all_gather(u_one.astype(BF16), "tiles", axis=1, tiled=True)
    readers = pick(current, positions, width)
    partial_value = jnp.einsum("tic,tri->rc", products, readers, preferred_element_type=F32)
    project = lax.psum(partial_value, ("tiles", "rep")).astype(BF16)
    z_tile = jnp.einsum("rc,tic->tri", project, products, preferred_element_type=F32)
    term = jnp.einsum("tri,tn->rni", z_tile, onehot, precision=HI).reshape(rank, rows_total)
    rows = lax.psum(term, ("tiles", "rep"))
    current = orthonormal(rows, rows_total)
    tile_factor = pick(current.astype(BF16), positions, width).reshape(count, rank * width)
    own = u_one.shape[1]
    factor = lax.dynamic_slice_in_dim(current, lax.axis_index("tiles") * own, own, 1)
    return (factor, tile_factor)


def split(a):
    high = a.astype(BF16)
    return high, (a - high.astype(F32)).astype(BF16)


def dot3(a, b, axis=0):
    (ah, al), (bh, bl) = split(a), split(b)
    dims = (((1,), (axis,)), ((), ()))
    parts = [lax.dot_general(p, q, dims, preferred_element_type=F32) for p, q in ((ah, bh), (ah, bl), (al, bh))]
    return parts[0] + (parts[1] + parts[2])


def lane_iota(shape):
    return lax.broadcasted_iota(jnp.int32, shape, len(shape) - 1)


def row_iota(shape):
    return lax.broadcasted_iota(jnp.int32, shape, len(shape) - 2)


def nt(a, b, precision=None):
    return lax.dot_general(
        a, b, (((1,), (1,)), ((), ())), precision=precision, preferred_element_type=F32
    )


def first_kernel(
    one_hbm, two_hbm, three_hbm, owner_hbm, tiles_hbm, u_three_hbm, u_two_hbm, u_one_hbm, out, places, pack,
    one, two, three, owner, tiles, u_three, u_two, u_one, two_f32, in_sems, tile_sems,
):
    side = lax.axis_index("half")
    count, width = tiles.shape[:2]
    rank = u_three.shape[0]
    half = LANES // 2
    share = META // 2
    span = share * width
    pieces = tiles.shape[2] // (2 * span)
    moves = [(three_hbm, three), (u_three_hbm, u_three), (two_hbm, two), (one_hbm, one)]
    moves += [(owner_hbm, owner), (u_two_hbm, u_two), (u_one_hbm, u_one)]
    copies = [pltpu.make_async_copy(a, b, in_sems.at[i]) for i, (a, b) in enumerate(moves)]
    loads = [
        pltpu.make_async_copy(tiles_hbm.at[t], tiles.at[t], tile_sems.at[t]) for t in range(count)
    ]
    for copy in copies + loads:
        copy.start()
    copies[0].wait()
    copies[1].wait()
    weights = []
    for t in range(count):
        block = three[t]
        start = pl.multiple_of((block // 2) * LANES, LANES)
        window = u_three[:, pl.ds(start, LANES)].astype(F32)
        same = (lane_iota(window.shape) // half) == (block % 2)
        both = jnp.where(same, window, pltpu.roll(window, half, 1))
        tall = jnp.broadcast_to(both[:, None, :], (rank, share, LANES)).reshape(rank * share, LANES)
        full = jnp.concatenate([tall] * (span // LANES), axis=1)
        keep = (row_iota(full.shape) % share) == (lane_iota(full.shape) // width)
        weights.append(jnp.where(keep, full, 0.0).astype(BF16))
    for copy in copies[2:]:
        copy.wait()
    q = lax.axis_index("rep")
    pack[:rank, :] = u_two[...]
    pair = [u_one[: rank // 2, :], u_one[rank // 2 :, :]]
    pack[rank:, :] = jnp.concatenate(pair, axis=1).astype(BF16)
    two_f32[...] = u_two[...].astype(F32)
    top = two_f32[pl.ds(pl.multiple_of(q * share, share), share), :]
    low = u_one[pl.ds(pl.multiple_of(q * share, share), share), :]
    lane = lane_iota((share, half))
    ints = jnp.zeros((share, half), F32)
    spot = lane_iota(places.shape)
    place = jnp.zeros(places.shape, jnp.int32)
    for t in range(count):
        position = owner[one[t]]
        ints = jnp.where(lane == t, two[t].astype(F32), ints)
        ints = jnp.where(lane == count + t, position.astype(F32), ints)
        place = jnp.where(spot == t, position, place)
    places[...] = place
    meta = jnp.concatenate([top, jnp.concatenate([low, ints], axis=1)], axis=0).astype(BF16)
    rows = slice(2 * width, 2 * width + META)
    for k in range(out.shape[0]):
        out[k, rows, :] = meta
    for copy in loads:
        copy.wait()
    for n in range(pieces // 2):
        wide = []
        for t in range(count):
            groups = [tiles[t, :, (4 * n + g) * span : (4 * n + g + 1) * span] for g in range(4)]
            wide.append(nt(weights[t], jnp.concatenate(groups, axis=0)))
        for s in range(rank):
            at = slice(s * share, (s + 1) * share)
            for h in range(2):
                block = []
                for g in (2 * h, 2 * h + 1):
                    lanes = slice(g * width, (g + 1) * width)
                    block.append(jnp.concatenate([part[at, lanes] for part in wide], axis=1))
                start = (s % 2) * width + (2 * n + h) * META
                rows = slice(start, start + META)
                out[(s // 2) ^ side, rows, :] = jnp.concatenate(block, axis=0).astype(BF16)


def table_kernel(reps, got, far0, far1, far2, far3, out, readers, two, one, total):
    sources, depth = got.shape[:2]
    half = LANES // 2
    share = META // 2
    width = (depth - META) // 2
    rank = share * reps
    count = LANES // width
    owners = 2 * sources // reps
    blocks = 2 * owners
    side = lax.axis_index("half")
    lines = []
    halves = lane_iota((META, LANES)) // half
    for src in range(0, sources, 2):
        t, q = divmod(src, reps)
        rows = slice(q * share, (q + 2) * share)
        pair = [got[src + k, 2 * width : 2 * width + META, :].astype(F32) for k in range(2)]
        mine = jnp.concatenate([meta[:share] for meta in pair], axis=0)
        shard = side * (owners // 2) + t
        for k in range(2):
            two[2 * shard + k, rows, :] = jnp.where(halves == k, mine, 0.0).astype(BF16)
        one[shard, rows, :] = jnp.concatenate([meta[share:] for meta in pair], axis=0)
        lines += [meta[share : share + 1] for meta in pair]
    halves = lane_iota((rank, LANES)) // half
    for k, ref in enumerate((far0, far1, far2, far3)):
        shard = (1 - side) * (owners // 2) + (lax.axis_index("rest") ^ k)
        theirs = ref[:rank, :].astype(F32)
        for k in range(2):
            two[2 * shard + k] = jnp.where(halves == k, theirs, 0.0).astype(BF16)
        theirs = ref[rank:, :].astype(F32)
        one[shard, : rank // 2, :] = theirs
        one[shard, rank // 2 :, :] = pltpu.roll(theirs, half, 1)
    lines = jnp.concatenate(lines, axis=0)
    lane = lane_iota(lines.shape)
    scale = jnp.zeros(lines.shape, F32)
    for k in range(2 * count):
        scale = jnp.where(lane == half + k, float(blocks**k), scale)
    code = jnp.sum(lines * scale, axis=1, keepdims=True).astype(jnp.int32)
    total[...] = jnp.zeros_like(total)
    for src in range(sources):
        moving = []
        for s in range(2):
            block = got[src, s * width : (s + 1) * width, :]
            moving.append(jnp.concatenate([block, block], axis=0))
        moving = jnp.concatenate(moving, axis=1)
        left = code[src, 0]
        digits = []
        for _ in range(2 * count):
            digits.append(left % blocks)
            left = left // blocks
        stacked = jnp.concatenate([two[b] for b in digits[:count]], axis=0)
        product = jnp.dot(stacked, moving, preferred_element_type=F32).astype(BF16).astype(F32)
        for t, p in enumerate(digits[count:]):
            total[t, src % 2, p] += product[t * rank : (t + 1) * rank]
    for s in range(2):
        sums = []
        lanes = slice(s * LANES, (s + 1) * LANES)
        for p in range(owners):
            low = (total[0, 0, p, :, lanes] + total[0, 1, p, :, lanes])[:, :half]
            high = total[1, 0, p, :, lanes] + total[1, 1, p, :, lanes]
            sums.append(low + pltpu.roll(high, half, 1)[:, :half])
        out[s * rank : (s + 1) * rank, :] = jnp.concatenate(sums, axis=1).astype(BF16)
    readers[...] = jnp.concatenate([one[p][:, :half] for p in range(owners)], axis=1).astype(BF16)


def rows_kernel(mine, theirs, readers, out):
    high, low = split(mine[...].astype(F32) + theirs[...].astype(F32))
    project = (nt(readers[...], high) + nt(readers[...], low)).astype(BF16)
    part = jnp.dot(project, high, preferred_element_type=F32)
    part += jnp.dot(project, low, preferred_element_type=F32)
    out[...] = part.astype(BF16)


def final_kernel(places, a, b, factor, tile_factor, table):
    rank, rows_total = a.shape
    half = LANES // 2
    rows = a[...].astype(F32) + b[...].astype(F32)
    table[...] = rows
    g0 = dot3(rows, rows, 1)
    eye = (row_iota(g0.shape) == lane_iota(g0.shape)).astype(F32)
    msq = jnp.sum(rows * rows, keepdims=True) / rows_total
    inv = 1.0 / jnp.sqrt(msq + 1e-06)
    g = g0 * (inv * inv) / rows_total
    square = dot3(g, g)
    outer = dot3(square, 0.0625 * square - 0.5625 * g)
    step = (outer + (1.6875 * square - 2.4375 * g + 2.25 * eye)) * inv

    def block(p):
        window = table[:, pl.ds(pl.multiple_of((p // 2) * LANES, LANES), LANES)]
        return jnp.where(p % 2 == 1, pltpu.roll(window, half, 1), window)[:, :half]

    place = places[...]
    picks = [lax.axis_index(("half", "rest"))] + [place[0, t] for t in range(tile_factor.shape[0])]
    picked = jnp.concatenate([block(p) for p in picks], axis=1)
    x = dot3(step, picked)
    factor[...] = x[:, :half]
    for t in range(tile_factor.shape[0]):
        value = x[:, (t + 1) * half : (t + 2) * half]
        for r in range(0, rank, 2):
            line = jnp.concatenate([value[r : r + 1], value[r + 1 : r + 2]], axis=1)
            tile_factor[t : t + 1, r * half : (r + 2) * half] = line.astype(BF16)


def swap(x, size, mask):
    return lax.ppermute(x, ("half", "rest", "rep"), [(i, i ^ mask) for i in range(size)])


def sliced(tiles, block_one, block_two, block_three, owner_map, u_one, u_two, u_three):
    count, width = tiles.shape[:2]
    rank = u_three.shape[0]
    owners = 2 * lax.axis_size("rest")
    reps = lax.axis_size("rep")
    size = owners * reps
    sources = size // 2
    rows_total = owner_map.shape[0] * width
    depth = 2 * width + META
    vmem = pl.BlockSpec(memory_space=pltpu.VMEM)
    narrow = pltpu.CompilerParams(vmem_limit_bytes=NARROW)
    core, x, y, near, far = 1, 2, 4, 8, 16
    ints = (block_one, block_two, block_three, owner_map)
    arrays = (tiles, u_three, u_two, u_one)
    sends, places, pack = pl.pallas_call(
        first_kernel,
        out_shape=(
            jax.ShapeDtypeStruct((sources, depth, LANES), BF16),
            jax.ShapeDtypeStruct((META // 2, LANES), jnp.int32),
            jax.ShapeDtypeStruct((rank + rank // 2, LANES), BF16),
        ),
        in_specs=[pl.BlockSpec(memory_space=pltpu.HBM)] * 8,
        out_specs=(vmem, vmem, vmem),
        scratch_shapes=[pltpu.SMEM(a.shape, a.dtype) for a in ints]
        + [pltpu.VMEM(a.shape, a.dtype) for a in arrays]
        + [
            pltpu.VMEM(u_two.shape, F32),
            pltpu.SemaphoreType.DMA((7,)),
            pltpu.SemaphoreType.DMA((count,)),
        ],
        compiler_params=narrow,
        name="first",
    )(*[pltpu.with_memory_space_constraint(a, pltpu.HBM) for a in ints + arrays])
    theirs = [swap(pack, size, far | core | k * y) for k in range(4)]
    got = lax.all_to_all(sends, ("rest", "rep"), 0, 0, tiled=True)
    table, readers = pl.pallas_call(
        functools.partial(table_kernel, reps),
        out_shape=(
            jax.ShapeDtypeStruct((2 * rank, rows_total), BF16),
            jax.ShapeDtypeStruct((rank, rows_total), BF16),
        ),
        in_specs=[vmem] * 5,
        out_specs=(vmem, vmem),
        scratch_shapes=[
            pltpu.VMEM((2 * owners, rank, LANES), BF16),
            pltpu.VMEM((owners, rank, LANES), F32),
            pltpu.VMEM((count, 2, owners, rank, 2 * LANES), F32),
        ],
        compiler_params=narrow,
        name="table",
    )(got, *theirs)
    part = pl.pallas_call(
        rows_kernel,
        out_shape=jax.ShapeDtypeStruct((rank, rows_total), BF16),
        in_specs=[vmem] * 3,
        out_specs=vmem,
        compiler_params=narrow,
        name="rows_part",
    )(table, swap(table, size, far | core), readers)
    part = (part.astype(F32) + swap(part, size, core).astype(F32)).astype(BF16)
    pair = part.astype(F32) + swap(part, size, x | core).astype(F32)
    other = swap(part, size, y | core).astype(F32) + swap(part, size, x ^ y).astype(F32)
    part = (pair + other).astype(BF16)
    return pl.pallas_call(
        final_kernel,
        out_shape=(
            jax.ShapeDtypeStruct(u_one.shape, F32),
            jax.ShapeDtypeStruct((count, rank * width), BF16),
        ),
        in_specs=[vmem] * 3,
        out_specs=(vmem, vmem),
        scratch_shapes=[pltpu.VMEM((rank, rows_total), F32)],
        compiler_params=narrow,
        name="final",
    )(places, part, swap(part, size, near | core))


def fits(mesh, tiles, block_one, block_two, block_three, owner_map, u_one, u_two, u_three):
    owners, reps = mesh.shape["tiles"], mesh.shape["rep"]
    rank = u_three.shape[0]
    width = tiles.shape[1]
    return (
        owners == 8
        and reps == 4
        and rank == owners * reps == reps * META // 2
        and tiles.shape[0] == 2 * owners * reps
        and 2 * width == LANES
        and owner_map.shape[0] == owners
        and u_one.shape[1] == owners * width
        and u_two.shape[1] == owners * LANES
        and u_three.shape[1] % LANES == 0
    )


def specs(tiles, rep):
    both = tiles + rep
    ins = (P(both, None, None), P(both), P(both), P(both), P(), P(None, tiles), P(None, tiles), P())
    return ins, (P(None, tiles), P(both, None))


def solution(mesh):
    def run(*args):
        if fits(mesh, *args):
            axes = ("half", "rest", "rep")
            grid = mesh.devices.reshape(2, -1, mesh.shape["rep"])
            halves = jax.sharding.Mesh(grid, axes)
            ins, outs = specs(axes[:2], axes[2:])
            body, where = sliced, halves
        else:
            ins, outs = specs(("tiles",), ("rep",))
            body, where = general, mesh
        return jax.shard_map(body, mesh=where, in_specs=ins, out_specs=outs, check_vma=False)(*args)

    return run
```

```python
import functools

import jax
import jax.numpy as jnp
from jax import lax
from jax.experimental import pallas as pl
from jax.experimental.pallas import tpu as pltpu
from jax.sharding import PartitionSpec as P

NS_STEPS = 2
HI = lax.Precision.HIGHEST
LANES = 128
NARROW = 16 * 1024 * 1024
META = 16
F32 = jnp.float32
BF16 = jnp.bfloat16


def pick(table, index, width):
    grid = table.reshape(table.shape[0], -1, width)
    return jnp.transpose(jnp.take(grid, index, axis=1), (1, 0, 2))


def orthonormal(rows, rows_total):
    rank = rows.shape[0]
    g0 = jnp.dot(rows, rows.T, precision=HI, preferred_element_type=F32)
    msq = jnp.trace(g0) / rows_total
    inv = 1.0 / jnp.sqrt(msq + 1e-06)
    x = rows * inv
    g = g0 * (inv * inv) / rows_total
    eye = jnp.eye(rank, dtype=F32)
    for step in range(NS_STEPS):
        if step > 0:
            g = jnp.dot(x, x.T, precision=HI, preferred_element_type=F32) / rows_total
        x = jnp.dot(1.5 * eye - 0.5 * g, x, precision=HI, preferred_element_type=F32)
    return x


def general(tiles, block_one, block_two, block_three, owner_map, u_one, u_two, u_three):
    count, width = tiles.shape[:2]
    rank = u_three.shape[0]
    blocks_total = owner_map.shape[0]
    rows_total = blocks_total * width
    two_full = lax.all_gather(u_two, "tiles", axis=1, tiled=True)
    two_pick = pick(two_full, block_two, width)
    three_pick = pick(u_three, block_three, width)
    cube = tiles.reshape(count, width, width, width)
    first = jnp.einsum("tijk,tsk->tijs", cube, three_pick, preferred_element_type=F32).astype(BF16)
    second = jnp.einsum("tijs,trj->tirs", first, two_pick, preferred_element_type=F32)
    products = second.reshape(count, width, rank * rank).astype(BF16)
    positions = jnp.take(owner_map, block_one)
    onehot = (positions[:, None] == jnp.arange(blocks_total, dtype=jnp.int32)[None, :]).astype(F32)
    current = lax.all_gather(u_one.astype(BF16), "tiles", axis=1, tiled=True)
    readers = pick(current, positions, width)
    partial_value = jnp.einsum("tic,tri->rc", products, readers, preferred_element_type=F32)
    project = lax.psum(partial_value, ("tiles", "rep")).astype(BF16)
    z_tile = jnp.einsum("rc,tic->tri", project, products, preferred_element_type=F32)
    term = jnp.einsum("tri,tn->rni", z_tile, onehot, precision=HI).reshape(rank, rows_total)
    rows = lax.psum(term, ("tiles", "rep"))
    current = orthonormal(rows, rows_total)
    tile_factor = pick(current.astype(BF16), positions, width).reshape(count, rank * width)
    own = u_one.shape[1]
    factor = lax.dynamic_slice_in_dim(current, lax.axis_index("tiles") * own, own, 1)
    return (factor, tile_factor)


def split(a):
    high = a.astype(BF16)
    return high, (a - high.astype(F32)).astype(BF16)


def dot3(a, b, axis=0):
    (ah, al), (bh, bl) = split(a), split(b)
    dims = (((1,), (axis,)), ((), ()))
    parts = [lax.dot_general(p, q, dims, preferred_element_type=F32) for p, q in ((ah, bh), (ah, bl), (al, bh))]
    return parts[0] + (parts[1] + parts[2])


def lane_iota(shape):
    return lax.broadcasted_iota(jnp.int32, shape, len(shape) - 1)


def row_iota(shape):
    return lax.broadcasted_iota(jnp.int32, shape, len(shape) - 2)


def nt(a, b, precision=None):
    return lax.dot_general(
        a, b, (((1,), (1,)), ((), ())), precision=precision, preferred_element_type=F32
    )


def first_kernel(
    one_hbm, two_hbm, three_hbm, owner_hbm, tiles_hbm, u_three_hbm, u_two_hbm, u_one_hbm, out, places, pack,
    one, two, three, owner, tiles, u_three, u_two, u_one, two_f32, in_sems, tile_sems,
):
    side = lax.axis_index("half")
    count, width = tiles.shape[:2]
    rank = u_three.shape[0]
    half = LANES // 2
    share = META // 2
    span = share * width
    pieces = tiles.shape[2] // (2 * span)
    moves = [(three_hbm, three), (u_three_hbm, u_three), (two_hbm, two), (one_hbm, one)]
    moves += [(owner_hbm, owner), (u_two_hbm, u_two), (u_one_hbm, u_one)]
    copies = [pltpu.make_async_copy(a, b, in_sems.at[i]) for i, (a, b) in enumerate(moves)]
    loads = [
        pltpu.make_async_copy(tiles_hbm.at[t], tiles.at[t], tile_sems.at[t]) for t in range(count)
    ]
    for copy in copies + loads:
        copy.start()
    copies[0].wait()
    copies[1].wait()
    weights = []
    for t in range(count):
        block = three[t]
        start = pl.multiple_of((block // 2) * LANES, LANES)
        window = u_three[:, pl.ds(start, LANES)].astype(F32)
        same = (lane_iota(window.shape) // half) == (block % 2)
        both = jnp.where(same, window, pltpu.roll(window, half, 1))
        tall = jnp.broadcast_to(both[:, None, :], (rank, share, LANES)).reshape(rank * share, LANES)
        full = jnp.concatenate([tall] * (span // LANES), axis=1)
        keep = (row_iota(full.shape) % share) == (lane_iota(full.shape) // width)
        weights.append(jnp.where(keep, full, 0.0).astype(BF16))
    for copy in copies[2:]:
        copy.wait()
    q = lax.axis_index("rep")
    pack[:rank, :] = u_two[...]
    pair = [u_one[: rank // 2, :], u_one[rank // 2 :, :]]
    pack[rank:, :] = jnp.concatenate(pair, axis=1).astype(BF16)
    two_f32[...] = u_two[...].astype(F32)
    top = two_f32[pl.ds(pl.multiple_of(q * share, share), share), :]
    low = u_one[pl.ds(pl.multiple_of(q * share, share), share), :]
    lane = lane_iota((share, half))
    ints = jnp.zeros((share, half), F32)
    spot = lane_iota(places.shape)
    place = jnp.zeros(places.shape, jnp.int32)
    for t in range(count):
        position = owner[one[t]]
        ints = jnp.where(lane == t, two[t].astype(F32), ints)
        ints = jnp.where(lane == count + t, position.astype(F32), ints)
        place = jnp.where(spot == t, position, place)
    places[...] = place
    meta = jnp.concatenate([top, jnp.concatenate([low, ints], axis=1)], axis=0).astype(BF16)
    rows = slice(2 * width, 2 * width + META)
    for k in range(out.shape[0]):
        out[k, rows, :] = meta
    for copy in loads:
        copy.wait()
    for n in range(pieces // 2):
        wide = []
        for t in range(count):
            groups = [tiles[t, :, (4 * n + g) * span : (4 * n + g + 1) * span] for g in range(4)]
            wide.append(nt(weights[t], jnp.concatenate(groups, axis=0)))
        for s in range(rank):
            at = slice(s * share, (s + 1) * share)
            for h in range(2):
                block = []
                for g in (2 * h, 2 * h + 1):
                    lanes = slice(g * width, (g + 1) * width)
                    block.append(jnp.concatenate([part[at, lanes] for part in wide], axis=1))
                start = (s % 2) * width + (2 * n + h) * META
                rows = slice(start, start + META)
                out[(s // 2) ^ side, rows, :] = jnp.concatenate(block, axis=0).astype(BF16)


def table_kernel(reps, got, far0, far1, far2, far3, out, readers, two, one, total):
    sources, depth = got.shape[:2]
    half = LANES // 2
    share = META // 2
    width = (depth - META) // 2
    rank = share * reps
    count = LANES // width
    owners = 2 * sources // reps
    blocks = 2 * owners
    side = lax.axis_index("half")
    lines = []
    halves = lane_iota((META, LANES)) // half
    for src in range(0, sources, 2):
        t, q = divmod(src, reps)
        rows = slice(q * share, (q + 2) * share)
        pair = [got[src + k, 2 * width : 2 * width + META, :].astype(F32) for k in range(2)]
        mine = jnp.concatenate([meta[:share] for meta in pair], axis=0)
        shard = side * (owners // 2) + t
        for k in range(2):
            two[2 * shard + k, rows, :] = jnp.where(halves == k, mine, 0.0).astype(BF16)
        one[shard, rows, :] = jnp.concatenate([meta[share:] for meta in pair], axis=0)
        lines += [meta[share : share + 1] for meta in pair]
    halves = lane_iota((rank, LANES)) // half
    for k, ref in enumerate((far0, far1, far2, far3)):
        shard = (1 - side) * (owners // 2) + (lax.axis_index("rest") ^ k)
        theirs = ref[:rank, :].astype(F32)
        for k in range(2):
            two[2 * shard + k] = jnp.where(halves == k, theirs, 0.0).astype(BF16)
        theirs = ref[rank:, :].astype(F32)
        one[shard, : rank // 2, :] = theirs
        one[shard, rank // 2 :, :] = pltpu.roll(theirs, half, 1)
    lines = jnp.concatenate(lines, axis=0)
    lane = lane_iota(lines.shape)
    scale = jnp.zeros(lines.shape, F32)
    for k in range(2 * count):
        scale = jnp.where(lane == half + k, float(blocks**k), scale)
    code = jnp.sum(lines * scale, axis=1, keepdims=True).astype(jnp.int32)
    total[...] = jnp.zeros_like(total)
    for src in range(sources):
        moving = []
        for s in range(2):
            block = got[src, s * width : (s + 1) * width, :]
            moving.append(jnp.concatenate([block, block], axis=0))
        moving = jnp.concatenate(moving, axis=1)
        left = code[src, 0]
        digits = []
        for _ in range(2 * count):
            digits.append(left % blocks)
            left = left // blocks
        stacked = jnp.concatenate([two[b] for b in digits[:count]], axis=0)
        product = jnp.dot(stacked, moving, preferred_element_type=F32).astype(BF16).astype(F32)
        for t, p in enumerate(digits[count:]):
            total[t, src % 2, p] += product[t * rank : (t + 1) * rank]
    for s in range(2):
        sums = []
        lanes = slice(s * LANES, (s + 1) * LANES)
        for p in range(owners):
            low = (total[0, 0, p, :, lanes] + total[0, 1, p, :, lanes])[:, :half]
            high = total[1, 0, p, :, lanes] + total[1, 1, p, :, lanes]
            sums.append(low + pltpu.roll(high, half, 1)[:, :half])
        out[s * rank : (s + 1) * rank, :] = jnp.concatenate(sums, axis=1).astype(BF16)
    readers[...] = jnp.concatenate([one[p][:, :half] for p in range(owners)], axis=1).astype(BF16)


def rows_kernel(mine, theirs, readers, out):
    high, low = split(mine[...].astype(F32) + theirs[...].astype(F32))
    project = (nt(readers[...], high) + nt(readers[...], low)).astype(BF16)
    part = jnp.dot(project, high, preferred_element_type=F32)
    part += jnp.dot(project, low, preferred_element_type=F32)
    out[...] = part.astype(BF16)


def final_kernel(places, a, b, factor, tile_factor, table):
    rank, rows_total = a.shape
    half = LANES // 2
    rows = a[...].astype(F32) + b[...].astype(F32)
    table[...] = rows
    g0 = dot3(rows, rows, 1)
    eye = (row_iota(g0.shape) == lane_iota(g0.shape)).astype(F32)
    msq = jnp.sum(rows * rows, keepdims=True) / rows_total
    inv = 1.0 / jnp.sqrt(msq + 1e-06)
    g = g0 * (inv * inv) / rows_total
    square = dot3(g, g)
    outer = dot3(square, 0.0625 * square - 0.5625 * g)
    step = (outer + (1.6875 * square - 2.4375 * g + 2.25 * eye)) * inv

    def block(p):
        window = table[:, pl.ds(pl.multiple_of((p // 2) * LANES, LANES), LANES)]
        return jnp.where(p % 2 == 1, pltpu.roll(window, half, 1), window)[:, :half]

    place = places[...]
    picks = [lax.axis_index(("half", "rest"))] + [place[0, t] for t in range(tile_factor.shape[0])]
    picked = jnp.concatenate([block(p) for p in picks], axis=1)
    x = dot3(step, picked)
    factor[...] = x[:, :half]
    for t in range(tile_factor.shape[0]):
        value = x[:, (t + 1) * half : (t + 2) * half]
        for r in range(0, rank, 2):
            line = jnp.concatenate([value[r : r + 1], value[r + 1 : r + 2]], axis=1)
            tile_factor[t : t + 1, r * half : (r + 2) * half] = line.astype(BF16)


def swap(x, size, mask):
    return lax.ppermute(x, ("half", "rest", "rep"), [(i, i ^ mask) for i in range(size)])


def sliced(tiles, block_one, block_two, block_three, owner_map, u_one, u_two, u_three):
    count, width = tiles.shape[:2]
    rank = u_three.shape[0]
    owners = 2 * lax.axis_size("rest")
    reps = lax.axis_size("rep")
    size = owners * reps
    sources = size // 2
    rows_total = owner_map.shape[0] * width
    depth = 2 * width + META
    vmem = pl.BlockSpec(memory_space=pltpu.VMEM)
    narrow = pltpu.CompilerParams(vmem_limit_bytes=NARROW)
    core, x, y, near, far = 1, 2, 4, 8, 16
    ints = (block_one, block_two, block_three, owner_map)
    arrays = (tiles, u_three, u_two, u_one)
    sends, places, pack = pl.pallas_call(
        first_kernel,
        out_shape=(
            jax.ShapeDtypeStruct((sources, depth, LANES), BF16),
            jax.ShapeDtypeStruct((META // 2, LANES), jnp.int32),
            jax.ShapeDtypeStruct((rank + rank // 2, LANES), BF16),
        ),
        in_specs=[pl.BlockSpec(memory_space=pltpu.HBM)] * 8,
        out_specs=(vmem, vmem, vmem),
        scratch_shapes=[pltpu.SMEM(a.shape, a.dtype) for a in ints]
        + [pltpu.VMEM(a.shape, a.dtype) for a in arrays]
        + [
            pltpu.VMEM(u_two.shape, F32),
            pltpu.SemaphoreType.DMA((7,)),
            pltpu.SemaphoreType.DMA((count,)),
        ],
        compiler_params=narrow,
        name="first",
    )(*[pltpu.with_memory_space_constraint(a, pltpu.HBM) for a in ints + arrays])
    theirs = [swap(pack, size, far | core | k * y) for k in range(4)]
    got = lax.all_to_all(sends, ("rest", "rep"), 0, 0, tiled=True)
    table, readers = pl.pallas_call(
        functools.partial(table_kernel, reps),
        out_shape=(
            jax.ShapeDtypeStruct((2 * rank, rows_total), BF16),
            jax.ShapeDtypeStruct((rank, rows_total), BF16),
        ),
        in_specs=[vmem] * 5,
        out_specs=(vmem, vmem),
        scratch_shapes=[
            pltpu.VMEM((2 * owners, rank, LANES), BF16),
            pltpu.VMEM((owners, rank, LANES), F32),
            pltpu.VMEM((count, 2, owners, rank, 2 * LANES), F32),
        ],
        compiler_params=narrow,
        name="table",
    )(got, *theirs)
    part = pl.pallas_call(
        rows_kernel,
        out_shape=jax.ShapeDtypeStruct((rank, rows_total), BF16),
        in_specs=[vmem] * 3,
        out_specs=vmem,
        compiler_params=narrow,
        name="rows_part",
    )(table, swap(table, size, far | core), readers)
    part = (part.astype(F32) + swap(part, size, core).astype(F32)).astype(BF16)
    pair = part.astype(F32) + swap(part, size, y | core).astype(F32)
    other = swap(part, size, x | core).astype(F32) + swap(part, size, x ^ y).astype(F32)
    part = (pair + other).astype(BF16)
    return pl.pallas_call(
        final_kernel,
        out_shape=(
            jax.ShapeDtypeStruct(u_one.shape, F32),
            jax.ShapeDtypeStruct((count, rank * width), BF16),
        ),
        in_specs=[vmem] * 3,
        out_specs=(vmem, vmem),
        scratch_shapes=[pltpu.VMEM((rank, rows_total), F32)],
        compiler_params=narrow,
        name="final",
    )(places, part, swap(part, size, near | core))


def fits(mesh, tiles, block_one, block_two, block_three, owner_map, u_one, u_two, u_three):
    owners, reps = mesh.shape["tiles"], mesh.shape["rep"]
    rank = u_three.shape[0]
    width = tiles.shape[1]
    return (
        owners == 8
        and reps == 4
        and rank == owners * reps == reps * META // 2
        and tiles.shape[0] == 2 * owners * reps
        and 2 * width == LANES
        and owner_map.shape[0] == owners
        and u_one.shape[1] == owners * width
        and u_two.shape[1] == owners * LANES
        and u_three.shape[1] % LANES == 0
    )


def specs(tiles, rep):
    both = tiles + rep
    ins = (P(both, None, None), P(both), P(both), P(both), P(), P(None, tiles), P(None, tiles), P())
    return ins, (P(None, tiles), P(both, None))


def solution(mesh):
    def run(*args):
        if fits(mesh, *args):
            axes = ("half", "rest", "rep")
            grid = mesh.devices.reshape(2, -1, mesh.shape["rep"])
            halves = jax.sharding.Mesh(grid, axes)
            ins, outs = specs(axes[:2], axes[2:])
            body, where = sliced, halves
        else:
            ins, outs = specs(("tiles",), ("rep",))
            body, where = general, mesh
        return jax.shard_map(body, mesh=where, in_specs=ins, out_specs=outs, check_vma=False)(*args)

    return run
```

```python
import functools

import jax
import jax.numpy as jnp
from jax import lax
from jax.experimental import pallas as pl
from jax.experimental.pallas import tpu as pltpu
from jax.sharding import PartitionSpec as P

NS_STEPS = 2
HI = lax.Precision.HIGHEST
LANES = 128
NARROW = 16 * 1024 * 1024
META = 16
F32 = jnp.float32
BF16 = jnp.bfloat16


def pick(table, index, width):
    grid = table.reshape(table.shape[0], -1, width)
    return jnp.transpose(jnp.take(grid, index, axis=1), (1, 0, 2))


def orthonormal(rows, rows_total):
    rank = rows.shape[0]
    g0 = jnp.dot(rows, rows.T, precision=HI, preferred_element_type=F32)
    msq = jnp.trace(g0) / rows_total
    inv = 1.0 / jnp.sqrt(msq + 1e-06)
    x = rows * inv
    g = g0 * (inv * inv) / rows_total
    eye = jnp.eye(rank, dtype=F32)
    for step in range(NS_STEPS):
        if step > 0:
            g = jnp.dot(x, x.T, precision=HI, preferred_element_type=F32) / rows_total
        x = jnp.dot(1.5 * eye - 0.5 * g, x, precision=HI, preferred_element_type=F32)
    return x


def general(tiles, block_one, block_two, block_three, owner_map, u_one, u_two, u_three):
    count, width = tiles.shape[:2]
    rank = u_three.shape[0]
    blocks_total = owner_map.shape[0]
    rows_total = blocks_total * width
    two_full = lax.all_gather(u_two, "tiles", axis=1, tiled=True)
    two_pick = pick(two_full, block_two, width)
    three_pick = pick(u_three, block_three, width)
    cube = tiles.reshape(count, width, width, width)
    first = jnp.einsum("tijk,tsk->tijs", cube, three_pick, preferred_element_type=F32).astype(BF16)
    second = jnp.einsum("tijs,trj->tirs", first, two_pick, preferred_element_type=F32)
    products = second.reshape(count, width, rank * rank).astype(BF16)
    positions = jnp.take(owner_map, block_one)
    onehot = (positions[:, None] == jnp.arange(blocks_total, dtype=jnp.int32)[None, :]).astype(F32)
    current = lax.all_gather(u_one.astype(BF16), "tiles", axis=1, tiled=True)
    readers = pick(current, positions, width)
    partial_value = jnp.einsum("tic,tri->rc", products, readers, preferred_element_type=F32)
    project = lax.psum(partial_value, ("tiles", "rep")).astype(BF16)
    z_tile = jnp.einsum("rc,tic->tri", project, products, preferred_element_type=F32)
    term = jnp.einsum("tri,tn->rni", z_tile, onehot, precision=HI).reshape(rank, rows_total)
    rows = lax.psum(term, ("tiles", "rep"))
    current = orthonormal(rows, rows_total)
    tile_factor = pick(current.astype(BF16), positions, width).reshape(count, rank * width)
    own = u_one.shape[1]
    factor = lax.dynamic_slice_in_dim(current, lax.axis_index("tiles") * own, own, 1)
    return (factor, tile_factor)


def split(a):
    high = a.astype(BF16)
    return high, (a - high.astype(F32)).astype(BF16)


def dot3(a, b, axis=0):
    (ah, al), (bh, bl) = split(a), split(b)
    dims = (((1,), (axis,)), ((), ()))
    parts = [lax.dot_general(p, q, dims, preferred_element_type=F32) for p, q in ((ah, bh), (ah, bl), (al, bh))]
    return parts[0] + (parts[1] + parts[2])


def lane_iota(shape):
    return lax.broadcasted_iota(jnp.int32, shape, len(shape) - 1)


def row_iota(shape):
    return lax.broadcasted_iota(jnp.int32, shape, len(shape) - 2)


def nt(a, b, precision=None):
    return lax.dot_general(
        a, b, (((1,), (1,)), ((), ())), precision=precision, preferred_element_type=F32
    )


def first_kernel(
    one_hbm, two_hbm, three_hbm, owner_hbm, tiles_hbm, u_three_hbm, u_two_hbm, u_one_hbm, out, places, pack,
    one, two, three, owner, tiles, u_three, u_two, u_one, two_f32, in_sems, tile_sems,
):
    side = lax.axis_index("half")
    count, width = tiles.shape[:2]
    rank = u_three.shape[0]
    half = LANES // 2
    share = META // 2
    span = share * width
    pieces = tiles.shape[2] // (2 * span)
    moves = [(three_hbm, three), (u_three_hbm, u_three), (two_hbm, two), (one_hbm, one)]
    moves += [(owner_hbm, owner), (u_two_hbm, u_two), (u_one_hbm, u_one)]
    copies = [pltpu.make_async_copy(a, b, in_sems.at[i]) for i, (a, b) in enumerate(moves)]
    loads = [
        pltpu.make_async_copy(tiles_hbm.at[t], tiles.at[t], tile_sems.at[t]) for t in range(count)
    ]
    for copy in copies + loads:
        copy.start()
    copies[0].wait()
    copies[1].wait()
    weights = []
    for t in range(count):
        block = three[t]
        start = pl.multiple_of((block // 2) * LANES, LANES)
        window = u_three[:, pl.ds(start, LANES)].astype(F32)
        same = (lane_iota(window.shape) // half) == (block % 2)
        both = jnp.where(same, window, pltpu.roll(window, half, 1))
        tall = jnp.broadcast_to(both[:, None, :], (rank, share, LANES)).reshape(rank * share, LANES)
        full = jnp.concatenate([tall] * (span // LANES), axis=1)
        keep = (row_iota(full.shape) % share) == (lane_iota(full.shape) // width)
        weights.append(jnp.where(keep, full, 0.0).astype(BF16))
    for copy in copies[2:]:
        copy.wait()
    q = lax.axis_index("rep")
    pack[:rank, :] = u_two[...]
    pair = [u_one[: rank // 2, :], u_one[rank // 2 :, :]]
    pack[rank:, :] = jnp.concatenate(pair, axis=1).astype(BF16)
    two_f32[...] = u_two[...].astype(F32)
    top = two_f32[pl.ds(pl.multiple_of(q * share, share), share), :]
    low = u_one[pl.ds(pl.multiple_of(q * share, share), share), :]
    lane = lane_iota((share, half))
    ints = jnp.zeros((share, half), F32)
    spot = lane_iota(places.shape)
    place = jnp.zeros(places.shape, jnp.int32)
    for t in range(count):
        position = owner[one[t]]
        ints = jnp.where(lane == t, two[t].astype(F32), ints)
        ints = jnp.where(lane == count + t, position.astype(F32), ints)
        place = jnp.where(spot == t, position, place)
    places[...] = place
    meta = jnp.concatenate([top, jnp.concatenate([low, ints], axis=1)], axis=0).astype(BF16)
    rows = slice(2 * width, 2 * width + META)
    for k in range(out.shape[0]):
        out[k, rows, :] = meta
    for copy in loads:
        copy.wait()
    for n in range(pieces // 2):
        wide = []
        for t in range(count):
            groups = [tiles[t, :, (4 * n + g) * span : (4 * n + g + 1) * span] for g in range(4)]
            wide.append(nt(weights[t], jnp.concatenate(groups, axis=0)))
        for s in range(rank):
            at = slice(s * share, (s + 1) * share)
            for h in range(2):
                block = []
                for g in (2 * h, 2 * h + 1):
                    lanes = slice(g * width, (g + 1) * width)
                    block.append(jnp.concatenate([part[at, lanes] for part in wide], axis=1))
                start = (s % 2) * width + (2 * n + h) * META
                rows = slice(start, start + META)
                out[(s // 2) ^ side, rows, :] = jnp.concatenate(block, axis=0).astype(BF16)


def table_kernel(reps, got, far0, far1, far2, far3, out, readers, two, one, total):
    sources, depth = got.shape[:2]
    half = LANES // 2
    share = META // 2
    width = (depth - META) // 2
    rank = share * reps
    count = LANES // width
    owners = 2 * sources // reps
    blocks = 2 * owners
    side = lax.axis_index("half")
    lines = []
    halves = lane_iota((META, LANES)) // half
    for src in range(0, sources, 2):
        t, q = divmod(src, reps)
        rows = slice(q * share, (q + 2) * share)
        pair = [got[src + k, 2 * width : 2 * width + META, :].astype(F32) for k in range(2)]
        mine = jnp.concatenate([meta[:share] for meta in pair], axis=0)
        shard = side * (owners // 2) + t
        for k in range(2):
            two[2 * shard + k, rows, :] = jnp.where(halves == k, mine, 0.0).astype(BF16)
        one[shard, rows, :] = jnp.concatenate([meta[share:] for meta in pair], axis=0)
        lines += [meta[share : share + 1] for meta in pair]
    halves = lane_iota((rank, LANES)) // half
    for k, ref in enumerate((far0, far1, far2, far3)):
        shard = (1 - side) * (owners // 2) + (lax.axis_index("rest") ^ k)
        theirs = ref[:rank, :].astype(F32)
        for k in range(2):
            two[2 * shard + k] = jnp.where(halves == k, theirs, 0.0).astype(BF16)
        theirs = ref[rank:, :].astype(F32)
        one[shard, : rank // 2, :] = theirs
        one[shard, rank // 2 :, :] = pltpu.roll(theirs, half, 1)
    lines = jnp.concatenate(lines, axis=0)
    lane = lane_iota(lines.shape)
    scale = jnp.zeros(lines.shape, F32)
    for k in range(2 * count):
        scale = jnp.where(lane == half + k, float(blocks**k), scale)
    code = jnp.sum(lines * scale, axis=1, keepdims=True).astype(jnp.int32)
    total[...] = jnp.zeros_like(total)
    for src in range(sources):
        moving = []
        for s in range(2):
            block = got[src, s * width : (s + 1) * width, :]
            moving.append(jnp.concatenate([block, block], axis=0))
        moving = jnp.concatenate(moving, axis=1)
        left = code[src, 0]
        digits = []
        for _ in range(2 * count):
            digits.append(left % blocks)
            left = left // blocks
        stacked = jnp.concatenate([two[b] for b in digits[:count]], axis=0)
        product = jnp.dot(stacked, moving, preferred_element_type=F32).astype(BF16).astype(F32)
        for t, p in enumerate(digits[count:]):
            total[t, src % 2, p] += product[t * rank : (t + 1) * rank]
    for s in range(2):
        sums = []
        lanes = slice(s * LANES, (s + 1) * LANES)
        for p in range(owners):
            low = (total[0, 0, p, :, lanes] + total[0, 1, p, :, lanes])[:, :half]
            high = total[1, 0, p, :, lanes] + total[1, 1, p, :, lanes]
            sums.append(low + pltpu.roll(high, half, 1)[:, :half])
        out[s * rank : (s + 1) * rank, :] = jnp.concatenate(sums, axis=1).astype(BF16)
    readers[...] = jnp.concatenate([one[p][:, :half] for p in range(owners)], axis=1).astype(BF16)


def known_kernel(mine, readers, out):
    out[...] = nt(readers[...], mine[...])


def rows_kernel(mine, theirs, readers, known, out):
    project = (known[...] + nt(readers[...], theirs[...])).astype(BF16)
    part = jnp.dot(project, mine[...], preferred_element_type=F32)
    part += jnp.dot(project, theirs[...], preferred_element_type=F32)
    out[...] = part.astype(BF16)


def final_kernel(places, a, b, c, d, factor, tile_factor, table):
    rank, rows_total = a.shape
    half = LANES // 2
    rows = (a[...].astype(F32) + b[...].astype(F32)) + (c[...].astype(F32) + d[...].astype(F32))
    table[...] = rows
    g0 = dot3(rows, rows, 1)
    eye = (row_iota(g0.shape) == lane_iota(g0.shape)).astype(F32)
    msq = jnp.sum(rows * rows, keepdims=True) / rows_total
    inv = 1.0 / jnp.sqrt(msq + 1e-06)
    g = g0 * (inv * inv) / rows_total
    square = dot3(g, g)
    outer = dot3(square, 0.0625 * square - 0.5625 * g)
    step = (outer + (1.6875 * square - 2.4375 * g + 2.25 * eye)) * inv

    def block(p):
        window = table[:, pl.ds(pl.multiple_of((p // 2) * LANES, LANES), LANES)]
        return jnp.where(p % 2 == 1, pltpu.roll(window, half, 1), window)[:, :half]

    place = places[...]
    picks = [lax.axis_index(("half", "rest"))] + [place[0, t] for t in range(tile_factor.shape[0])]
    picked = jnp.concatenate([block(p) for p in picks], axis=1)
    x = dot3(step, picked)
    factor[...] = x[:, :half]
    for t in range(tile_factor.shape[0]):
        value = x[:, (t + 1) * half : (t + 2) * half]
        for r in range(0, rank, 2):
            line = jnp.concatenate([value[r : r + 1], value[r + 1 : r + 2]], axis=1)
            tile_factor[t : t + 1, r * half : (r + 2) * half] = line.astype(BF16)


def swap(x, size, mask):
    return lax.ppermute(x, ("half", "rest", "rep"), [(i, i ^ mask) for i in range(size)])


def sliced(tiles, block_one, block_two, block_three, owner_map, u_one, u_two, u_three):
    count, width = tiles.shape[:2]
    rank = u_three.shape[0]
    owners = 2 * lax.axis_size("rest")
    reps = lax.axis_size("rep")
    size = owners * reps
    sources = size // 2
    rows_total = owner_map.shape[0] * width
    depth = 2 * width + META
    vmem = pl.BlockSpec(memory_space=pltpu.VMEM)
    narrow = pltpu.CompilerParams(vmem_limit_bytes=NARROW)
    core, x, y, near, far = 1, 2, 4, 8, 16
    ints = (block_one, block_two, block_three, owner_map)
    arrays = (tiles, u_three, u_two, u_one)
    sends, places, pack = pl.pallas_call(
        first_kernel,
        out_shape=(
            jax.ShapeDtypeStruct((sources, depth, LANES), BF16),
            jax.ShapeDtypeStruct((META // 2, LANES), jnp.int32),
            jax.ShapeDtypeStruct((rank + rank // 2, LANES), BF16),
        ),
        in_specs=[pl.BlockSpec(memory_space=pltpu.HBM)] * 8,
        out_specs=(vmem, vmem, vmem),
        scratch_shapes=[pltpu.SMEM(a.shape, a.dtype) for a in ints]
        + [pltpu.VMEM(a.shape, a.dtype) for a in arrays]
        + [
            pltpu.VMEM(u_two.shape, F32),
            pltpu.SemaphoreType.DMA((7,)),
            pltpu.SemaphoreType.DMA((count,)),
        ],
        compiler_params=narrow,
        name="first",
    )(*[pltpu.with_memory_space_constraint(a, pltpu.HBM) for a in ints + arrays])
    theirs = [swap(pack, size, far | core | k * y) for k in range(4)]
    got = lax.all_to_all(sends, ("rest", "rep"), 0, 0, tiled=True)
    table, readers = pl.pallas_call(
        functools.partial(table_kernel, reps),
        out_shape=(
            jax.ShapeDtypeStruct((2 * rank, rows_total), BF16),
            jax.ShapeDtypeStruct((rank, rows_total), BF16),
        ),
        in_specs=[vmem] * 5,
        out_specs=(vmem, vmem),
        scratch_shapes=[
            pltpu.VMEM((2 * owners, rank, LANES), BF16),
            pltpu.VMEM((owners, rank, LANES), F32),
            pltpu.VMEM((count, 2, owners, rank, 2 * LANES), F32),
        ],
        compiler_params=narrow,
        name="table",
    )(got, *theirs)
    known = pl.pallas_call(
        known_kernel,
        out_shape=jax.ShapeDtypeStruct((rank, 2 * rank), F32),
        in_specs=[vmem] * 2,
        out_specs=vmem,
        compiler_params=narrow,
        name="known",
    )(table, readers)
    part = pl.pallas_call(
        rows_kernel,
        out_shape=jax.ShapeDtypeStruct((rank, rows_total), BF16),
        in_specs=[vmem] * 4,
        out_specs=vmem,
        compiler_params=narrow,
        name="rows_part",
    )(table, swap(table, size, far | core), readers, known)
    part = (part.astype(F32) + swap(part, size, core).astype(F32)).astype(BF16)
    part = (part.astype(F32) + swap(part, size, near | core).astype(F32)).astype(BF16)
    rest = [swap(part, size, mask) for mask in (y | core, x | core, x ^ y)]
    return pl.pallas_call(
        final_kernel,
        out_shape=(
            jax.ShapeDtypeStruct(u_one.shape, F32),
            jax.ShapeDtypeStruct((count, rank * width), BF16),
        ),
        in_specs=[vmem] * 5,
        out_specs=(vmem, vmem),
        scratch_shapes=[pltpu.VMEM((rank, rows_total), F32)],
        compiler_params=narrow,
        name="final",
    )(places, part, *rest)


def fits(mesh, tiles, block_one, block_two, block_three, owner_map, u_one, u_two, u_three):
    owners, reps = mesh.shape["tiles"], mesh.shape["rep"]
    rank = u_three.shape[0]
    width = tiles.shape[1]
    return (
        owners == 8
        and reps == 4
        and rank == owners * reps == reps * META // 2
        and tiles.shape[0] == 2 * owners * reps
        and 2 * width == LANES
        and owner_map.shape[0] == owners
        and u_one.shape[1] == owners * width
        and u_two.shape[1] == owners * LANES
        and u_three.shape[1] % LANES == 0
    )


def specs(tiles, rep):
    both = tiles + rep
    ins = (P(both, None, None), P(both), P(both), P(both), P(), P(None, tiles), P(None, tiles), P())
    return ins, (P(None, tiles), P(both, None))


def solution(mesh):
    def run(*args):
        if fits(mesh, *args):
            axes = ("half", "rest", "rep")
            grid = mesh.devices.reshape(2, -1, mesh.shape["rep"])
            halves = jax.sharding.Mesh(grid, axes)
            ins, outs = specs(axes[:2], axes[2:])
            body, where = sliced, halves
        else:
            ins, outs = specs(("tiles",), ("rep",))
            body, where = general, mesh
        return jax.shard_map(body, mesh=where, in_specs=ins, out_specs=outs, check_vma=False)(*args)

    return run
```

```python
import functools

import jax
import jax.numpy as jnp
from jax import lax
from jax.experimental import pallas as pl
from jax.experimental.pallas import tpu as pltpu
from jax.sharding import PartitionSpec as P

NS_STEPS = 2
HI = lax.Precision.HIGHEST
LANES = 128
NARROW = 16 * 1024 * 1024
META = 16
F32 = jnp.float32
BF16 = jnp.bfloat16


def pick(table, index, width):
    grid = table.reshape(table.shape[0], -1, width)
    return jnp.transpose(jnp.take(grid, index, axis=1), (1, 0, 2))


def orthonormal(rows, rows_total):
    rank = rows.shape[0]
    g0 = jnp.dot(rows, rows.T, precision=HI, preferred_element_type=F32)
    msq = jnp.trace(g0) / rows_total
    inv = 1.0 / jnp.sqrt(msq + 1e-06)
    x = rows * inv
    g = g0 * (inv * inv) / rows_total
    eye = jnp.eye(rank, dtype=F32)
    for step in range(NS_STEPS):
        if step > 0:
            g = jnp.dot(x, x.T, precision=HI, preferred_element_type=F32) / rows_total
        x = jnp.dot(1.5 * eye - 0.5 * g, x, precision=HI, preferred_element_type=F32)
    return x


def general(tiles, block_one, block_two, block_three, owner_map, u_one, u_two, u_three):
    count, width = tiles.shape[:2]
    rank = u_three.shape[0]
    blocks_total = owner_map.shape[0]
    rows_total = blocks_total * width
    two_full = lax.all_gather(u_two, "tiles", axis=1, tiled=True)
    two_pick = pick(two_full, block_two, width)
    three_pick = pick(u_three, block_three, width)
    cube = tiles.reshape(count, width, width, width)
    first = jnp.einsum("tijk,tsk->tijs", cube, three_pick, preferred_element_type=F32).astype(BF16)
    second = jnp.einsum("tijs,trj->tirs", first, two_pick, preferred_element_type=F32)
    products = second.reshape(count, width, rank * rank).astype(BF16)
    positions = jnp.take(owner_map, block_one)
    onehot = (positions[:, None] == jnp.arange(blocks_total, dtype=jnp.int32)[None, :]).astype(F32)
    current = lax.all_gather(u_one.astype(BF16), "tiles", axis=1, tiled=True)
    readers = pick(current, positions, width)
    partial_value = jnp.einsum("tic,tri->rc", products, readers, preferred_element_type=F32)
    project = lax.psum(partial_value, ("tiles", "rep")).astype(BF16)
    z_tile = jnp.einsum("rc,tic->tri", project, products, preferred_element_type=F32)
    term = jnp.einsum("tri,tn->rni", z_tile, onehot, precision=HI).reshape(rank, rows_total)
    rows = lax.psum(term, ("tiles", "rep"))
    current = orthonormal(rows, rows_total)
    tile_factor = pick(current.astype(BF16), positions, width).reshape(count, rank * width)
    own = u_one.shape[1]
    factor = lax.dynamic_slice_in_dim(current, lax.axis_index("tiles") * own, own, 1)
    return (factor, tile_factor)


def split(a):
    high = a.astype(BF16)
    return high, (a - high.astype(F32)).astype(BF16)


def dot3(a, b, axis=0):
    (ah, al), (bh, bl) = split(a), split(b)
    dims = (((1,), (axis,)), ((), ()))
    parts = [lax.dot_general(p, q, dims, preferred_element_type=F32) for p, q in ((ah, bh), (ah, bl), (al, bh))]
    return parts[0] + (parts[1] + parts[2])


def lane_iota(shape):
    return lax.broadcasted_iota(jnp.int32, shape, len(shape) - 1)


def row_iota(shape):
    return lax.broadcasted_iota(jnp.int32, shape, len(shape) - 2)


def nt(a, b, precision=None):
    return lax.dot_general(
        a, b, (((1,), (1,)), ((), ())), precision=precision, preferred_element_type=F32
    )


def first_kernel(
    one_hbm, two_hbm, three_hbm, owner_hbm, tiles_hbm, u_three_hbm, u_two_hbm, u_one_hbm, out, places, pack,
    one, two, three, owner, tiles, u_three, u_two, u_one, two_f32, in_sems, tile_sems,
):
    side = lax.axis_index("half")
    count, width = tiles.shape[:2]
    rank = u_three.shape[0]
    half = LANES // 2
    share = META // 2
    span = share * width
    pieces = tiles.shape[2] // (2 * span)
    moves = [(three_hbm, three), (u_three_hbm, u_three), (two_hbm, two), (one_hbm, one)]
    moves += [(owner_hbm, owner), (u_two_hbm, u_two), (u_one_hbm, u_one)]
    copies = [pltpu.make_async_copy(a, b, in_sems.at[i]) for i, (a, b) in enumerate(moves)]
    loads = [
        pltpu.make_async_copy(tiles_hbm.at[t], tiles.at[t], tile_sems.at[t]) for t in range(count)
    ]
    for copy in copies + loads:
        copy.start()
    copies[0].wait()
    copies[1].wait()
    weights = []
    for t in range(count):
        block = three[t]
        start = pl.multiple_of((block // 2) * LANES, LANES)
        window = u_three[:, pl.ds(start, LANES)].astype(F32)
        same = (lane_iota(window.shape) // half) == (block % 2)
        both = jnp.where(same, window, pltpu.roll(window, half, 1))
        tall = jnp.broadcast_to(both[:, None, :], (rank, share, LANES)).reshape(rank * share, LANES)
        full = jnp.concatenate([tall] * (span // LANES), axis=1)
        keep = (row_iota(full.shape) % share) == (lane_iota(full.shape) // width)
        weights.append(jnp.where(keep, full, 0.0).astype(BF16))
    for copy in copies[2:]:
        copy.wait()
    q = lax.axis_index("rep")
    pack[:rank, :] = u_two[...]
    pair = [u_one[: rank // 2, :], u_one[rank // 2 :, :]]
    pack[rank:, :] = jnp.concatenate(pair, axis=1).astype(BF16)
    two_f32[...] = u_two[...].astype(F32)
    top = two_f32[pl.ds(pl.multiple_of(q * share, share), share), :]
    low = u_one[pl.ds(pl.multiple_of(q * share, share), share), :]
    lane = lane_iota((share, half))
    ints = jnp.zeros((share, half), F32)
    spot = lane_iota(places.shape)
    place = jnp.zeros(places.shape, jnp.int32)
    for t in range(count):
        position = owner[one[t]]
        ints = jnp.where(lane == t, two[t].astype(F32), ints)
        ints = jnp.where(lane == count + t, position.astype(F32), ints)
        place = jnp.where(spot == t, position, place)
    places[...] = place
    meta = jnp.concatenate([top, jnp.concatenate([low, ints], axis=1)], axis=0).astype(BF16)
    rows = slice(2 * width, 2 * width + META)
    for k in range(out.shape[0]):
        out[k, rows, :] = meta
    for copy in loads:
        copy.wait()
    for n in range(pieces // 2):
        wide = []
        for t in range(count):
            groups = [tiles[t, :, (4 * n + g) * span : (4 * n + g + 1) * span] for g in range(4)]
            wide.append(nt(weights[t], jnp.concatenate(groups, axis=0)))
        for s in range(rank):
            at = slice(s * share, (s + 1) * share)
            for h in range(2):
                block = []
                for g in (2 * h, 2 * h + 1):
                    lanes = slice(g * width, (g + 1) * width)
                    block.append(jnp.concatenate([part[at, lanes] for part in wide], axis=1))
                start = (s % 2) * width + (2 * n + h) * META
                rows = slice(start, start + META)
                out[(s // 2) ^ side, rows, :] = jnp.concatenate(block, axis=0).astype(BF16)


def table_kernel(reps, got, far0, far1, far2, far3, out, readers, two, one, total):
    sources, depth = got.shape[:2]
    half = LANES // 2
    share = META // 2
    width = (depth - META) // 2
    rank = share * reps
    count = LANES // width
    owners = 2 * sources // reps
    blocks = 2 * owners
    side = lax.axis_index("half")
    lines = []
    halves = lane_iota((META, LANES)) // half
    for src in range(0, sources, 2):
        t, q = divmod(src, reps)
        rows = slice(q * share, (q + 2) * share)
        pair = [got[src + k, 2 * width : 2 * width + META, :].astype(F32) for k in range(2)]
        mine = jnp.concatenate([meta[:share] for meta in pair], axis=0)
        shard = side * (owners // 2) + t
        for k in range(2):
            two[2 * shard + k, rows, :] = jnp.where(halves == k, mine, 0.0).astype(BF16)
        one[shard, rows, :] = jnp.concatenate([meta[share:] for meta in pair], axis=0)
        lines += [meta[share : share + 1] for meta in pair]
    halves = lane_iota((rank, LANES)) // half
    for k, ref in enumerate((far0, far1, far2, far3)):
        shard = (1 - side) * (owners // 2) + (lax.axis_index("rest") ^ k)
        theirs = ref[:rank, :].astype(F32)
        for k in range(2):
            two[2 * shard + k] = jnp.where(halves == k, theirs, 0.0).astype(BF16)
        theirs = ref[rank:, :].astype(F32)
        one[shard, : rank // 2, :] = theirs
        one[shard, rank // 2 :, :] = pltpu.roll(theirs, half, 1)
    lines = jnp.concatenate(lines, axis=0)
    lane = lane_iota(lines.shape)
    scale = jnp.zeros(lines.shape, F32)
    for k in range(2 * count):
        scale = jnp.where(lane == half + k, float(blocks**k), scale)
    code = jnp.sum(lines * scale, axis=1, keepdims=True).astype(jnp.int32)
    total[...] = jnp.zeros_like(total)
    for src in range(sources):
        moving = []
        for s in range(2):
            block = got[src, s * width : (s + 1) * width, :]
            moving.append(jnp.concatenate([block, block], axis=0))
        moving = jnp.concatenate(moving, axis=1)
        left = code[src, 0]
        digits = []
        for _ in range(2 * count):
            digits.append(left % blocks)
            left = left // blocks
        stacked = jnp.concatenate([two[b] for b in digits[:count]], axis=0)
        product = jnp.dot(stacked, moving, preferred_element_type=F32).astype(BF16).astype(F32)
        for t, p in enumerate(digits[count:]):
            total[t, src % 2, p] += product[t * rank : (t + 1) * rank]
    for s in range(2):
        sums = []
        lanes = slice(s * LANES, (s + 1) * LANES)
        for p in range(owners):
            low = (total[0, 0, p, :, lanes] + total[0, 1, p, :, lanes])[:, :half]
            high = total[1, 0, p, :, lanes] + total[1, 1, p, :, lanes]
            sums.append(low + pltpu.roll(high, half, 1)[:, :half])
        out[s * rank : (s + 1) * rank, :] = jnp.concatenate(sums, axis=1).astype(BF16)
    readers[...] = jnp.concatenate([one[p][:, :half] for p in range(owners)], axis=1).astype(BF16)


def known_kernel(mine, readers, out):
    out[...] = nt(readers[...], mine[...])


def rows_kernel(mine, theirs, readers, known, out):
    project = (known[...] + nt(readers[...], theirs[...])).astype(BF16)
    part = jnp.dot(project, mine[...], preferred_element_type=F32)
    part += jnp.dot(project, theirs[...], preferred_element_type=F32)
    out[...] = part.astype(BF16)


def final_kernel(places, a, b, c, d, factor, tile_factor, table):
    rank, rows_total = a.shape
    half = LANES // 2
    rows = (a[...].astype(F32) + b[...].astype(F32)) + (c[...].astype(F32) + d[...].astype(F32))
    table[...] = rows
    g0 = dot3(rows, rows, 1)
    eye = (row_iota(g0.shape) == lane_iota(g0.shape)).astype(F32)
    msq = jnp.sum(rows * rows, keepdims=True) / rows_total
    inv = 1.0 / jnp.sqrt(msq + 1e-06)
    g = g0 * (inv * inv) / rows_total
    square = dot3(g, g)
    outer = dot3(square, 0.0625 * square - 0.5625 * g)
    step = (outer + (1.6875 * square - 2.4375 * g + 2.25 * eye)) * inv

    def block(p):
        window = table[:, pl.ds(pl.multiple_of((p // 2) * LANES, LANES), LANES)]
        return jnp.where(p % 2 == 1, pltpu.roll(window, half, 1), window)[:, :half]

    place = places[...]
    picks = [lax.axis_index(("half", "rest"))] + [place[0, t] for t in range(tile_factor.shape[0])]
    picked = jnp.concatenate([block(p) for p in picks], axis=1)
    x = dot3(step, picked)
    factor[...] = x[:, :half]
    for t in range(tile_factor.shape[0]):
        value = x[:, (t + 1) * half : (t + 2) * half]
        for r in range(0, rank, 2):
            line = jnp.concatenate([value[r : r + 1], value[r + 1 : r + 2]], axis=1)
            tile_factor[t : t + 1, r * half : (r + 2) * half] = line.astype(BF16)


def swap(x, size, mask):
    return lax.ppermute(x, ("half", "rest", "rep"), [(i, i ^ mask) for i in range(size)])


def sliced(tiles, block_one, block_two, block_three, owner_map, u_one, u_two, u_three):
    count, width = tiles.shape[:2]
    rank = u_three.shape[0]
    owners = 2 * lax.axis_size("rest")
    reps = lax.axis_size("rep")
    size = owners * reps
    sources = size // 2
    rows_total = owner_map.shape[0] * width
    depth = 2 * width + META
    vmem = pl.BlockSpec(memory_space=pltpu.VMEM)
    narrow = pltpu.CompilerParams(vmem_limit_bytes=NARROW)
    core, x, y, near, far = 1, 2, 4, 8, 16
    ints = (block_one, block_two, block_three, owner_map)
    arrays = (tiles, u_three, u_two, u_one)
    sends, places, pack = pl.pallas_call(
        first_kernel,
        out_shape=(
            jax.ShapeDtypeStruct((sources, depth, LANES), BF16),
            jax.ShapeDtypeStruct((META // 2, LANES), jnp.int32),
            jax.ShapeDtypeStruct((rank + rank // 2, LANES), BF16),
        ),
        in_specs=[pl.BlockSpec(memory_space=pltpu.HBM)] * 8,
        out_specs=(vmem, vmem, vmem),
        scratch_shapes=[pltpu.SMEM(a.shape, a.dtype) for a in ints]
        + [pltpu.VMEM(a.shape, a.dtype) for a in arrays]
        + [
            pltpu.VMEM(u_two.shape, F32),
            pltpu.SemaphoreType.DMA((7,)),
            pltpu.SemaphoreType.DMA((count,)),
        ],
        compiler_params=narrow,
        name="first",
    )(*[pltpu.with_memory_space_constraint(a, pltpu.HBM) for a in ints + arrays])
    theirs = [swap(pack, size, far | core | k * y) for k in range(4)]
    got = lax.all_to_all(sends, ("rest", "rep"), 0, 0, tiled=True)
    table, readers = pl.pallas_call(
        functools.partial(table_kernel, reps),
        out_shape=(
            jax.ShapeDtypeStruct((2 * rank, rows_total), BF16),
            jax.ShapeDtypeStruct((rank, rows_total), BF16),
        ),
        in_specs=[vmem] * 5,
        out_specs=(vmem, vmem),
        scratch_shapes=[
            pltpu.VMEM((2 * owners, rank, LANES), BF16),
            pltpu.VMEM((owners, rank, LANES), F32),
            pltpu.VMEM((count, 2, owners, rank, 2 * LANES), F32),
        ],
        compiler_params=narrow,
        name="table",
    )(got, *theirs)
    known = pl.pallas_call(
        known_kernel,
        out_shape=jax.ShapeDtypeStruct((rank, 2 * rank), F32),
        in_specs=[vmem] * 2,
        out_specs=vmem,
        compiler_params=narrow,
        name="known",
    )(table, readers)
    part = pl.pallas_call(
        rows_kernel,
        out_shape=jax.ShapeDtypeStruct((rank, rows_total), BF16),
        in_specs=[vmem] * 4,
        out_specs=vmem,
        compiler_params=narrow,
        name="rows_part",
    )(table, swap(table, size, far | core), readers, known)
    part = (part.astype(F32) + swap(part, size, core).astype(F32)).astype(BF16)
    part = (part.astype(F32) + swap(part, size, x | core).astype(F32)).astype(BF16)
    rest = [swap(part, size, mask) for mask in (near | core, y | core, y ^ near)]
    return pl.pallas_call(
        final_kernel,
        out_shape=(
            jax.ShapeDtypeStruct(u_one.shape, F32),
            jax.ShapeDtypeStruct((count, rank * width), BF16),
        ),
        in_specs=[vmem] * 5,
        out_specs=(vmem, vmem),
        scratch_shapes=[pltpu.VMEM((rank, rows_total), F32)],
        compiler_params=narrow,
        name="final",
    )(places, part, *rest)


def fits(mesh, tiles, block_one, block_two, block_three, owner_map, u_one, u_two, u_three):
    owners, reps = mesh.shape["tiles"], mesh.shape["rep"]
    rank = u_three.shape[0]
    width = tiles.shape[1]
    return (
        owners == 8
        and reps == 4
        and rank == owners * reps == reps * META // 2
        and tiles.shape[0] == 2 * owners * reps
        and 2 * width == LANES
        and owner_map.shape[0] == owners
        and u_one.shape[1] == owners * width
        and u_two.shape[1] == owners * LANES
        and u_three.shape[1] % LANES == 0
    )


def specs(tiles, rep):
    both = tiles + rep
    ins = (P(both, None, None), P(both), P(both), P(both), P(), P(None, tiles), P(None, tiles), P())
    return ins, (P(None, tiles), P(both, None))


def solution(mesh):
    def run(*args):
        if fits(mesh, *args):
            axes = ("half", "rest", "rep")
            grid = mesh.devices.reshape(2, -1, mesh.shape["rep"])
            halves = jax.sharding.Mesh(grid, axes)
            ins, outs = specs(axes[:2], axes[2:])
            body, where = sliced, halves
        else:
            ins, outs = specs(("tiles",), ("rep",))
            body, where = general, mesh
        return jax.shard_map(body, mesh=where, in_specs=ins, out_specs=outs, check_vma=False)(*args)

    return run
```

```python
import functools

import jax
import jax.numpy as jnp
from jax import lax
from jax.experimental import pallas as pl
from jax.experimental.pallas import tpu as pltpu
from jax.sharding import PartitionSpec as P

NS_STEPS = 2
HI = lax.Precision.HIGHEST
LANES = 128
NARROW = 16 * 1024 * 1024
META = 16
F32 = jnp.float32
BF16 = jnp.bfloat16


def pick(table, index, width):
    grid = table.reshape(table.shape[0], -1, width)
    return jnp.transpose(jnp.take(grid, index, axis=1), (1, 0, 2))


def orthonormal(rows, rows_total):
    rank = rows.shape[0]
    g0 = jnp.dot(rows, rows.T, precision=HI, preferred_element_type=F32)
    msq = jnp.trace(g0) / rows_total
    inv = 1.0 / jnp.sqrt(msq + 1e-06)
    x = rows * inv
    g = g0 * (inv * inv) / rows_total
    eye = jnp.eye(rank, dtype=F32)
    for step in range(NS_STEPS):
        if step > 0:
            g = jnp.dot(x, x.T, precision=HI, preferred_element_type=F32) / rows_total
        x = jnp.dot(1.5 * eye - 0.5 * g, x, precision=HI, preferred_element_type=F32)
    return x


def general(tiles, block_one, block_two, block_three, owner_map, u_one, u_two, u_three):
    count, width = tiles.shape[:2]
    rank = u_three.shape[0]
    blocks_total = owner_map.shape[0]
    rows_total = blocks_total * width
    two_full = lax.all_gather(u_two, "tiles", axis=1, tiled=True)
    two_pick = pick(two_full, block_two, width)
    three_pick = pick(u_three, block_three, width)
    cube = tiles.reshape(count, width, width, width)
    first = jnp.einsum("tijk,tsk->tijs", cube, three_pick, preferred_element_type=F32).astype(BF16)
    second = jnp.einsum("tijs,trj->tirs", first, two_pick, preferred_element_type=F32)
    products = second.reshape(count, width, rank * rank).astype(BF16)
    positions = jnp.take(owner_map, block_one)
    onehot = (positions[:, None] == jnp.arange(blocks_total, dtype=jnp.int32)[None, :]).astype(F32)
    current = lax.all_gather(u_one.astype(BF16), "tiles", axis=1, tiled=True)
    readers = pick(current, positions, width)
    partial_value = jnp.einsum("tic,tri->rc", products, readers, preferred_element_type=F32)
    project = lax.psum(partial_value, ("tiles", "rep")).astype(BF16)
    z_tile = jnp.einsum("rc,tic->tri", project, products, preferred_element_type=F32)
    term = jnp.einsum("tri,tn->rni", z_tile, onehot, precision=HI).reshape(rank, rows_total)
    rows = lax.psum(term, ("tiles", "rep"))
    current = orthonormal(rows, rows_total)
    tile_factor = pick(current.astype(BF16), positions, width).reshape(count, rank * width)
    own = u_one.shape[1]
    factor = lax.dynamic_slice_in_dim(current, lax.axis_index("tiles") * own, own, 1)
    return (factor, tile_factor)


def split(a):
    high = a.astype(BF16)
    return high, (a - high.astype(F32)).astype(BF16)


def dot3(a, b, axis=0):
    (ah, al), (bh, bl) = split(a), split(b)
    dims = (((1,), (axis,)), ((), ()))
    parts = [lax.dot_general(p, q, dims, preferred_element_type=F32) for p, q in ((ah, bh), (ah, bl), (al, bh))]
    return parts[0] + (parts[1] + parts[2])


def lane_iota(shape):
    return lax.broadcasted_iota(jnp.int32, shape, len(shape) - 1)


def row_iota(shape):
    return lax.broadcasted_iota(jnp.int32, shape, len(shape) - 2)


def nt(a, b, precision=None):
    return lax.dot_general(
        a, b, (((1,), (1,)), ((), ())), precision=precision, preferred_element_type=F32
    )


def first_kernel(
    one_hbm, two_hbm, three_hbm, owner_hbm, tiles_hbm, u_three_hbm, u_two_hbm, u_one_hbm, out_hbm, places, pack,
    one, two, three, owner, tiles, u_three, u_two, u_one, two_f32, out, in_sems, tile_sems, out_sems,
):
    side = lax.axis_index("half")
    count, width = tiles.shape[:2]
    rank = u_three.shape[0]
    half = LANES // 2
    share = META // 2
    span = share * width
    pieces = tiles.shape[2] // (2 * span)
    moves = [(three_hbm, three), (u_three_hbm, u_three), (two_hbm, two), (one_hbm, one)]
    moves += [(owner_hbm, owner), (u_two_hbm, u_two), (u_one_hbm, u_one)]
    copies = [pltpu.make_async_copy(a, b, in_sems.at[i]) for i, (a, b) in enumerate(moves)]
    loads = [
        pltpu.make_async_copy(tiles_hbm.at[t], tiles.at[t], tile_sems.at[t]) for t in range(count)
    ]
    for copy in copies + loads:
        copy.start()
    copies[0].wait()
    copies[1].wait()
    weights = []
    for t in range(count):
        block = three[t]
        start = pl.multiple_of((block // 2) * LANES, LANES)
        window = u_three[:, pl.ds(start, LANES)].astype(F32)
        same = (lane_iota(window.shape) // half) == (block % 2)
        both = jnp.where(same, window, pltpu.roll(window, half, 1))
        tall = jnp.broadcast_to(both[:, None, :], (rank, share, LANES)).reshape(rank * share, LANES)
        full = jnp.concatenate([tall] * (span // LANES), axis=1)
        keep = (row_iota(full.shape) % share) == (lane_iota(full.shape) // width)
        weights.append(jnp.where(keep, full, 0.0).astype(BF16))
    for copy in copies[2:]:
        copy.wait()
    q = lax.axis_index("rep")
    pack[:rank, :] = u_two[...]
    pair = [u_one[: rank // 2, :], u_one[rank // 2 :, :]]
    pack[rank:, :] = jnp.concatenate(pair, axis=1).astype(BF16)
    two_f32[...] = u_two[...].astype(F32)
    top = two_f32[pl.ds(pl.multiple_of(q * share, share), share), :]
    low = u_one[pl.ds(pl.multiple_of(q * share, share), share), :]
    lane = lane_iota((share, half))
    ints = jnp.zeros((share, half), F32)
    spot = lane_iota(places.shape)
    place = jnp.zeros(places.shape, jnp.int32)
    for t in range(count):
        position = owner[one[t]]
        ints = jnp.where(lane == t, two[t].astype(F32), ints)
        ints = jnp.where(lane == count + t, position.astype(F32), ints)
        place = jnp.where(spot == t, position, place)
    places[...] = place
    meta = jnp.concatenate([top, jnp.concatenate([low, ints], axis=1)], axis=0).astype(BF16)
    rows = slice(2 * width, 2 * width + META)
    for k in range(out.shape[0]):
        out[k, rows, :] = meta
    stores = []

    def send(rows):
        copy = pltpu.make_async_copy(
            out.at[:, rows, :], out_hbm.at[:, rows, :], out_sems.at[len(stores)]
        )
        copy.start()
        stores.append(copy)

    send(rows)
    for copy in loads:
        copy.wait()
    for n in range(pieces // 2):
        wide = []
        for t in range(count):
            groups = [tiles[t, :, (4 * n + g) * span : (4 * n + g + 1) * span] for g in range(4)]
            wide.append(nt(weights[t], jnp.concatenate(groups, axis=0)))
        for s in range(rank):
            at = slice(s * share, (s + 1) * share)
            for h in range(2):
                block = []
                for g in (2 * h, 2 * h + 1):
                    lanes = slice(g * width, (g + 1) * width)
                    block.append(jnp.concatenate([part[at, lanes] for part in wide], axis=1))
                start = n * width + (s % 2) * (width // 2) + h * META
                rows = slice(start, start + META)
                out[(s // 2) ^ side, rows, :] = jnp.concatenate(block, axis=0).astype(BF16)
        send(slice(n * width, (n + 1) * width))
    for copy in stores:
        copy.wait()


def table_kernel(reps, got, far0, far1, far2, far3, out, readers, two, one, total):
    sources, depth = got.shape[:2]
    half = LANES // 2
    share = META // 2
    width = (depth - META) // 2
    rank = share * reps
    count = LANES // width
    owners = 2 * sources // reps
    blocks = 2 * owners
    side = lax.axis_index("half")
    lines = []
    halves = lane_iota((META, LANES)) // half
    for src in range(0, sources, 2):
        t, q = divmod(src, reps)
        rows = slice(q * share, (q + 2) * share)
        pair = [got[src + k, 2 * width : 2 * width + META, :].astype(F32) for k in range(2)]
        mine = jnp.concatenate([meta[:share] for meta in pair], axis=0)
        shard = side * (owners // 2) + t
        for k in range(2):
            two[2 * shard + k, rows, :] = jnp.where(halves == k, mine, 0.0).astype(BF16)
        one[shard, rows, :] = jnp.concatenate([meta[share:] for meta in pair], axis=0)
        lines += [meta[share : share + 1] for meta in pair]
    halves = lane_iota((rank, LANES)) // half
    for k, ref in enumerate((far0, far1, far2, far3)):
        shard = (1 - side) * (owners // 2) + (lax.axis_index("rest") ^ k)
        theirs = ref[:rank, :].astype(F32)
        for k in range(2):
            two[2 * shard + k] = jnp.where(halves == k, theirs, 0.0).astype(BF16)
        theirs = ref[rank:, :].astype(F32)
        one[shard, : rank // 2, :] = theirs
        one[shard, rank // 2 :, :] = pltpu.roll(theirs, half, 1)
    lines = jnp.concatenate(lines, axis=0)
    lane = lane_iota(lines.shape)
    scale = jnp.zeros(lines.shape, F32)
    for k in range(2 * count):
        scale = jnp.where(lane == half + k, float(blocks**k), scale)
    code = jnp.sum(lines * scale, axis=1, keepdims=True).astype(jnp.int32)
    total[...] = jnp.zeros_like(total)
    for src in range(sources):
        moving = []
        for s in range(2):
            lines = [got[src, at : at + width // 2, :] for at in (s * width // 2, (s + 2) * width // 2)]
            moving.append(jnp.concatenate(lines + lines, axis=0))
        moving = jnp.concatenate(moving, axis=1)
        left = code[src, 0]
        digits = []
        for _ in range(2 * count):
            digits.append(left % blocks)
            left = left // blocks
        stacked = jnp.concatenate([two[b] for b in digits[:count]], axis=0)
        product = jnp.dot(stacked, moving, preferred_element_type=F32).astype(BF16).astype(F32)
        for t, p in enumerate(digits[count:]):
            total[t, src % 2, p] += product[t * rank : (t + 1) * rank]
    for s in range(2):
        sums = []
        lanes = slice(s * LANES, (s + 1) * LANES)
        for p in range(owners):
            low = (total[0, 0, p, :, lanes] + total[0, 1, p, :, lanes])[:, :half]
            high = total[1, 0, p, :, lanes] + total[1, 1, p, :, lanes]
            sums.append(low + pltpu.roll(high, half, 1)[:, :half])
        out[s * rank : (s + 1) * rank, :] = jnp.concatenate(sums, axis=1).astype(BF16)
    readers[...] = jnp.concatenate([one[p][:, :half] for p in range(owners)], axis=1).astype(BF16)


def known_kernel(mine, readers, out):
    out[...] = nt(readers[...], mine[...])


def rows_kernel(mine, theirs, readers, known, out):
    project = (known[...] + nt(readers[...], theirs[...])).astype(BF16)
    part = jnp.dot(project, mine[...], preferred_element_type=F32)
    part += jnp.dot(project, theirs[...], preferred_element_type=F32)
    out[...] = part.astype(BF16)


def final_kernel(places, a, b, c, d, factor, tile_factor, table):
    rank, rows_total = a.shape
    half = LANES // 2
    rows = (a[...].astype(F32) + b[...].astype(F32)) + (c[...].astype(F32) + d[...].astype(F32))
    table[...] = rows
    g0 = dot3(rows, rows, 1)
    eye = (row_iota(g0.shape) == lane_iota(g0.shape)).astype(F32)
    msq = jnp.sum(rows * rows, keepdims=True) / rows_total
    inv = 1.0 / jnp.sqrt(msq + 1e-06)
    g = g0 * (inv * inv) / rows_total
    square = dot3(g, g)
    outer = dot3(square, 0.0625 * square - 0.5625 * g)
    step = (outer + (1.6875 * square - 2.4375 * g + 2.25 * eye)) * inv

    def block(p):
        window = table[:, pl.ds(pl.multiple_of((p // 2) * LANES, LANES), LANES)]
        return jnp.where(p % 2 == 1, pltpu.roll(window, half, 1), window)[:, :half]

    place = places[...]
    picks = [lax.axis_index(("half", "rest"))] + [place[0, t] for t in range(tile_factor.shape[0])]
    picked = jnp.concatenate([block(p) for p in picks], axis=1)
    x = dot3(step, picked)
    factor[...] = x[:, :half]
    for t in range(tile_factor.shape[0]):
        value = x[:, (t + 1) * half : (t + 2) * half]
        for r in range(0, rank, 2):
            line = jnp.concatenate([value[r : r + 1], value[r + 1 : r + 2]], axis=1)
            tile_factor[t : t + 1, r * half : (r + 2) * half] = line.astype(BF16)


def swap(x, size, mask):
    return lax.ppermute(x, ("half", "rest", "rep"), [(i, i ^ mask) for i in range(size)])


def sliced(tiles, block_one, block_two, block_three, owner_map, u_one, u_two, u_three):
    count, width = tiles.shape[:2]
    rank = u_three.shape[0]
    owners = 2 * lax.axis_size("rest")
    reps = lax.axis_size("rep")
    size = owners * reps
    sources = size // 2
    rows_total = owner_map.shape[0] * width
    depth = 2 * width + META
    vmem = pl.BlockSpec(memory_space=pltpu.VMEM)
    narrow = pltpu.CompilerParams(vmem_limit_bytes=NARROW)
    core, x, y, near, far = 1, 2, 4, 8, 16
    ints = (block_one, block_two, block_three, owner_map)
    arrays = (tiles, u_three, u_two, u_one)
    sends, places, pack = pl.pallas_call(
        first_kernel,
        out_shape=(
            jax.ShapeDtypeStruct((sources, depth, LANES), BF16),
            jax.ShapeDtypeStruct((META // 2, LANES), jnp.int32),
            jax.ShapeDtypeStruct((rank + rank // 2, LANES), BF16),
        ),
        in_specs=[pl.BlockSpec(memory_space=pltpu.HBM)] * 8,
        out_specs=(pl.BlockSpec(memory_space=pltpu.HBM), vmem, vmem),
        scratch_shapes=[pltpu.SMEM(a.shape, a.dtype) for a in ints]
        + [pltpu.VMEM(a.shape, a.dtype) for a in arrays]
        + [
            pltpu.VMEM(u_two.shape, F32),
            pltpu.VMEM((sources, depth, LANES), BF16),
            pltpu.SemaphoreType.DMA((7,)),
            pltpu.SemaphoreType.DMA((count,)),
            pltpu.SemaphoreType.DMA((3,)),
        ],
        compiler_params=narrow,
        name="first",
    )(*[pltpu.with_memory_space_constraint(a, pltpu.HBM) for a in ints + arrays])
    theirs = [swap(pack, size, far | core | k * y) for k in (3, 2, 1, 0)][::-1]
    got = lax.all_to_all(sends, ("rest", "rep"), 0, 0, tiled=True)
    table, readers = pl.pallas_call(
        functools.partial(table_kernel, reps),
        out_shape=(
            jax.ShapeDtypeStruct((2 * rank, rows_total), BF16),
            jax.ShapeDtypeStruct((rank, rows_total), BF16),
        ),
        in_specs=[vmem] * 5,
        out_specs=(vmem, vmem),
        scratch_shapes=[
            pltpu.VMEM((2 * owners, rank, LANES), BF16),
            pltpu.VMEM((owners, rank, LANES), F32),
            pltpu.VMEM((count, 2, owners, rank, 2 * LANES), F32),
        ],
        compiler_params=narrow,
        name="table",
    )(got, *theirs)
    known = pl.pallas_call(
        known_kernel,
        out_shape=jax.ShapeDtypeStruct((rank, 2 * rank), F32),
        in_specs=[vmem] * 2,
        out_specs=vmem,
        compiler_params=narrow,
        name="known",
    )(table, readers)
    part = pl.pallas_call(
        rows_kernel,
        out_shape=jax.ShapeDtypeStruct((rank, rows_total), BF16),
        in_specs=[vmem] * 4,
        out_specs=vmem,
        compiler_params=narrow,
        name="rows_part",
    )(table, swap(table, size, far | core), readers, known)
    part = (part.astype(F32) + swap(part, size, core).astype(F32)).astype(BF16)
    part = (part.astype(F32) + swap(part, size, x | core).astype(F32)).astype(BF16)
    rest = [swap(part, size, mask) for mask in (near | core, y | core, y ^ near)]
    return pl.pallas_call(
        final_kernel,
        out_shape=(
            jax.ShapeDtypeStruct(u_one.shape, F32),
            jax.ShapeDtypeStruct((count, rank * width), BF16),
        ),
        in_specs=[vmem] * 5,
        out_specs=(vmem, vmem),
        scratch_shapes=[pltpu.VMEM((rank, rows_total), F32)],
        compiler_params=narrow,
        name="final",
    )(places, part, *rest)


def fits(mesh, tiles, block_one, block_two, block_three, owner_map, u_one, u_two, u_three):
    owners, reps = mesh.shape["tiles"], mesh.shape["rep"]
    rank = u_three.shape[0]
    width = tiles.shape[1]
    return (
        owners == 8
        and reps == 4
        and rank == owners * reps == reps * META // 2
        and tiles.shape[0] == 2 * owners * reps
        and 2 * width == LANES
        and owner_map.shape[0] == owners
        and u_one.shape[1] == owners * width
        and u_two.shape[1] == owners * LANES
        and u_three.shape[1] % LANES == 0
    )


def specs(tiles, rep):
    both = tiles + rep
    ins = (P(both, None, None), P(both), P(both), P(both), P(), P(None, tiles), P(None, tiles), P())
    return ins, (P(None, tiles), P(both, None))


def solution(mesh):
    def run(*args):
        if fits(mesh, *args):
            axes = ("half", "rest", "rep")
            grid = mesh.devices.reshape(2, -1, mesh.shape["rep"])
            halves = jax.sharding.Mesh(grid, axes)
            ins, outs = specs(axes[:2], axes[2:])
            body, where = sliced, halves
        else:
            ins, outs = specs(("tiles",), ("rep",))
            body, where = general, mesh
        return jax.shard_map(body, mesh=where, in_specs=ins, out_specs=outs, check_vma=False)(*args)

    return run
```

```python
import functools

import jax
import jax.numpy as jnp
from jax import lax
from jax.experimental import pallas as pl
from jax.experimental.pallas import tpu as pltpu
from jax.sharding import PartitionSpec as P

NS_STEPS = 2
HI = lax.Precision.HIGHEST
LANES = 128
NARROW = 16 * 1024 * 1024
META = 16
F32 = jnp.float32
BF16 = jnp.bfloat16


def pick(table, index, width):
    grid = table.reshape(table.shape[0], -1, width)
    return jnp.transpose(jnp.take(grid, index, axis=1), (1, 0, 2))


def orthonormal(rows, rows_total):
    rank = rows.shape[0]
    g0 = jnp.dot(rows, rows.T, precision=HI, preferred_element_type=F32)
    msq = jnp.trace(g0) / rows_total
    inv = 1.0 / jnp.sqrt(msq + 1e-06)
    x = rows * inv
    g = g0 * (inv * inv) / rows_total
    eye = jnp.eye(rank, dtype=F32)
    for step in range(NS_STEPS):
        if step > 0:
            g = jnp.dot(x, x.T, precision=HI, preferred_element_type=F32) / rows_total
        x = jnp.dot(1.5 * eye - 0.5 * g, x, precision=HI, preferred_element_type=F32)
    return x


def general(tiles, block_one, block_two, block_three, owner_map, u_one, u_two, u_three):
    count, width = tiles.shape[:2]
    rank = u_three.shape[0]
    blocks_total = owner_map.shape[0]
    rows_total = blocks_total * width
    two_full = lax.all_gather(u_two, "tiles", axis=1, tiled=True)
    two_pick = pick(two_full, block_two, width)
    three_pick = pick(u_three, block_three, width)
    cube = tiles.reshape(count, width, width, width)
    first = jnp.einsum("tijk,tsk->tijs", cube, three_pick, preferred_element_type=F32).astype(BF16)
    second = jnp.einsum("tijs,trj->tirs", first, two_pick, preferred_element_type=F32)
    products = second.reshape(count, width, rank * rank).astype(BF16)
    positions = jnp.take(owner_map, block_one)
    onehot = (positions[:, None] == jnp.arange(blocks_total, dtype=jnp.int32)[None, :]).astype(F32)
    current = lax.all_gather(u_one.astype(BF16), "tiles", axis=1, tiled=True)
    readers = pick(current, positions, width)
    partial_value = jnp.einsum("tic,tri->rc", products, readers, preferred_element_type=F32)
    project = lax.psum(partial_value, ("tiles", "rep")).astype(BF16)
    z_tile = jnp.einsum("rc,tic->tri", project, products, preferred_element_type=F32)
    term = jnp.einsum("tri,tn->rni", z_tile, onehot, precision=HI).reshape(rank, rows_total)
    rows = lax.psum(term, ("tiles", "rep"))
    current = orthonormal(rows, rows_total)
    tile_factor = pick(current.astype(BF16), positions, width).reshape(count, rank * width)
    own = u_one.shape[1]
    factor = lax.dynamic_slice_in_dim(current, lax.axis_index("tiles") * own, own, 1)
    return (factor, tile_factor)


def split(a):
    high = a.astype(BF16)
    return high, (a - high.astype(F32)).astype(BF16)


def dot3(a, b, axis=0):
    (ah, al), (bh, bl) = split(a), split(b)
    dims = (((1,), (axis,)), ((), ()))
    parts = [lax.dot_general(p, q, dims, preferred_element_type=F32) for p, q in ((ah, bh), (ah, bl), (al, bh))]
    return parts[0] + (parts[1] + parts[2])


def lane_iota(shape):
    return lax.broadcasted_iota(jnp.int32, shape, len(shape) - 1)


def row_iota(shape):
    return lax.broadcasted_iota(jnp.int32, shape, len(shape) - 2)


def nt(a, b, precision=None):
    return lax.dot_general(
        a, b, (((1,), (1,)), ((), ())), precision=precision, preferred_element_type=F32
    )


def first_kernel(
    one_hbm, two_hbm, three_hbm, owner_hbm, tiles_hbm, u_three_hbm, u_two_hbm, u_one_hbm, out_hbm, places, pack,
    one, two, three, owner, tiles, u_three, u_two, u_one, two_f32, out, in_sems, tile_sems, out_sems,
):
    side = lax.axis_index("half")
    count, width = tiles.shape[:2]
    rank = u_three.shape[0]
    half = LANES // 2
    share = META // 2
    span = share * width
    pieces = tiles.shape[2] // (2 * span)
    moves = [(three_hbm, three), (u_three_hbm, u_three), (two_hbm, two), (one_hbm, one)]
    moves += [(owner_hbm, owner), (u_two_hbm, u_two), (u_one_hbm, u_one)]
    copies = [pltpu.make_async_copy(a, b, in_sems.at[i]) for i, (a, b) in enumerate(moves)]
    loads = [
        pltpu.make_async_copy(tiles_hbm.at[t], tiles.at[t], tile_sems.at[t]) for t in range(count)
    ]
    for copy in copies + loads:
        copy.start()
    copies[0].wait()
    copies[1].wait()
    weights = []
    for t in range(count):
        block = three[t]
        start = pl.multiple_of((block // 2) * LANES, LANES)
        window = u_three[:, pl.ds(start, LANES)].astype(F32)
        same = (lane_iota(window.shape) // half) == (block % 2)
        both = jnp.where(same, window, pltpu.roll(window, half, 1))
        tall = jnp.broadcast_to(both[:, None, :], (rank, share, LANES)).reshape(rank * share, LANES)
        full = jnp.concatenate([tall] * (span // LANES), axis=1)
        keep = (row_iota(full.shape) % share) == (lane_iota(full.shape) // width)
        weights.append(jnp.where(keep, full, 0.0).astype(BF16))
    for copy in copies[2:]:
        copy.wait()
    q = lax.axis_index("rep")
    pack[:rank, :] = u_two[...]
    pair = [u_one[: rank // 2, :], u_one[rank // 2 :, :]]
    pack[rank:, :] = jnp.concatenate(pair, axis=1).astype(BF16)
    two_f32[...] = u_two[...].astype(F32)
    top = two_f32[pl.ds(pl.multiple_of(q * share, share), share), :]
    low = u_one[pl.ds(pl.multiple_of(q * share, share), share), :]
    lane = lane_iota((share, half))
    ints = jnp.zeros((share, half), F32)
    spot = lane_iota(places.shape)
    place = jnp.zeros(places.shape, jnp.int32)
    for t in range(count):
        position = owner[one[t]]
        ints = jnp.where(lane == t, two[t].astype(F32), ints)
        ints = jnp.where(lane == count + t, position.astype(F32), ints)
        place = jnp.where(spot == t, position, place)
    places[...] = place
    meta = jnp.concatenate([top, jnp.concatenate([low, ints], axis=1)], axis=0).astype(BF16)
    rows = slice(2 * width, 2 * width + META)
    for k in range(out.shape[0]):
        out[k, rows, :] = meta
    stores = []

    def send(rows):
        copy = pltpu.make_async_copy(
            out.at[:, rows, :], out_hbm.at[:, rows, :], out_sems.at[len(stores)]
        )
        copy.start()
        stores.append(copy)

    send(rows)
    for copy in loads:
        copy.wait()
    for n in range(pieces // 2):
        wide = []
        for t in range(count):
            groups = [tiles[t, :, (4 * n + g) * span : (4 * n + g + 1) * span] for g in range(4)]
            wide.append(nt(weights[t], jnp.concatenate(groups, axis=0)))
        for s in range(rank):
            at = slice(s * share, (s + 1) * share)
            for h in range(2):
                block = []
                for g in (2 * h, 2 * h + 1):
                    lanes = slice(g * width, (g + 1) * width)
                    block.append(jnp.concatenate([part[at, lanes] for part in wide], axis=1))
                start = n * width + (s % 2) * (width // 2) + h * META
                rows = slice(start, start + META)
                out[(s // 2) ^ side, rows, :] = jnp.concatenate(block, axis=0).astype(BF16)
        send(slice(n * width, (n + 1) * width))
    for copy in stores:
        copy.wait()


def table_kernel(reps, got, far0, far1, far2, far3, out, readers, two, one, total):
    sources, depth = got.shape[:2]
    half = LANES // 2
    share = META // 2
    width = (depth - META) // 2
    rank = share * reps
    count = LANES // width
    owners = 2 * sources // reps
    blocks = 2 * owners
    side = lax.axis_index("half")
    lines = []
    halves = lane_iota((META, LANES)) // half
    for src in range(0, sources, 2):
        t, q = divmod(src, reps)
        rows = slice(q * share, (q + 2) * share)
        pair = [got[src + k, 2 * width : 2 * width + META, :].astype(F32) for k in range(2)]
        mine = jnp.concatenate([meta[:share] for meta in pair], axis=0)
        shard = side * (owners // 2) + t
        for k in range(2):
            two[2 * shard + k, rows, :] = jnp.where(halves == k, mine, 0.0).astype(BF16)
        one[shard, rows, :] = jnp.concatenate([meta[share:] for meta in pair], axis=0)
        lines += [meta[share : share + 1] for meta in pair]
    halves = lane_iota((rank, LANES)) // half
    for k, ref in enumerate((far0, far1, far2, far3)):
        shard = (1 - side) * (owners // 2) + (lax.axis_index("rest") ^ k)
        theirs = ref[:rank, :].astype(F32)
        for k in range(2):
            two[2 * shard + k] = jnp.where(halves == k, theirs, 0.0).astype(BF16)
        theirs = ref[rank:, :].astype(F32)
        one[shard, : rank // 2, :] = theirs
        one[shard, rank // 2 :, :] = pltpu.roll(theirs, half, 1)
    lines = jnp.concatenate(lines, axis=0)
    lane = lane_iota(lines.shape)
    scale = jnp.zeros(lines.shape, F32)
    for k in range(2 * count):
        scale = jnp.where(lane == half + k, float(blocks**k), scale)
    code = jnp.sum(lines * scale, axis=1, keepdims=True).astype(jnp.int32)
    total[...] = jnp.zeros_like(total)
    for src in range(sources):
        moving = []
        for s in range(2):
            lines = [got[src, at : at + width // 2, :] for at in (s * width // 2, (s + 2) * width // 2)]
            moving.append(jnp.concatenate(lines + lines, axis=0))
        moving = jnp.concatenate(moving, axis=1)
        left = code[src, 0]
        digits = []
        for _ in range(2 * count):
            digits.append(left % blocks)
            left = left // blocks
        stacked = jnp.concatenate([two[b] for b in digits[:count]], axis=0)
        product = jnp.dot(stacked, moving, preferred_element_type=F32)
        for t, p in enumerate(digits[count:]):
            total[t, p] += product[t * rank : (t + 1) * rank]
    for s in range(2):
        sums = []
        lanes = slice(s * LANES, (s + 1) * LANES)
        for p in range(owners):
            low = total[0, p, :, lanes][:, :half]
            high = total[1, p, :, lanes]
            sums.append(low + pltpu.roll(high, half, 1)[:, :half])
        out[s * rank : (s + 1) * rank, :] = jnp.concatenate(sums, axis=1).astype(BF16)
    readers[...] = jnp.concatenate([one[p][:, :half] for p in range(owners)], axis=1).astype(BF16)


def known_kernel(mine, readers, out):
    out[...] = nt(readers[...], mine[...])


def rows_kernel(mine, theirs, readers, known, out):
    project = (known[...] + nt(readers[...], theirs[...])).astype(BF16)
    part = jnp.dot(project, mine[...], preferred_element_type=F32)
    part += jnp.dot(project, theirs[...], preferred_element_type=F32)
    out[...] = part.astype(BF16)


def final_kernel(places, a, b, c, d, factor, tile_factor, table):
    rank, rows_total = a.shape
    half = LANES // 2
    rows = (a[...].astype(F32) + b[...].astype(F32)) + (c[...].astype(F32) + d[...].astype(F32))
    table[...] = rows
    g0 = dot3(rows, rows, 1)
    eye = (row_iota(g0.shape) == lane_iota(g0.shape)).astype(F32)
    msq = jnp.sum(rows * rows, keepdims=True) / rows_total
    inv = 1.0 / jnp.sqrt(msq + 1e-06)
    g = g0 * (inv * inv) / rows_total
    square = dot3(g, g)
    outer = dot3(square, 0.0625 * square - 0.5625 * g)
    step = (outer + (1.6875 * square - 2.4375 * g + 2.25 * eye)) * inv

    def block(p):
        window = table[:, pl.ds(pl.multiple_of((p // 2) * LANES, LANES), LANES)]
        return jnp.where(p % 2 == 1, pltpu.roll(window, half, 1), window)[:, :half]

    place = places[...]
    picks = [lax.axis_index(("half", "rest"))] + [place[0, t] for t in range(tile_factor.shape[0])]
    picked = jnp.concatenate([block(p) for p in picks], axis=1)
    x = dot3(step, picked)
    factor[...] = x[:, :half]
    for t in range(tile_factor.shape[0]):
        value = x[:, (t + 1) * half : (t + 2) * half]
        for r in range(0, rank, 2):
            line = jnp.concatenate([value[r : r + 1], value[r + 1 : r + 2]], axis=1)
            tile_factor[t : t + 1, r * half : (r + 2) * half] = line.astype(BF16)


def swap(x, size, mask):
    return lax.ppermute(x, ("half", "rest", "rep"), [(i, i ^ mask) for i in range(size)])


def sliced(tiles, block_one, block_two, block_three, owner_map, u_one, u_two, u_three):
    count, width = tiles.shape[:2]
    rank = u_three.shape[0]
    owners = 2 * lax.axis_size("rest")
    reps = lax.axis_size("rep")
    size = owners * reps
    sources = size // 2
    rows_total = owner_map.shape[0] * width
    depth = 2 * width + META
    vmem = pl.BlockSpec(memory_space=pltpu.VMEM)
    narrow = pltpu.CompilerParams(vmem_limit_bytes=NARROW)
    core, x, y, near, far = 1, 2, 4, 8, 16
    ints = (block_one, block_two, block_three, owner_map)
    arrays = (tiles, u_three, u_two, u_one)
    sends, places, pack = pl.pallas_call(
        first_kernel,
        out_shape=(
            jax.ShapeDtypeStruct((sources, depth, LANES), BF16),
            jax.ShapeDtypeStruct((META // 2, LANES), jnp.int32),
            jax.ShapeDtypeStruct((rank + rank // 2, LANES), BF16),
        ),
        in_specs=[pl.BlockSpec(memory_space=pltpu.HBM)] * 8,
        out_specs=(pl.BlockSpec(memory_space=pltpu.HBM), vmem, vmem),
        scratch_shapes=[pltpu.SMEM(a.shape, a.dtype) for a in ints]
        + [pltpu.VMEM(a.shape, a.dtype) for a in arrays]
        + [
            pltpu.VMEM(u_two.shape, F32),
            pltpu.VMEM((sources, depth, LANES), BF16),
            pltpu.SemaphoreType.DMA((7,)),
            pltpu.SemaphoreType.DMA((count,)),
            pltpu.SemaphoreType.DMA((3,)),
        ],
        compiler_params=narrow,
        name="first",
    )(*[pltpu.with_memory_space_constraint(a, pltpu.HBM) for a in ints + arrays])
    theirs = [swap(pack, size, far | core | k * y) for k in (3, 2, 1, 0)][::-1]
    got = lax.all_to_all(sends, ("rest", "rep"), 0, 0, tiled=True)
    table, readers = pl.pallas_call(
        functools.partial(table_kernel, reps),
        out_shape=(
            jax.ShapeDtypeStruct((2 * rank, rows_total), BF16),
            jax.ShapeDtypeStruct((rank, rows_total), BF16),
        ),
        in_specs=[vmem] * 5,
        out_specs=(vmem, vmem),
        scratch_shapes=[
            pltpu.VMEM((2 * owners, rank, LANES), BF16),
            pltpu.VMEM((owners, rank, LANES), F32),
            pltpu.VMEM((count, owners, rank, 2 * LANES), F32),
        ],
        compiler_params=narrow,
        name="table",
    )(got, *theirs)
    known = pl.pallas_call(
        known_kernel,
        out_shape=jax.ShapeDtypeStruct((rank, 2 * rank), F32),
        in_specs=[vmem] * 2,
        out_specs=vmem,
        compiler_params=narrow,
        name="known",
    )(table, readers)
    part = pl.pallas_call(
        rows_kernel,
        out_shape=jax.ShapeDtypeStruct((rank, rows_total), BF16),
        in_specs=[vmem] * 4,
        out_specs=vmem,
        compiler_params=narrow,
        name="rows_part",
    )(table, swap(table, size, far | core), readers, known)
    part = (part.astype(F32) + swap(part, size, core).astype(F32)).astype(BF16)
    part = (part.astype(F32) + swap(part, size, x | core).astype(F32)).astype(BF16)
    rest = [swap(part, size, mask) for mask in (near | core, y | core, y ^ near)]
    return pl.pallas_call(
        final_kernel,
        out_shape=(
            jax.ShapeDtypeStruct(u_one.shape, F32),
            jax.ShapeDtypeStruct((count, rank * width), BF16),
        ),
        in_specs=[vmem] * 5,
        out_specs=(vmem, vmem),
        scratch_shapes=[pltpu.VMEM((rank, rows_total), F32)],
        compiler_params=narrow,
        name="final",
    )(places, part, *rest)


def fits(mesh, tiles, block_one, block_two, block_three, owner_map, u_one, u_two, u_three):
    owners, reps = mesh.shape["tiles"], mesh.shape["rep"]
    rank = u_three.shape[0]
    width = tiles.shape[1]
    return (
        owners == 8
        and reps == 4
        and rank == owners * reps == reps * META // 2
        and tiles.shape[0] == 2 * owners * reps
        and 2 * width == LANES
        and owner_map.shape[0] == owners
        and u_one.shape[1] == owners * width
        and u_two.shape[1] == owners * LANES
        and u_three.shape[1] % LANES == 0
    )


def specs(tiles, rep):
    both = tiles + rep
    ins = (P(both, None, None), P(both), P(both), P(both), P(), P(None, tiles), P(None, tiles), P())
    return ins, (P(None, tiles), P(both, None))


def solution(mesh):
    def run(*args):
        if fits(mesh, *args):
            axes = ("half", "rest", "rep")
            grid = mesh.devices.reshape(2, -1, mesh.shape["rep"])
            halves = jax.sharding.Mesh(grid, axes)
            ins, outs = specs(axes[:2], axes[2:])
            body, where = sliced, halves
        else:
            ins, outs = specs(("tiles",), ("rep",))
            body, where = general, mesh
        return jax.shard_map(body, mesh=where, in_specs=ins, out_specs=outs, check_vma=False)(*args)

    return run
```

```python
import functools

import jax
import jax.numpy as jnp
from jax import lax
from jax.experimental import pallas as pl
from jax.experimental.pallas import tpu as pltpu
from jax.sharding import PartitionSpec as P

NS_STEPS = 2
HI = lax.Precision.HIGHEST
LANES = 128
NARROW = 16 * 1024 * 1024
META = 16
F32 = jnp.float32
BF16 = jnp.bfloat16


def pick(table, index, width):
    grid = table.reshape(table.shape[0], -1, width)
    return jnp.transpose(jnp.take(grid, index, axis=1), (1, 0, 2))


def orthonormal(rows, rows_total):
    rank = rows.shape[0]
    g0 = jnp.dot(rows, rows.T, precision=HI, preferred_element_type=F32)
    msq = jnp.trace(g0) / rows_total
    inv = 1.0 / jnp.sqrt(msq + 1e-06)
    x = rows * inv
    g = g0 * (inv * inv) / rows_total
    eye = jnp.eye(rank, dtype=F32)
    for step in range(NS_STEPS):
        if step > 0:
            g = jnp.dot(x, x.T, precision=HI, preferred_element_type=F32) / rows_total
        x = jnp.dot(1.5 * eye - 0.5 * g, x, precision=HI, preferred_element_type=F32)
    return x


def general(tiles, block_one, block_two, block_three, owner_map, u_one, u_two, u_three):
    count, width = tiles.shape[:2]
    rank = u_three.shape[0]
    blocks_total = owner_map.shape[0]
    rows_total = blocks_total * width
    two_full = lax.all_gather(u_two, "tiles", axis=1, tiled=True)
    two_pick = pick(two_full, block_two, width)
    three_pick = pick(u_three, block_three, width)
    cube = tiles.reshape(count, width, width, width)
    first = jnp.einsum("tijk,tsk->tijs", cube, three_pick, preferred_element_type=F32).astype(BF16)
    second = jnp.einsum("tijs,trj->tirs", first, two_pick, preferred_element_type=F32)
    products = second.reshape(count, width, rank * rank).astype(BF16)
    positions = jnp.take(owner_map, block_one)
    onehot = (positions[:, None] == jnp.arange(blocks_total, dtype=jnp.int32)[None, :]).astype(F32)
    current = lax.all_gather(u_one.astype(BF16), "tiles", axis=1, tiled=True)
    readers = pick(current, positions, width)
    partial_value = jnp.einsum("tic,tri->rc", products, readers, preferred_element_type=F32)
    project = lax.psum(partial_value, ("tiles", "rep")).astype(BF16)
    z_tile = jnp.einsum("rc,tic->tri", project, products, preferred_element_type=F32)
    term = jnp.einsum("tri,tn->rni", z_tile, onehot, precision=HI).reshape(rank, rows_total)
    rows = lax.psum(term, ("tiles", "rep"))
    current = orthonormal(rows, rows_total)
    tile_factor = pick(current.astype(BF16), positions, width).reshape(count, rank * width)
    own = u_one.shape[1]
    factor = lax.dynamic_slice_in_dim(current, lax.axis_index("tiles") * own, own, 1)
    return (factor, tile_factor)


def split(a):
    high = a.astype(BF16)
    return high, (a - high.astype(F32)).astype(BF16)


def dot3(a, b, axis=0):
    (ah, al), (bh, bl) = split(a), split(b)
    dims = (((1,), (axis,)), ((), ()))
    parts = [lax.dot_general(p, q, dims, preferred_element_type=F32) for p, q in ((ah, bh), (ah, bl), (al, bh))]
    return parts[0] + (parts[1] + parts[2])


def lane_iota(shape):
    return lax.broadcasted_iota(jnp.int32, shape, len(shape) - 1)


def row_iota(shape):
    return lax.broadcasted_iota(jnp.int32, shape, len(shape) - 2)


def nt(a, b, precision=None):
    return lax.dot_general(
        a, b, (((1,), (1,)), ((), ())), precision=precision, preferred_element_type=F32
    )


def first_kernel(
    one_hbm, two_hbm, three_hbm, owner_hbm, tiles_hbm, u_three_hbm, u_two_hbm, u_one_hbm, out_hbm, places, pack,
    one, two, three, owner, tiles, u_three, u_two, u_one, two_f32, out, in_sems, tile_sems, out_sems,
):
    side = lax.axis_index("half")
    count, width = tiles.shape[:2]
    rank = u_three.shape[0]
    half = LANES // 2
    share = META // 2
    span = share * width
    pieces = tiles.shape[2] // (2 * span)
    moves = [(three_hbm, three), (u_three_hbm, u_three), (two_hbm, two), (one_hbm, one)]
    moves += [(owner_hbm, owner), (u_two_hbm, u_two), (u_one_hbm, u_one)]
    copies = [pltpu.make_async_copy(a, b, in_sems.at[i]) for i, (a, b) in enumerate(moves)]
    loads = [
        pltpu.make_async_copy(tiles_hbm.at[t], tiles.at[t], tile_sems.at[t]) for t in range(count)
    ]
    for copy in loads + copies:
        copy.start()
    copies[0].wait()
    copies[1].wait()
    weights = []
    for t in range(count):
        block = three[t]
        start = pl.multiple_of((block // 2) * LANES, LANES)
        window = u_three[:, pl.ds(start, LANES)].astype(F32)
        same = (lane_iota(window.shape) // half) == (block % 2)
        both = jnp.where(same, window, pltpu.roll(window, half, 1))
        tall = jnp.broadcast_to(both[:, None, :], (rank, share, LANES)).reshape(rank * share, LANES)
        full = jnp.concatenate([tall] * (span // LANES), axis=1)
        keep = (row_iota(full.shape) % share) == (lane_iota(full.shape) // width)
        weights.append(jnp.where(keep, full, 0.0).astype(BF16))
    for copy in copies[2:]:
        copy.wait()
    q = lax.axis_index("rep")
    pack[:rank, :] = u_two[...]
    pair = [u_one[: rank // 2, :], u_one[rank // 2 :, :]]
    pack[rank:, :] = jnp.concatenate(pair, axis=1).astype(BF16)
    two_f32[...] = u_two[...].astype(F32)
    top = two_f32[pl.ds(pl.multiple_of(q * share, share), share), :]
    low = u_one[pl.ds(pl.multiple_of(q * share, share), share), :]
    lane = lane_iota((share, half))
    ints = jnp.zeros((share, half), F32)
    spot = lane_iota(places.shape)
    place = jnp.zeros(places.shape, jnp.int32)
    for t in range(count):
        position = owner[one[t]]
        ints = jnp.where(lane == t, two[t].astype(F32), ints)
        ints = jnp.where(lane == count + t, position.astype(F32), ints)
        place = jnp.where(spot == t, position, place)
    places[...] = place
    meta = jnp.concatenate([top, jnp.concatenate([low, ints], axis=1)], axis=0).astype(BF16)
    rows = slice(2 * width, 2 * width + META)
    for k in range(out.shape[0]):
        out[k, rows, :] = meta
    stores = []

    def send(rows):
        copy = pltpu.make_async_copy(
            out.at[:, rows, :], out_hbm.at[:, rows, :], out_sems.at[len(stores)]
        )
        copy.start()
        stores.append(copy)

    send(rows)
    for copy in loads:
        copy.wait()
    for n in range(pieces // 2):
        wide = []
        for t in range(count):
            groups = [tiles[t, :, (4 * n + g) * span : (4 * n + g + 1) * span] for g in range(4)]
            wide.append(nt(weights[t], jnp.concatenate(groups, axis=0)))
        for s in range(rank):
            at = slice(s * share, (s + 1) * share)
            for h in range(2):
                block = []
                for g in (2 * h, 2 * h + 1):
                    lanes = slice(g * width, (g + 1) * width)
                    block.append(jnp.concatenate([part[at, lanes] for part in wide], axis=1))
                start = n * width + (s % 2) * (width // 2) + h * META
                rows = slice(start, start + META)
                out[(s // 2) ^ side, rows, :] = jnp.concatenate(block, axis=0).astype(BF16)
        send(slice(n * width, (n + 1) * width))
    for copy in stores:
        copy.wait()


def table_kernel(reps, got, far0, far1, far2, far3, out, readers, two, one, total):
    sources, depth = got.shape[:2]
    half = LANES // 2
    share = META // 2
    width = (depth - META) // 2
    rank = share * reps
    count = LANES // width
    owners = 2 * sources // reps
    blocks = 2 * owners
    side = lax.axis_index("half")
    lines = []
    halves = lane_iota((META, LANES)) // half
    for src in range(0, sources, 2):
        t, q = divmod(src, reps)
        rows = slice(q * share, (q + 2) * share)
        pair = [got[src + k, 2 * width : 2 * width + META, :].astype(F32) for k in range(2)]
        mine = jnp.concatenate([meta[:share] for meta in pair], axis=0)
        shard = side * (owners // 2) + t
        for k in range(2):
            two[2 * shard + k, rows, :] = jnp.where(halves == k, mine, 0.0).astype(BF16)
        one[shard, rows, :] = jnp.concatenate([meta[share:] for meta in pair], axis=0)
        lines += [meta[share : share + 1] for meta in pair]
    halves = lane_iota((rank, LANES)) // half
    for k, ref in enumerate((far0, far1, far2, far3)):
        shard = (1 - side) * (owners // 2) + (lax.axis_index("rest") ^ k)
        theirs = ref[:rank, :].astype(F32)
        for k in range(2):
            two[2 * shard + k] = jnp.where(halves == k, theirs, 0.0).astype(BF16)
        theirs = ref[rank:, :].astype(F32)
        one[shard, : rank // 2, :] = theirs
        one[shard, rank // 2 :, :] = pltpu.roll(theirs, half, 1)
    lines = jnp.concatenate(lines, axis=0)
    lane = lane_iota(lines.shape)
    scale = jnp.zeros(lines.shape, F32)
    for k in range(2 * count):
        scale = jnp.where(lane == half + k, float(blocks**k), scale)
    code = jnp.sum(lines * scale, axis=1, keepdims=True).astype(jnp.int32)
    total[...] = jnp.zeros_like(total)
    for src in range(sources):
        moving = []
        for s in range(2):
            lines = [got[src, at : at + width // 2, :] for at in (s * width // 2, (s + 2) * width // 2)]
            moving.append(jnp.concatenate(lines + lines, axis=0))
        moving = jnp.concatenate(moving, axis=1)
        left = code[src, 0]
        digits = []
        for _ in range(2 * count):
            digits.append(left % blocks)
            left = left // blocks
        stacked = jnp.concatenate([two[b] for b in digits[:count]], axis=0)
        product = jnp.dot(stacked, moving, preferred_element_type=F32)
        for t, p in enumerate(digits[count:]):
            total[t, p] += product[t * rank : (t + 1) * rank]
    for s in range(2):
        sums = []
        lanes = slice(s * LANES, (s + 1) * LANES)
        for p in range(owners):
            low = total[0, p, :, lanes][:, :half]
            high = total[1, p, :, lanes]
            sums.append(low + pltpu.roll(high, half, 1)[:, :half])
        out[s * rank : (s + 1) * rank, :] = jnp.concatenate(sums, axis=1).astype(BF16)
    readers[...] = jnp.concatenate([one[p][:, :half] for p in range(owners)], axis=1).astype(BF16)


def known_kernel(mine, readers, out):
    out[...] = nt(readers[...], mine[...])


def rows_kernel(mine, theirs, readers, known, out):
    project = (known[...] + nt(readers[...], theirs[...])).astype(BF16)
    part = jnp.dot(project, mine[...], preferred_element_type=F32)
    part += jnp.dot(project, theirs[...], preferred_element_type=F32)
    out[...] = part.astype(BF16)


def final_kernel(places, a, b, c, d, factor, tile_factor, table):
    rank, rows_total = a.shape
    half = LANES // 2
    rows = (a[...].astype(F32) + b[...].astype(F32)) + (c[...].astype(F32) + d[...].astype(F32))
    table[...] = rows
    g0 = dot3(rows, rows, 1)
    eye = (row_iota(g0.shape) == lane_iota(g0.shape)).astype(F32)
    msq = jnp.sum(rows * rows, keepdims=True) / rows_total
    inv = 1.0 / jnp.sqrt(msq + 1e-06)
    g = g0 * (inv * inv) / rows_total
    square = dot3(g, g)
    outer = dot3(square, 0.0625 * square - 0.5625 * g)
    step = (outer + (1.6875 * square - 2.4375 * g + 2.25 * eye)) * inv

    def block(p):
        window = table[:, pl.ds(pl.multiple_of((p // 2) * LANES, LANES), LANES)]
        return jnp.where(p % 2 == 1, pltpu.roll(window, half, 1), window)[:, :half]

    place = places[...]
    picks = [lax.axis_index(("half", "rest"))] + [place[0, t] for t in range(tile_factor.shape[0])]
    picked = jnp.concatenate([block(p) for p in picks], axis=1)
    x = dot3(step, picked)
    factor[...] = x[:, :half]
    for t in range(tile_factor.shape[0]):
        value = x[:, (t + 1) * half : (t + 2) * half]
        for r in range(0, rank, 2):
            line = jnp.concatenate([value[r : r + 1], value[r + 1 : r + 2]], axis=1)
            tile_factor[t : t + 1, r * half : (r + 2) * half] = line.astype(BF16)


def swap(x, size, mask):
    return lax.ppermute(x, ("half", "rest", "rep"), [(i, i ^ mask) for i in range(size)])


def sliced(tiles, block_one, block_two, block_three, owner_map, u_one, u_two, u_three):
    count, width = tiles.shape[:2]
    rank = u_three.shape[0]
    owners = 2 * lax.axis_size("rest")
    reps = lax.axis_size("rep")
    size = owners * reps
    sources = size // 2
    rows_total = owner_map.shape[0] * width
    depth = 2 * width + META
    vmem = pl.BlockSpec(memory_space=pltpu.VMEM)
    narrow = pltpu.CompilerParams(vmem_limit_bytes=NARROW)
    core, x, y, near, far = 1, 2, 4, 8, 16
    ints = (block_one, block_two, block_three, owner_map)
    arrays = (tiles, u_three, u_two, u_one)
    sends, places, pack = pl.pallas_call(
        first_kernel,
        out_shape=(
            jax.ShapeDtypeStruct((sources, depth, LANES), BF16),
            jax.ShapeDtypeStruct((META // 2, LANES), jnp.int32),
            jax.ShapeDtypeStruct((rank + rank // 2, LANES), BF16),
        ),
        in_specs=[pl.BlockSpec(memory_space=pltpu.HBM)] * 8,
        out_specs=(pl.BlockSpec(memory_space=pltpu.HBM), vmem, vmem),
        scratch_shapes=[pltpu.SMEM(a.shape, a.dtype) for a in ints]
        + [pltpu.VMEM(a.shape, a.dtype) for a in arrays]
        + [
            pltpu.VMEM(u_two.shape, F32),
            pltpu.VMEM((sources, depth, LANES), BF16),
            pltpu.SemaphoreType.DMA((7,)),
            pltpu.SemaphoreType.DMA((count,)),
            pltpu.SemaphoreType.DMA((3,)),
        ],
        compiler_params=narrow,
        name="first",
    )(*[pltpu.with_memory_space_constraint(a, pltpu.HBM) for a in ints + arrays])
    theirs = [swap(pack, size, far | core | k * y) for k in (3, 2, 1, 0)][::-1]
    got = lax.all_to_all(sends, ("rest", "rep"), 0, 0, tiled=True)
    table, readers = pl.pallas_call(
        functools.partial(table_kernel, reps),
        out_shape=(
            jax.ShapeDtypeStruct((2 * rank, rows_total), BF16),
            jax.ShapeDtypeStruct((rank, rows_total), BF16),
        ),
        in_specs=[vmem] * 5,
        out_specs=(vmem, vmem),
        scratch_shapes=[
            pltpu.VMEM((2 * owners, rank, LANES), BF16),
            pltpu.VMEM((owners, rank, LANES), F32),
            pltpu.VMEM((count, owners, rank, 2 * LANES), F32),
        ],
        compiler_params=narrow,
        name="table",
    )(got, *theirs)
    known = pl.pallas_call(
        known_kernel,
        out_shape=jax.ShapeDtypeStruct((rank, 2 * rank), F32),
        in_specs=[vmem] * 2,
        out_specs=vmem,
        compiler_params=narrow,
        name="known",
    )(table, readers)
    part = pl.pallas_call(
        rows_kernel,
        out_shape=jax.ShapeDtypeStruct((rank, rows_total), BF16),
        in_specs=[vmem] * 4,
        out_specs=vmem,
        compiler_params=narrow,
        name="rows_part",
    )(table, swap(table, size, far | core), readers, known)
    part = (part.astype(F32) + swap(part, size, core).astype(F32)).astype(BF16)
    part = (part.astype(F32) + swap(part, size, x | core).astype(F32)).astype(BF16)
    rest = [swap(part, size, mask) for mask in (near | core, y | core, y ^ near)]
    return pl.pallas_call(
        final_kernel,
        out_shape=(
            jax.ShapeDtypeStruct(u_one.shape, F32),
            jax.ShapeDtypeStruct((count, rank * width), BF16),
        ),
        in_specs=[vmem] * 5,
        out_specs=(vmem, vmem),
        scratch_shapes=[pltpu.VMEM((rank, rows_total), F32)],
        compiler_params=narrow,
        name="final",
    )(places, part, *rest)


def fits(mesh, tiles, block_one, block_two, block_three, owner_map, u_one, u_two, u_three):
    owners, reps = mesh.shape["tiles"], mesh.shape["rep"]
    rank = u_three.shape[0]
    width = tiles.shape[1]
    return (
        owners == 8
        and reps == 4
        and rank == owners * reps == reps * META // 2
        and tiles.shape[0] == 2 * owners * reps
        and 2 * width == LANES
        and owner_map.shape[0] == owners
        and u_one.shape[1] == owners * width
        and u_two.shape[1] == owners * LANES
        and u_three.shape[1] % LANES == 0
    )


def specs(tiles, rep):
    both = tiles + rep
    ins = (P(both, None, None), P(both), P(both), P(both), P(), P(None, tiles), P(None, tiles), P())
    return ins, (P(None, tiles), P(both, None))


def solution(mesh):
    def run(*args):
        if fits(mesh, *args):
            axes = ("half", "rest", "rep")
            grid = mesh.devices.reshape(2, -1, mesh.shape["rep"])
            halves = jax.sharding.Mesh(grid, axes)
            ins, outs = specs(axes[:2], axes[2:])
            body, where = sliced, halves
        else:
            ins, outs = specs(("tiles",), ("rep",))
            body, where = general, mesh
        return jax.shard_map(body, mesh=where, in_specs=ins, out_specs=outs, check_vma=False)(*args)

    return run
```
